32 devices in a mesh: ep: 8 (over z, y), es: 4 (over x, core).
Axes of the slice: x: 2, y: 2, z: 4, core: 2. Of those that a mesh axis runs over, the one named last changes fastest.
Arguments:
- tokens: bfloat16 [16384, 1024], P(('ep', 'es')), may hold values from -26 to 26
- cotangent: bfloat16 [16384, 1024], P(('ep', 'es')), may hold values from -6 to 6
- w_qkv: bfloat16 [1024, 3072], P(('ep', 'es')), may hold values from -0.1875 to 0.1875
- w_out: bfloat16 [1024, 1024], P(('ep', 'es')), may hold values from -6 to 6
- w_fc_in: bfloat16 [1024, 4096], P(('ep', 'es')), may hold values from -0.5 to 0.5
- w_fc_out: bfloat16 [4096, 1024], P(('ep', 'es')), may hold values from -0.25 to 0.25
- norm1_gain: bfloat16 [1024], P(('ep', 'es')), may hold values from 0.25 to 1.75
- norm1_bias: bfloat16 [1024], P(('ep', 'es')), may hold values from -0.119628906 to 0.119628906
- norm2_gain: bfloat16 [1024], P(('ep', 'es')), may hold values from 0.25 to 1.75
- norm2_bias: bfloat16 [1024], P(('ep', 'es')), may hold values from -1.796875 to 1.796875
- coef_weight: bfloat16 [1024, 2], P(('ep', 'es')), may hold values from -0.1875 to 0.1875
- expert_up: bfloat16 [8, 4096, 1024], P('ep', 'es'), may hold values from -0.5 to 0.5
- expert_down: bfloat16 [8, 4096, 1024], P('ep', 'es'), may hold values from -0.25 to 0.25
- routes: int32 [16384, 1], P(('ep', 'es')), may hold values from 0 to 7; in each aligned block of 512 rows (0 to 511, 512 to 1023, ...) at most 128 rows name the same one
- keep_mask: int32 [16384], P(('ep', 'es')), may hold values 0 or 1
Outputs:
- out_tokens: bfloat16 [16384, 1024], P(('ep', 'es'))
- grad_tokens: float32 [16384, 1024], P(('ep', 'es'))
- grad_w_qkv: float32 [1024, 3072], P(('ep', 'es'))
- grad_w_out: float32 [1024, 1024], P(('ep', 'es'))
- grad_w_fc_in: float32 [1024, 4096], P(('ep', 'es'))
- grad_w_fc_out: float32 [4096, 1024], P(('ep', 'es'))
- grad_norm1_gain: float32 [1024], P(('ep', 'es'))
- grad_norm1_bias: float32 [1024], P(('ep', 'es'))
- grad_norm2_gain: float32 [1024], P(('ep', 'es'))
- grad_norm2_bias: float32 [1024], P(('ep', 'es'))
- grad_coef_weight: float32 [1024, 2], P(('ep', 'es'))
- grad_expert_up: float32 [8, 4096, 1024], P('ep', 'es')
- grad_expert_down: float32 [8, 4096, 1024], P('ep', 'es')
The draws below stay inside these ranges and needn't reach their ends.
Inputs may be any that keep to these rules, and one draw needn't show every extreme that they name: `routes`: within the rows of one device no expert is named more than 128 times, a bound that some block reaches.
All inputs are finite; a program needn't handle non-finite values. No bound on the sum of `keep_mask` on one device may be relied on, other than what follows from the above.
Results may differ from the reference program's by a relative error of at most 0.015.
Values may be sent and summed in bfloat16 or wider, within the bound.
No kernel may reach another device: no remote copies, remote signals or barrier semaphores. Data moves between devices by JAX's collectives and lax.ppermute only.
A program may use at most 320 MiB of HBM per device.

```python
import math
import jax
import jax.numpy as jnp
import numpy as np
from jax import lax

D = 1024
HEADS = 16
HEAD_DIM = 64
FF = 4096
FFE = 4096
TOK_DEV = 512
SEQ = 2048
EXPERTS = 8
CAP = 128
TOKENS = 16384
N_EP = 8
N_ES = 4


def draw_tokens(key, part):
    key = jax.random.fold_in(key, 11)
    key_values, key_rows, key_columns = jax.random.split(key, 3)
    values = jnp.clip(jax.random.normal(key_values, (TOKENS, D), jnp.float32), -4.0, 4.0)
    row_scale = jnp.exp(jax.random.uniform(key_rows, (TOKENS, 1), jnp.float32, -1.15, 1.15))
    column_scale = jnp.exp(jax.random.uniform(key_columns, (1, D), jnp.float32, -0.7, 0.7))
    return (values * row_scale * column_scale).astype(jnp.bfloat16)


def touch_ends(array, stream_key, low, high):
    spot = [jax.random.randint(jax.random.fold_in(stream_key, axis), (), 0, length) for axis, length in enumerate(array.shape)]
    widest = array.shape.index(max(array.shape))
    next_to = spot[:widest] + [(spot[widest] + 1) % array.shape[widest]] + spot[widest + 1:]
    return array.at[tuple(spot)].set(low).at[tuple(next_to)].set(high)


def level_of(rng, extent, cuts, low, top_value):
    factor_of = 1.0
    for position, shards_of in cuts:
        heights = jax.random.uniform(jax.random.fold_in(jax.random.fold_in(rng, 6), position), (shards_of,), jnp.float32, low / len(cuts), top_value / len(cuts))
        factor_of = factor_of * jnp.repeat(jnp.exp(heights), extent[position] // shards_of).reshape((-1,) + (1,) * (len(extent) - 1 - position))
    return factor_of


def routed_block(key, own, number, rows, count, top, bound, lean):
    sequence = jax.random.permutation(key, count)
    crowded, ordinary = portions_of(count, rows * top, bound, lean, True), portions_of(count, rows * top, bound, lean, False)
    places = jnp.arange(count)

    def named(lengths, turn):
        used = int((lengths > 0).sum())
        fixed = max(1, used // 4)
        shifted = fixed + (places - fixed + turn * (used - fixed)) % max(1, count - fixed)
        return jnp.zeros((count,), jnp.int32).at[sequence[jnp.where(places < fixed, places, shifted)]].set(jnp.asarray(lengths, jnp.int32))

    lengths = jnp.where(number % 4 == 0, named(crowded, number // 4), named(ordinary, number - number // 4 - 1))
    mixed = jax.random.permutation(jax.random.fold_in(own, 3), count)
    donor, receiver = mixed[0:count // 2 * 2:2], mixed[1:count // 2 * 2:2]
    slack = jnp.minimum(lengths[donor] - 1, bound - lengths[receiver]) // 2
    slack = jnp.where((donor == sequence[0]) | (receiver == sequence[0]) | (lengths[receiver] == 0), 0, jnp.maximum(slack, 0))
    shifted = jax.random.randint(jax.random.fold_in(own, 4), (count // 2,), 0, 1 << 20) % (slack + 1)
    lengths = lengths.at[donor].add(-shifted).at[receiver].add(shifted)
    labels = jnp.searchsorted(jnp.cumsum(lengths), jnp.arange(rows * top), side="right").astype(jnp.int32)
    table = labels.reshape(top, rows).T
    table = table[jax.random.permutation(jax.random.fold_in(own, 1), rows)]
    turn = jax.random.randint(jax.random.fold_in(own, 2), (rows, 1), 0, top)
    return jnp.take_along_axis(table, (jnp.arange(top)[None, :] + turn) % top, axis=1)


def portions_of(count, total, bound, skew, full):
    portions = [(1 << 20) // math.isqrt(standing ** skew) + 1 for standing in range(1, count + 1)]
    largest = bound if full else min(bound, max(-(-total // count), total * portions[0] // sum(portions)))
    least = 1 if total - largest >= count - 1 else 0
    given, spare = [largest] + [least] * (count - 1), total - largest - least * (count - 1)
    while spare > 0:
        free = [i for i in range(1, count) if given[i] < largest] or [i for i in range(1, count) if given[i] < bound]
        pool, left = sum([portions[i] for i in free]), spare
        for i in free:
            addition = min(bound - given[i], max(1, left * portions[i] // pool), spare)
            given[i] = given[i] + addition
            spare = spare - addition
    return np.array(given)


def scatter_about(rng, shape, spread, bound, pieces=(), kind=jnp.bfloat16):
    values = spread * jax.random.normal(rng, shape, jnp.float32)
    if pieces:
        values = values * level_of(rng, shape, pieces, -0.22, 0.18)
    return jnp.clip(values, -bound, bound).astype(kind)


def setup_inputs(seed: int = 0) -> dict:
    streams_of = jax.random.split(jax.random.key(seed), 16)
    tokens = draw_tokens(jax.random.fold_in(streams_of[15], 71), 0)
    cotangent = scatter_about(streams_of[1], (TOKENS, D), 1.0, 6.0, ((0, 32),))
    w_qkv = scatter_about(streams_of[2], (D, 3 * D), D ** -0.5, 0.1875, ((0, 32),))
    w_out = scatter_about(streams_of[3], (D, D), (max(1, 2 * D // SEQ)) ** -0.5, 6.0, ((0, 32),))
    w_fc_in = scatter_about(streams_of[4], (D, FF), (D // 8) ** -0.5, 0.5, ((0, 32),))
    w_fc_out = scatter_about(streams_of[5], (FF, D), (FF // 8) ** -0.5, 0.25, ((0, 32),))
    norm1_gain = jnp.clip(1.0 + 0.15 * jax.random.normal(streams_of[6], (D,), jnp.float32), 0.25, 1.75).astype(jnp.bfloat16)
    norm1_bias = scatter_about(streams_of[7], (D,), 0.02, 0.119628906, ((0, 32),))
    norm2_gain = jnp.clip(1.0 + 0.15 * jax.random.normal(streams_of[8], (D,), jnp.float32), 0.25, 1.75).astype(jnp.bfloat16)
    norm2_bias = scatter_about(streams_of[9], (D,), 0.3, 1.796875, ((0, 32),))
    coef_weight = scatter_about(streams_of[10], (D, 2), D ** -0.5, 0.1875, ((0, 32),))
    expert_up = scatter_about(streams_of[11], (EXPERTS, FFE, D), (D // 8) ** -0.5, 0.5, ((0, 8), (1, 4)))
    expert_down = scatter_about(streams_of[12], (EXPERTS, FFE, D), (FFE // 8) ** -0.5, 0.25, ((0, 8), (1, 4)))
    routes_keys = jax.random.split(jax.random.fold_in(streams_of[13], 1), TOKENS // TOK_DEV)
    routes_turns = jax.random.permutation(jax.random.fold_in(streams_of[13], 3), TOKENS // TOK_DEV)
    routes = jax.vmap(lambda own, number: routed_block(jax.random.fold_in(streams_of[13], 2), own, number, TOK_DEV, EXPERTS, 1, CAP, 2))(routes_keys, routes_turns).reshape((TOKENS, 1))
    keep_mask = touch_ends((jax.random.randint(streams_of[14], (TOKENS,), 0, 8) < 7).astype(jnp.int32), jax.random.fold_in(streams_of[14], 1), 0, 1)
    return {"tokens": tokens, "cotangent": cotangent, "w_qkv": w_qkv, "w_out": w_out, "w_fc_in": w_fc_in, "w_fc_out": w_fc_out, "norm1_gain": norm1_gain, "norm1_bias": norm1_bias, "norm2_gain": norm2_gain, "norm2_bias": norm2_bias, "coef_weight": coef_weight, "expert_up": expert_up, "expert_down": expert_down, "routes": routes, "keep_mask": keep_mask}


EPSILON = 1e-05
MASKED = -1e+30
HIGHEST_PRECISION = lax.Precision.HIGHEST

@jax.custom_vjp
def low(v):
    return lax.optimization_barrier(v.astype(jnp.bfloat16)).astype(jnp.float32)

@jax.custom_vjp
def low_back(v):
    return v

def low_keep(v):
    return (low(v), None)

def low_pass(kept, grad):
    return (grad,)

def back_keep(v):
    return (v, None)

def back_low(kept, grad):
    return (low(grad),)
low.defvjp(low_keep, low_pass)
low_back.defvjp(back_keep, back_low)

def layer_norm(values, gain, offset):
    average = lax.optimization_barrier(jnp.mean(values, axis=-1, keepdims=True))
    centred = values - average
    variance = lax.optimization_barrier(jnp.mean(centred * centred, axis=-1, keepdims=True))
    return centred * lax.rsqrt(variance + EPSILON) * gain + offset

def attend_sequence(qkv_rows):
    length = qkv_rows.shape[0]
    queries = qkv_rows[:, :D].reshape(length, HEADS, HEAD_DIM)
    keys_all = qkv_rows[:, D:2 * D].reshape(length, HEADS, HEAD_DIM)
    values_all = qkv_rows[:, 2 * D:].reshape(length, HEADS, HEAD_DIM)
    raw_scores = jnp.einsum('qhd,khd->hqk', queries, keys_all, precision=HIGHEST_PRECISION)
    scores = low_back(raw_scores) * HEAD_DIM ** (-0.5)
    places = jnp.arange(length, dtype=jnp.int32)
    scores = jnp.where(places[None, None, :] <= places[None, :, None], scores, MASKED)
    largest = lax.optimization_barrier(jnp.max(scores, axis=-1, keepdims=True))
    expanded = jnp.exp(scores - largest)
    probs = expanded / lax.optimization_barrier(jnp.sum(expanded, axis=-1, keepdims=True))
    attended = jnp.einsum('hqk,khd->qhd', low(probs), values_all, precision=HIGHEST_PRECISION)
    return low(low_back(attended.reshape(length, D)))

def expert_apply(operands):
    rows, up_matrix, down_matrix = operands
    inner = low_back(jnp.dot(rows, up_matrix.T, precision=HIGHEST_PRECISION))
    activated = low(jax.nn.gelu(inner, approximate=False))
    return low(low_back(jnp.dot(activated, down_matrix, precision=HIGHEST_PRECISION)))

def slot_numbers(expert_ids):
    devices = N_EP * N_ES
    per_device = expert_ids.reshape(devices, TOK_DEV)
    onehot = (per_device[:, :, None] == jnp.arange(EXPERTS, dtype=jnp.int32)[None, None, :]).astype(jnp.int32)
    ranks = lax.optimization_barrier(jnp.sum((jnp.cumsum(onehot, axis=1) - 1) * onehot, axis=2))
    sources = jnp.arange(devices, dtype=jnp.int32)[:, None]
    return (per_device * (devices * CAP) + sources * CAP + ranks).reshape(-1).astype(jnp.int32)

def reference(tokens, cotangent, w_qkv, w_out, w_fc_in, w_fc_out, norm1_gain, norm1_bias, norm2_gain, norm2_bias, coef_weight, expert_up, expert_down, routes, keep_mask):
    slots = slot_numbers(routes[:, 0].astype(jnp.int32))
    keep = keep_mask.astype(jnp.float32)[:, None]
    devices = N_EP * N_ES
    sequences = TOKENS // SEQ
    group = math.gcd(sequences, max(1, 4096 // SEQ))

    def forward(inputs, qkv_weight, out_weight, fc_in_weight, fc_out_weight, gain_one, bias_one, gain_two, bias_two, coef_matrix, up_stack, down_stack):
        normed_one = low(layer_norm(inputs, gain_one, bias_one))
        qkv_all = low(low_back(jnp.dot(normed_one, qkv_weight, precision=HIGHEST_PRECISION)))
        grouped = qkv_all.reshape(sequences // group, group, SEQ, 3 * D)
        attended = lax.map(jax.checkpoint(jax.vmap(attend_sequence)), grouped).reshape(TOKENS, D)
        hidden = inputs + low_back(jnp.dot(attended, out_weight, precision=HIGHEST_PRECISION))
        normed_two = layer_norm(hidden, gain_two, bias_two)
        normed_low = low(normed_two)
        logits = jnp.dot(normed_two, coef_matrix, precision=HIGHEST_PRECISION)
        largest = lax.optimization_barrier(jnp.max(logits, axis=-1, keepdims=True))
        expanded = jnp.exp(logits - largest)
        coefficients = expanded / lax.optimization_barrier(jnp.sum(expanded, axis=-1, keepdims=True))
        inner = low_back(jnp.dot(normed_low, fc_in_weight, precision=HIGHEST_PRECISION))
        activated = low(jax.nn.gelu(inner, approximate=False))
        dense = low_back(jnp.dot(activated, fc_out_weight, precision=HIGHEST_PRECISION))
        buffer = jnp.zeros((EXPERTS * devices * CAP, D), jnp.float32).at[slots].set(normed_low)
        buffer = low_back(buffer).reshape(EXPERTS, devices * CAP, D)
        expert_out = lax.map(jax.checkpoint(expert_apply), (buffer, up_stack, down_stack))
        expert_tokens = expert_out.reshape(EXPERTS * devices * CAP, D)[slots] * keep
        return hidden + coefficients[:, 0:1] * dense + coefficients[:, 1:2] * expert_tokens
    floats = (tokens.astype(jnp.float32), w_qkv.astype(jnp.float32), w_out.astype(jnp.float32), w_fc_in.astype(jnp.float32), w_fc_out.astype(jnp.float32), norm1_gain.astype(jnp.float32), norm1_bias.astype(jnp.float32), norm2_gain.astype(jnp.float32), norm2_bias.astype(jnp.float32), coef_weight.astype(jnp.float32), expert_up.astype(jnp.float32), expert_down.astype(jnp.float32))
    output, pullback = jax.vjp(forward, *floats)
    gradients = pullback(cotangent.astype(jnp.float32))
    return (output.astype(jnp.bfloat16), gradients[0], gradients[1], gradients[2], gradients[3], gradients[4], gradients[5], gradients[6], gradients[7], gradients[8], gradients[9], gradients[10], gradients[11])
```

```python
import functools

import jax
import jax.numpy as jnp
import numpy as np
from jax import lax
from jax.experimental import pallas as pl
from jax.experimental.pallas import tpu as pltpu
from jax.sharding import PartitionSpec as P

HEADS = 16
HEAD_DIM = 64
EPSILON = 1e-05
MASKED = -1e30
HIGHEST = lax.Precision.HIGHEST
BOTH = ("ep", "es")
MIB = 1 << 20


def norm_forward(values, gain, offset):
    average = jnp.mean(values, axis=-1, keepdims=True)
    centred = values - average
    variance = jnp.mean(centred * centred, axis=-1, keepdims=True)
    inverse = lax.rsqrt(variance + EPSILON)
    unit = centred * inverse
    return unit * gain + offset, unit, inverse


def norm_backward(grad, unit, inverse, gain):
    scaled = grad * gain
    mean_scaled = jnp.mean(scaled, axis=-1, keepdims=True)
    mean_unit = jnp.mean(scaled * unit, axis=-1, keepdims=True)
    grad_in = (scaled - mean_scaled - unit * mean_unit) * inverse
    return grad_in, jnp.sum(grad * unit, axis=0), jnp.sum(grad, axis=0)


def gelu_and_slope(values):
    cdf = 0.5 * (1.0 + lax.erf(values * (2.0**-0.5)))
    density = jnp.exp(-0.5 * values * values) * ((2.0 * np.pi) ** -0.5)
    return values * cdf, cdf + values * density


def dot(left, right, contract=((1,), (0,)), out=jnp.float32):
    return lax.dot_general(left, right, (contract, ((), ())), preferred_element_type=out)


def softmax_pair(logits):
    largest = jnp.max(logits, axis=-1, keepdims=True)
    expanded = jnp.exp(logits - largest)
    return expanded / jnp.sum(expanded, axis=-1, keepdims=True)


def digits(axis):
    size = lax.axis_size(axis)
    return [(axis, 1 << b) for b in range(size.bit_length() - 1)]


def exchange(x, digit):
    axis, stride = digit
    size = lax.axis_size(axis)
    return lax.ppermute(x, axis, [(i, i ^ stride) for i in range(size)])


def weight_of(digit):
    axis, stride = digit
    return stride * (lax.axis_size("es") if axis == "ep" else 1)


def relative_numbers(order):
    numbers = [0]
    for digit in order:
        numbers = numbers + [n + weight_of(digit) for n in numbers]
    return numbers


def gather_relative(shard, order):
    held = shard[None]
    for digit in order[:-1]:
        held = jnp.concatenate([held, exchange(held, digit)], axis=0)
    return held, exchange(held, order[-1])


def place_kernel(plan, me_ref, *refs):
    out, held, sems_in, sems_out = refs[-4:]
    me = me_ref[0]
    arriving, leaving = [], []
    for number, (which, row, relative, rows, first, width) in enumerate(plan):
        at = (pl.ds(number * rows, rows), pl.ds(0, width))
        copy = pltpu.make_async_copy(refs[which].at[row], held.at[at], sems_in.at[number])
        copy.start()
        arriving.append(copy)
        start = pl.multiple_of((me ^ relative) * rows, rows)
        leaving.append(
            pltpu.make_async_copy(
                held.at[at], out.at[pl.ds(start, rows), pl.ds(first, width)], sems_out.at[number]
            )
        )
    for number in range(len(plan)):
        arriving[number].wait()
        leaving[number].start()
    for copy in leaving:
        copy.wait()


def gather_rows(shard, orders, me):
    rows, columns = shard.shape
    width = columns // len(orders)
    count = 1 << len(orders[0])
    if rows % 16 or width % 128:
        axes = tuple(a for a in BOTH if any(d[0] == a for d in orders[0]))
        return lax.all_gather(shard, axes, axis=0, tiled=True)
    parts, plan = [], []
    for index, order in enumerate(orders):
        numbers = relative_numbers(order)
        first = index * width
        held, received = gather_relative(shard[:, first : first + width], order)
        for half, part in enumerate((held, received)):
            for row in range(count // 2):
                plan.append((len(parts), row, numbers[half * (count // 2) + row], rows, first, width))
            parts.append(part)
    return pl.pallas_call(
        functools.partial(place_kernel, tuple(plan)),
        out_shape=jax.ShapeDtypeStruct((count * rows, columns), shard.dtype),
        in_specs=[pl.BlockSpec(memory_space=pltpu.SMEM)] + [pl.BlockSpec(memory_space=pl.ANY)] * len(parts),
        out_specs=pl.BlockSpec(memory_space=pl.ANY),
        scratch_shapes=[
            pltpu.VMEM((len(plan) * rows, width), shard.dtype),
            pltpu.SemaphoreType.DMA((len(plan),)),
            pltpu.SemaphoreType.DMA((len(plan),)),
        ],
        compiler_params=pltpu.CompilerParams(vmem_limit_bytes=16 * MIB),
        name="place_rows",
    )(me, *parts)


def gather_small(shard, order, me):
    held = shard[None]
    for digit in order:
        held = jnp.concatenate([held, exchange(held, digit)], axis=0)
    numbers = relative_numbers(order)
    count = len(numbers)
    place = np.zeros(count, np.int32)
    place[np.array(numbers)] = np.arange(count)
    index = jnp.asarray(place)[jnp.arange(count, dtype=jnp.int32) ^ me]
    return held[index]


def scatter_sum(partial, order, kept=jnp.bfloat16):
    count = 1 << len(order)
    rows = partial.shape[0] // count
    remaining = sorted(order, key=weight_of, reverse=True)
    held = partial.reshape((2,) * len(order) + (rows,) + partial.shape[1:])
    for number, digit in enumerate(order):
        axis, stride = digit
        place = remaining.index(digit)
        remaining.remove(digit)
        bit = (lax.axis_index(axis) // stride) % 2
        mine = lax.dynamic_index_in_dim(held, bit, place, keepdims=False)
        theirs = lax.dynamic_index_in_dim(held, 1 - bit, place, keepdims=False)
        held = mine.astype(jnp.float32) + exchange(theirs, digit).astype(jnp.float32)
        if number < len(order) - 1:
            held = held.astype(kept)
    return held


def head_mask(rows, width, head):
    lane = lax.broadcasted_iota(jnp.int32, (rows, width), 1)
    return (lane // HEAD_DIM) == head


def causal_tile(block):
    key = lax.broadcasted_iota(jnp.int32, (block, block), 0)
    query = lax.broadcasted_iota(jnp.int32, (block, block), 1)
    return key <= query


def attend_kernel(heads, block, q_ref, k_ref, vt_ref, low_ref, full_ref, log_ref, qh, acc, top, total):
    i = pl.program_id(0)
    width = heads * HEAD_DIM
    scaled = q_ref[...] * jnp.asarray(HEAD_DIM**-0.5, jnp.bfloat16)
    for h in range(heads):
        qh[h] = jnp.where(head_mask(block, width, h), scaled, jnp.zeros_like(scaled))
    acc[...] = jnp.zeros_like(acc)
    total[...] = jnp.zeros_like(total)
    top[...] = jnp.full_like(top, MASKED)
    nt = ((1,), (1,))

    def scores(j, h, diagonal):
        s = dot(k_ref[pl.ds(j * block, block), :], qh[h], nt)
        return jnp.where(causal_tile(block), s, MASKED) if diagonal else s

    def find_top(j, diagonal):
        for h in range(heads):
            s = scores(j, h, diagonal)
            folded = jnp.max(s.reshape(block // 8, 8, block), axis=0)
            top[h] = jnp.maximum(top[h], folded)

    def add_block(j, diagonal):
        for h in range(heads):
            s = scores(j, h, diagonal)
            p = jnp.exp(s - jnp.max(top[h], axis=0, keepdims=True))
            total[h] = total[h] + jnp.sum(p.reshape(block // 8, 8, block), axis=0)
            low = slice(h * HEAD_DIM, (h + 1) * HEAD_DIM)
            acc[low, :] = acc[low, :] + dot(
                vt_ref[low, pl.ds(j * block, block)], p.astype(jnp.bfloat16)
            )

    @pl.loop(0, i)
    def _(j):
        find_top(j, False)

    find_top(i, True)
    for h in range(heads):
        top[h] = jnp.broadcast_to(jnp.max(top[h], axis=0, keepdims=True), top.shape[1:])

    @pl.loop(0, i)
    def _(j):
        add_block(j, False)

    add_block(i, True)
    for h in range(heads):
        summed = jnp.sum(total[h], axis=0, keepdims=True)
        log_ref[pl.ds(h, 1), :] = jnp.max(top[h], axis=0, keepdims=True) + jnp.log(summed)
        low = slice(h * HEAD_DIM, (h + 1) * HEAD_DIM)
        acc[low, :] = acc[low, :] / summed
    out = acc[...].T
    full_ref[...] = out
    low_ref[...] = out.astype(jnp.bfloat16)


def attend(q, k, v):
    rows, width = q.shape
    heads = width // HEAD_DIM
    block = min(256, rows)
    whole = lambda shape: pl.BlockSpec(shape, lambda i: (0, 0))
    return pl.pallas_call(
        functools.partial(attend_kernel, heads, block),
        grid=(rows // block,),
        in_specs=[
            pl.BlockSpec((block, width), lambda i: (i, 0)),
            whole((rows, width)),
            whole((width, rows)),
        ],
        out_specs=[
            pl.BlockSpec((block, width), lambda i: (i, 0)),
            pl.BlockSpec((block, width), lambda i: (i, 0)),
            pl.BlockSpec((heads, block), lambda i: (0, i)),
        ],
        out_shape=[
            jax.ShapeDtypeStruct((rows, width), jnp.bfloat16),
            jax.ShapeDtypeStruct((rows, width), jnp.float32),
            jax.ShapeDtypeStruct((heads, rows), jnp.float32),
        ],
        scratch_shapes=[
            pltpu.VMEM((heads, block, width), jnp.bfloat16),
            pltpu.VMEM((width, block), jnp.float32),
            pltpu.VMEM((heads, 8, block), jnp.float32),
            pltpu.VMEM((heads, 8, block), jnp.float32),
        ],
        compiler_params=pltpu.CompilerParams(vmem_limit_bytes=32 * MIB),
        cost_estimate=pl.CostEstimate(
            flops=3 * rows * rows * width * heads,
            bytes_accessed=12 * rows * width,
            transcendentals=heads * rows * rows // 2,
        ),
        name="attend",
    )(q, k, v.T)


def attend_back_kernel(
    heads, block, q_ref, k_ref, kt_ref, v_ref, g_ref, log_ref, delta_ref,
    gq_ref, gk_ref, gv_ref, qh, gh, acc, acc_k, acc_v,
):
    i = pl.program_id(0)
    width = heads * HEAD_DIM
    scale = HEAD_DIM**-0.5
    scaled = q_ref[...] * jnp.asarray(scale, jnp.bfloat16)
    grads = g_ref[...]
    for h in range(heads):
        mask = head_mask(block, width, h)
        qh[pl.ds(h * block, block), :] = jnp.where(mask, scaled, jnp.zeros_like(scaled))
        gh[pl.ds(h * block, block), :] = jnp.where(mask, grads, jnp.zeros_like(grads))
    acc[...] = jnp.zeros_like(acc)

    @pl.when(i == 0)
    def _():
        acc_k[...] = jnp.zeros_like(acc_k)
        acc_v[...] = jnp.zeros_like(acc_v)

    nt = ((1,), (1,))

    def one(j, diagonal):
        at = pl.ds(j * block, block)
        keys, values = k_ref[at, :], v_ref[at, :]
        probs, raws = [], []
        for h in range(heads):
            s = dot(keys, qh[pl.ds(h * block, block), :], nt)
            p = jnp.exp(s - log_ref[pl.ds(h, 1), :])
            if diagonal:
                p = jnp.where(causal_tile(block), p, 0.0)
            dp = dot(values, gh[pl.ds(h * block, block), :], nt)
            raw = (p * (dp - delta_ref[pl.ds(h, 1), :])).astype(jnp.bfloat16)
            low = slice(h * HEAD_DIM, (h + 1) * HEAD_DIM)
            acc[low, :] = acc[low, :] + dot(kt_ref[low, at], raw)
            probs.append(p.astype(jnp.bfloat16))
            raws.append(raw)
        acc_v[at, :] = acc_v[at, :] + dot(jnp.concatenate(probs, axis=1), gh[...])
        acc_k[at, :] = acc_k[at, :] + dot(jnp.concatenate(raws, axis=1), qh[...])

    @pl.loop(0, i)
    def _(j):
        one(j, False)

    one(i, True)
    gq_ref[...] = (acc[...].T * scale).astype(jnp.bfloat16)

    @pl.when(i == pl.num_programs(0) - 1)
    def _():
        gk_ref[...] = acc_k[...].astype(jnp.bfloat16)
        gv_ref[...] = acc_v[...].astype(jnp.bfloat16)


def attend_back(q, k, v, grad, logs, delta):
    rows, width = q.shape
    heads = width // HEAD_DIM
    block = min(256, rows)
    whole = lambda shape: pl.BlockSpec(shape, lambda i: (0, 0))
    strip = pl.BlockSpec((block, width), lambda i: (i, 0))
    line = pl.BlockSpec((heads, block), lambda i: (0, i))
    low = jax.ShapeDtypeStruct((rows, width), jnp.bfloat16)
    return pl.pallas_call(
        functools.partial(attend_back_kernel, heads, block),
        grid=(rows // block,),
        in_specs=[strip, whole((rows, width)), whole((width, rows)), whole((rows, width)), strip, line, line],
        out_specs=[strip, whole((rows, width)), whole((rows, width))],
        out_shape=[low, low, low],
        scratch_shapes=[
            pltpu.VMEM((heads * block, width), jnp.bfloat16),
            pltpu.VMEM((heads * block, width), jnp.bfloat16),
            pltpu.VMEM((width, block), jnp.float32),
            pltpu.VMEM((rows, width), jnp.float32),
            pltpu.VMEM((rows, width), jnp.float32),
        ],
        compiler_params=pltpu.CompilerParams(vmem_limit_bytes=48 * MIB),
        cost_estimate=pl.CostEstimate(
            flops=5 * rows * rows * width * heads,
            bytes_accessed=14 * rows * width,
            transcendentals=heads * rows * rows // 2,
        ),
        name="attend_back",
    )(q, k, k.T, v, grad, logs, delta)


def swap_groups(x, axis):
    return lax.all_to_all(x, axis, split_axis=0, concat_axis=0, tiled=True)


def on_device(
    tokens,
    cotangent,
    w_qkv,
    w_out,
    w_fc_in,
    w_fc_out,
    norm1_gain,
    norm1_bias,
    norm2_gain,
    norm2_bias,
    coef_weight,
    expert_up,
    expert_down,
    routes,
    keep_mask,
):
    rows, width = tokens.shape
    n_es = lax.axis_size("es")
    experts = lax.axis_size("ep")
    me_scalar = lax.axis_index("ep") * n_es + lax.axis_index("es")
    me = me_scalar.astype(jnp.int32).reshape(1)
    me_es = lax.axis_index("es").astype(jnp.int32).reshape(1)
    ep_up, es_up = digits("ep"), digits("es")
    order_a = ep_up[:0:-1] + ep_up[:1] + es_up[:0:-1] + es_up[:1]
    order_b = es_up[:0:-1] + ep_up[:0:-1] + ep_up[:1] + es_up[:1]
    order_e = es_up[::-1]

    full_qkv = gather_rows(w_qkv, (order_a, order_b), me)
    packed = jnp.concatenate(
        [
            jnp.stack([norm1_gain, norm1_bias, norm2_gain, norm2_bias]),
            coef_weight.T,
        ],
        axis=0,
    )
    small = gather_small(packed, order_a, me_scalar).transpose(1, 0, 2).reshape(6, width)
    small = small.astype(jnp.float32)
    gain_one, bias_one, gain_two, bias_two = (small[i : i + 1] for i in range(4))
    coef_full = small[4:6]
    full_out = gather_rows(w_out, (order_a, order_b), me)
    full_fc_in = gather_rows(w_fc_in, (order_a, order_b), me)
    full_fc_out = gather_rows(w_fc_out, (order_a, order_b), me)
    full_up = gather_rows(expert_up[0], (order_e,), me_es)
    full_down = gather_rows(expert_down[0], (order_e,), me_es)

    group = width // n_es
    inputs = tokens.astype(jnp.float32)
    normed_one, unit_one, inverse_one = norm_forward(inputs, gain_one, bias_one)
    normed_one_low = normed_one.astype(jnp.bfloat16)
    qkv_low = dot(normed_one_low, full_qkv).astype(jnp.bfloat16)
    by_group = qkv_low.reshape(rows, 3, n_es, group).transpose(2, 0, 1, 3).reshape(n_es, rows, 3 * group)
    mine = swap_groups(by_group, "es").reshape(n_es * rows, 3 * group)
    q, k, v = mine[:, :group], mine[:, group : 2 * group], mine[:, 2 * group :]
    attended_mine, attended_full, logs = attend(q, k, v)
    attended = (
        swap_groups(attended_mine.reshape(n_es, rows, group), "es").transpose(1, 0, 2).reshape(rows, width)
    )
    hidden = inputs + dot(attended, full_out)
    normed_two, unit_two, inverse_two = norm_forward(hidden, gain_two, bias_two)
    normed_two_low = normed_two.astype(jnp.bfloat16)
    coefficients = softmax_pair(
        lax.dot_general(normed_two, coef_full, (((1,), (1,)), ((), ())), precision=HIGHEST)
    )
    keep = keep_mask.astype(jnp.float32)[:, None]
    grad_out = cotangent.astype(jnp.float32)
    grad_dense_low = (coefficients[:, 0:1] * grad_out).astype(jnp.bfloat16)
    grad_expert_low = (coefficients[:, 1:2] * keep * grad_out).astype(jnp.bfloat16)

    capacity = 2 * rows // experts
    expert_ids = routes[:, 0]
    chosen = (expert_ids[:, None] == lax.broadcasted_iota(jnp.int32, (1, experts), 1)).astype(jnp.float32)
    before = (
        lax.broadcasted_iota(jnp.int32, (rows, rows), 1) < lax.broadcasted_iota(jnp.int32, (rows, rows), 0)
    ).astype(jnp.float32)
    ranks = jnp.sum(dot(before, chosen) * chosen, axis=1).astype(jnp.int32)
    slots = expert_ids * capacity + ranks
    in_slot = (slots[None, :] == lax.broadcasted_iota(jnp.int32, (experts * capacity, 1), 0)).astype(
        jnp.bfloat16
    )
    outgoing = dot(in_slot, jnp.concatenate([normed_two_low, grad_expert_low], axis=1)).astype(jnp.bfloat16)
    received = swap_groups(outgoing.reshape(experts, capacity, 2 * width), "ep").reshape(
        experts * capacity, 2 * width
    )
    expert_in, expert_grad = received[:, :width], received[:, width:]

    inner = dot(normed_two_low, full_fc_in)
    activated, slope = gelu_and_slope(inner)
    activated_low = activated.astype(jnp.bfloat16)
    dense = dot(activated_low, full_fc_out)
    grad_fc_out = dot(activated_low, grad_dense_low, ((0,), (0,))).astype(jnp.bfloat16)
    grad_inner_low = (dot(grad_dense_low, full_fc_out, ((1,), (1,))) * slope).astype(jnp.bfloat16)
    grad_fc_in = dot(normed_two_low, grad_inner_low, ((0,), (0,))).astype(jnp.bfloat16)
    grad_normed_dense = dot(grad_inner_low, full_fc_in, ((1,), (1,)))

    expert_inner = dot(expert_in, full_up, ((1,), (1,)))
    expert_act, expert_slope = gelu_and_slope(expert_inner)
    expert_act_low = expert_act.astype(jnp.bfloat16)
    expert_out = dot(expert_act_low, full_down).astype(jnp.bfloat16)
    grad_expert_inner = (dot(expert_grad, full_down, ((1,), (1,))) * expert_slope).astype(jnp.bfloat16)
    grad_expert_in = dot(grad_expert_inner, full_up).astype(jnp.bfloat16)
    returned = swap_groups(
        jnp.concatenate([expert_out, grad_expert_in], axis=1).reshape(experts, capacity, 2 * width), "ep"
    ).reshape(experts * capacity, 2 * width)
    grad_down = dot(expert_act_low, expert_grad, ((0,), (0,))).astype(jnp.bfloat16)
    grad_up = dot(grad_expert_inner, expert_in, ((0,), (0,))).astype(jnp.bfloat16)
    at_home = dot(in_slot, returned, ((0,), (0,)))
    expert_tokens = at_home[:, :width] * keep
    grad_expert_home = at_home[:, width:]

    mixed = hidden + coefficients[:, 0:1] * dense + coefficients[:, 1:2] * expert_tokens
    out_tokens = mixed.astype(jnp.bfloat16)
    grad_pair = jnp.concatenate(
        [
            jnp.sum(grad_out * dense, axis=1, keepdims=True),
            jnp.sum(grad_out * expert_tokens, axis=1, keepdims=True),
        ],
        axis=1,
    )
    grad_logits = coefficients * (
        grad_pair - jnp.sum(coefficients * grad_pair, axis=1, keepdims=True)
    )
    grad_coef = lax.dot_general(grad_logits, normed_two, (((0,), (0,)), ((), ())), precision=HIGHEST)
    grad_normed_two = (
        grad_normed_dense
        + grad_expert_home
        + grad_logits[:, 0:1] * coef_full[0:1]
        + grad_logits[:, 1:2] * coef_full[1:2]
    )
    grad_hidden_norm, grad_gain_two, grad_bias_two = norm_backward(
        grad_normed_two, unit_two, inverse_two, gain_two
    )
    grad_hidden = grad_out + grad_hidden_norm
    grad_att_low = grad_hidden.astype(jnp.bfloat16)
    grad_w_out = dot(attended, grad_att_low, ((0,), (0,))).astype(jnp.bfloat16)
    grad_attended = dot(grad_att_low, full_out, ((1,), (1,))).astype(jnp.bfloat16)

    grad_mine = swap_groups(grad_attended.reshape(rows, n_es, group).transpose(1, 0, 2), "es").reshape(
        n_es * rows, group
    )
    per_head = (
        lax.broadcasted_iota(jnp.int32, (group // HEAD_DIM, group), 1) // HEAD_DIM
        == lax.broadcasted_iota(jnp.int32, (group // HEAD_DIM, group), 0)
    ).astype(jnp.float32)
    delta = lax.dot_general(
        per_head,
        grad_mine.astype(jnp.float32) * attended_full,
        (((1,), (1,)), ((), ())),
        precision=HIGHEST,
    )
    grad_q, grad_k, grad_v = attend_back(q, k, v, grad_mine, logs, delta)
    grad_qkv_low = (
        swap_groups(
            jnp.concatenate([grad_q, grad_k, grad_v], axis=1).reshape(n_es, rows, 3 * group), "es"
        )
        .reshape(n_es, rows, 3, group)
        .transpose(1, 2, 0, 3)
        .reshape(rows, 3 * width)
    )
    grad_w_qkv = dot(normed_one_low, grad_qkv_low, ((0,), (0,))).astype(jnp.bfloat16)
    grad_inputs_norm, grad_gain_one, grad_bias_one = norm_backward(
        dot(grad_qkv_low, full_qkv, ((1,), (1,))), unit_one, inverse_one, gain_one
    )
    grad_tokens = grad_hidden + grad_inputs_norm

    back_a, back_b, back_e = order_a[::-1], order_b[::-1], order_e[::-1]

    def sum_halves(partial):
        half = partial.shape[1] // 2
        return jnp.concatenate(
            [scatter_sum(partial[:, :half], back_a), scatter_sum(partial[:, half:], back_b)], axis=1
        )

    small_grads = jnp.stack(
        [grad_gain_one, grad_bias_one, grad_gain_two, grad_bias_two, grad_coef[0], grad_coef[1]]
    )
    count = experts * n_es
    small_sum = scatter_sum(
        small_grads.reshape(6, count, width // count).transpose(1, 0, 2).reshape(count * 6, width // count),
        back_a,
        jnp.float32,
    )
    return (
        out_tokens,
        grad_tokens,
        sum_halves(grad_w_qkv),
        sum_halves(grad_w_out),
        sum_halves(grad_fc_in),
        sum_halves(grad_fc_out),
        small_sum[0],
        small_sum[1],
        small_sum[2],
        small_sum[3],
        small_sum[4:6].T,
        scatter_sum(grad_up, back_e)[None],
        scatter_sum(grad_down, back_e)[None],
    )


def solution(mesh):
    both = P(BOTH)
    table = P(BOTH, None)
    stack = P("ep", "es", None)
    return jax.shard_map(
        on_device,
        mesh=mesh,
        in_specs=(table,) * 6 + (both,) * 4 + (table, stack, stack, table, both),
        out_specs=(table,) * 6 + (both,) * 4 + (table, stack, stack),
        check_vma=False,
    )
```

```python
import functools

import jax
import jax.numpy as jnp
import numpy as np
from jax import lax
from jax.experimental import pallas as pl
from jax.experimental.pallas import tpu as pltpu
from jax.sharding import PartitionSpec as P

HEADS = 16
HEAD_DIM = 64
EPSILON = 1e-05
MASKED = -1e30
HIGHEST = lax.Precision.HIGHEST
BOTH = ("ep", "es")
MIB = 1 << 20


def norm_forward(values, gain, offset):
    average = jnp.mean(values, axis=-1, keepdims=True)
    centred = values - average
    variance = jnp.mean(centred * centred, axis=-1, keepdims=True)
    inverse = lax.rsqrt(variance + EPSILON)
    unit = centred * inverse
    return unit * gain + offset, unit, inverse


def norm_backward(grad, unit, inverse, gain):
    scaled = grad * gain
    mean_scaled = jnp.mean(scaled, axis=-1, keepdims=True)
    mean_unit = jnp.mean(scaled * unit, axis=-1, keepdims=True)
    grad_in = (scaled - mean_scaled - unit * mean_unit) * inverse
    return grad_in, jnp.sum(grad * unit, axis=0), jnp.sum(grad, axis=0)


def gelu_and_slope(values):
    cdf = 0.5 * (1.0 + lax.erf(values * (2.0**-0.5)))
    density = jnp.exp(-0.5 * values * values) * ((2.0 * np.pi) ** -0.5)
    return values * cdf, cdf + values * density


def dot(left, right, contract=((1,), (0,)), out=jnp.float32):
    return lax.dot_general(left, right, (contract, ((), ())), preferred_element_type=out)


def softmax_pair(logits):
    largest = jnp.max(logits, axis=-1, keepdims=True)
    expanded = jnp.exp(logits - largest)
    return expanded / jnp.sum(expanded, axis=-1, keepdims=True)


def digits(axis):
    size = lax.axis_size(axis)
    return [(axis, 1 << b) for b in range(size.bit_length() - 1)]


def exchange(x, digit):
    axis, stride = digit
    size = lax.axis_size(axis)
    return lax.ppermute(x, axis, [(i, i ^ stride) for i in range(size)])


def after(x, *others):
    return lax.optimization_barrier((x, *others))[0]


def weights_of(order):
    inner = 1 << sum(axis == "es" for axis, _ in order)
    return {(axis, stride): stride * (inner if axis == "ep" else 1) for axis, stride in order}


def relative_numbers(order):
    numbers, weights = [0], weights_of(order)
    for digit in order:
        numbers = numbers + [n + weights[digit] for n in numbers]
    return numbers


def gather_pieces(shard, order, hold=None):
    pieces = [shard]
    for number, digit in enumerate(order):
        if number == len(order) - 1 and hold is not None:
            pieces = [after(piece, hold) for piece in pieces]
        pieces = pieces + [exchange(piece, digit) for piece in pieces]
    return pieces


def gather_relative(shard, order, hold=None):
    held = shard[None]
    for number, digit in enumerate(order[:-1]):
        held = jnp.concatenate([held, exchange(held, digit)], axis=0)
        if number == len(order) - 2 and hold is not None:
            held = after(held, hold)
    return held, exchange(held, order[-1])


def place_kernel(plan, outputs, me_ref, *refs):
    sems_in, sems_out = refs[-2:]
    inputs = len(refs) - 2 - outputs - len({step[2] for step in plan})
    outs, held = refs[inputs : inputs + outputs], refs[inputs + outputs : -2]
    me = me_ref[0]
    arriving, leaving = [], []
    for which, row, chain, slot, relative, rows, segments in plan:
        here = held[chain].at[pl.ds(slot * rows, rows), :]
        copy = pltpu.make_async_copy(refs[which].at[row], here, sems_in.at[len(arriving)])
        copy.start()
        arriving.append(copy)
        start = pl.multiple_of((me ^ relative) * rows, rows)
        group = []
        for place, out, first, width in segments:
            group.append(
                pltpu.make_async_copy(
                    held[chain].at[pl.ds(slot * rows, rows), pl.ds(place, width)],
                    outs[out].at[pl.ds(start, rows), pl.ds(first, width)],
                    sems_out.at[sum(map(len, leaving)) + len(group)],
                )
            )
        leaving.append(group)
    for copy, group in zip(arriving, leaving):
        copy.wait()
        for out in group:
            out.start()
    for group in leaving:
        for out in group:
            out.wait()


def gather_rows(shards, chains, me, hold=None):
    rows = shards[0].shape[0]
    count = 1 << len(chains[0][0])
    if rows % 16 or any(w % 128 or f % 128 for _, ranges in chains for _, f, w in ranges):
        axes = tuple(a for a in BOTH if any(d[0] == a for d in chains[0][0]))
        return [lax.all_gather(shard, axes, axis=0, tiled=True) for shard in shards]
    parts, plan, widths = [], [], []
    for chain, (order, ranges) in enumerate(chains):
        numbers = relative_numbers(order)
        segments, place = [], 0
        for index, first, width in ranges:
            segments.append((place, index, first, width))
            place += width
        widths.append(place)
        cut = [shards[index][:, first : first + width] for index, first, width in ranges]
        joined = cut[0] if len(cut) == 1 else jnp.concatenate(cut, axis=1)
        for half, part in enumerate(gather_relative(joined, order, None if chain else hold)):
            for row in range(count // 2):
                slot = half * (count // 2) + row
                plan.append((len(parts), row, chain, slot, numbers[slot], rows, tuple(segments)))
            parts.append(part)
    return pl.pallas_call(
        functools.partial(place_kernel, tuple(plan), len(shards)),
        out_shape=[jax.ShapeDtypeStruct((count * rows, s.shape[1]), s.dtype) for s in shards],
        in_specs=[pl.BlockSpec(memory_space=pltpu.SMEM)] + [pl.BlockSpec(memory_space=pl.ANY)] * len(parts),
        out_specs=[pl.BlockSpec(memory_space=pl.ANY)] * len(shards),
        scratch_shapes=[pltpu.VMEM((count * rows, w), shards[0].dtype) for w in widths]
        + [
            pltpu.SemaphoreType.DMA((len(plan),)),
            pltpu.SemaphoreType.DMA((sum(len(step[-1]) for step in plan),)),
        ],
        compiler_params=pltpu.CompilerParams(vmem_limit_bytes=16 * MIB),
        name="place_rows",
    )(me, *parts)


def fold_pieces(pieces, digit):
    half = len(pieces) // 2
    return [
        kept.astype(jnp.float32) + exchange(sent.astype(jnp.bfloat16), digit).astype(jnp.float32)
        for kept, sent in zip(pieces[:half], pieces[half:])
    ]


def fold_all_but_last(pieces, order):
    for digit in order[:0:-1]:
        pieces = [piece.astype(jnp.bfloat16) for piece in fold_pieces(pieces, digit)]
    return pieces


def sum_pieces(pieces, order):
    for digit in order[::-1]:
        pieces = fold_pieces(pieces, digit)
    return pieces[0]


def scatter_sum(partial, order, hold=None, taps=None):
    count = 1 << len(order)
    rows = partial.shape[0] // count
    remaining = sorted(order, key=weights_of(order).get, reverse=True)
    held = partial.reshape((2,) * len(order) + (rows,) + partial.shape[1:])
    for number, digit in enumerate(order):
        axis, stride = digit
        place = remaining.index(digit)
        remaining.remove(digit)
        bit = (lax.axis_index(axis) // stride) % 2
        mine = lax.dynamic_index_in_dim(held, bit, place, keepdims=False)
        theirs = lax.dynamic_index_in_dim(held, 1 - bit, place, keepdims=False)
        held = mine.astype(jnp.float32) + exchange(theirs, digit).astype(jnp.float32)
        if number < len(order) - 1:
            held = held.astype(jnp.bfloat16)
        if taps is not None:
            taps.append(held)
        if number == 0 and hold is not None:
            held = after(held, *hold)
    return held


def norm_place_kernel(per, me_ref, *refs):
    gain_ref, bias_ref, out_ref = refs[-3:]
    for number, ref in enumerate(refs[:-3]):

        @pl.when(pl.program_id(0) // per == number)
        def _():
            values = ref[...].astype(jnp.float32)
            out_ref[...] = norm_forward(values, gain_ref[...], bias_ref[...])[0].astype(jnp.bfloat16)


def place_normed(pieces, order, me, gain, bias):
    rows, width = pieces[0].shape
    step = min(256, rows)
    per = rows // step
    weights = weights_of(order)

    def target(i, me_ref):
        block = me_ref[0]
        for bit, digit in enumerate(order):
            block = block ^ ((((i // per) >> bit) & 1) * weights[digit])
        return (block * per + i % per, 0)

    def source(number):
        return lambda i, me_ref: (jnp.clip(i - number * per, 0, per - 1), 0)

    line = pl.BlockSpec((1, width), lambda i, me_ref: (0, 0))
    return pl.pallas_call(
        functools.partial(norm_place_kernel, per),
        grid_spec=pltpu.PrefetchScalarGridSpec(
            num_scalar_prefetch=1,
            grid=(len(pieces) * per,),
            in_specs=[pl.BlockSpec((step, width), source(n)) for n in range(len(pieces))] + [line, line],
            out_specs=pl.BlockSpec((step, width), target),
        ),
        out_shape=jax.ShapeDtypeStruct((len(pieces) * rows, width), jnp.bfloat16),
        compiler_params=pltpu.CompilerParams(vmem_limit_bytes=24 * MIB),
        name="norm_place",
    )(me, *pieces, gain, bias)


def head_mask(rows, width, head):
    lane = lax.broadcasted_iota(jnp.int32, (rows, width), 1)
    return (lane // HEAD_DIM) == head


def causal_tile(block):
    key = lax.broadcasted_iota(jnp.int32, (block, block), 0)
    query = lax.broadcasted_iota(jnp.int32, (block, block), 1)
    return key <= query


def flip(dst, src, block):
    for start in range(0, src.shape[0], block):
        dst[:, start : start + block] = src[start : start + block, :].T


def attend_kernel(heads, block, q_ref, k_ref, v_ref, low_ref, full_ref, log_ref, vt, qh, acc, top, total):
    i = pl.program_id(0)
    width = heads * HEAD_DIM

    @pl.when(i == 0)
    def _():
        flip(vt, v_ref, block)

    scaled = q_ref[...] * jnp.asarray(HEAD_DIM**-0.5, jnp.bfloat16)
    for h in range(heads):
        qh[h] = jnp.where(head_mask(block, width, h), scaled, jnp.zeros_like(scaled))
    acc[...] = jnp.zeros_like(acc)
    total[...] = jnp.zeros_like(total)
    top[...] = jnp.full_like(top, MASKED)
    nt = ((1,), (1,))

    def scores(j, h, diagonal):
        s = dot(k_ref[pl.ds(j * block, block), :], qh[h], nt)
        return jnp.where(causal_tile(block), s, MASKED) if diagonal else s

    def find_top(j, diagonal):
        for h in range(heads):
            s = scores(j, h, diagonal)
            folded = jnp.max(s.reshape(block // 8, 8, block), axis=0)
            top[h] = jnp.maximum(top[h], folded)

    def add_block(j, diagonal):
        for h in range(heads):
            s = scores(j, h, diagonal)
            p = jnp.exp(s - top[h, pl.ds(0, 1), :])
            total[h] = total[h] + jnp.sum(p.reshape(block // 8, 8, block), axis=0)
            low = slice(h * HEAD_DIM, (h + 1) * HEAD_DIM)
            acc[low, :] = acc[low, :] + dot(vt[low, pl.ds(j * block, block)], p.astype(jnp.bfloat16))

    @pl.loop(0, i)
    def _(j):
        find_top(j, False)

    find_top(i, True)
    for h in range(heads):
        top[h] = jnp.broadcast_to(jnp.max(top[h], axis=0, keepdims=True), top.shape[1:])

    @pl.loop(0, i)
    def _(j):
        add_block(j, False)

    add_block(i, True)
    for h in range(heads):
        summed = jnp.sum(total[h], axis=0, keepdims=True)
        log_ref[pl.ds(h, 1), :] = top[h, pl.ds(0, 1), :] + jnp.log(summed)
        low = slice(h * HEAD_DIM, (h + 1) * HEAD_DIM)
        acc[low, :] = acc[low, :] / summed
    out = acc[...].T
    full_ref[...] = out
    low_ref[...] = out.astype(jnp.bfloat16)


def column(rows, width, place):
    return pl.BlockSpec((rows, width), lambda i: (0, place))


def attend(qkv):
    rows = qkv.shape[0]
    width = qkv.shape[1] // 3
    heads = width // HEAD_DIM
    block = min(256, rows)
    strip = pl.BlockSpec((block, width), lambda i: (i, 0))
    return pl.pallas_call(
        functools.partial(attend_kernel, heads, block),
        grid=(rows // block,),
        in_specs=[strip, column(rows, width, 1), column(rows, width, 2)],
        out_specs=[strip, strip, pl.BlockSpec((heads, block), lambda i: (0, i))],
        out_shape=[
            jax.ShapeDtypeStruct((rows, width), jnp.bfloat16),
            jax.ShapeDtypeStruct((rows, width), jnp.float32),
            jax.ShapeDtypeStruct((heads, rows), jnp.float32),
        ],
        scratch_shapes=[
            pltpu.VMEM((width, rows), jnp.bfloat16),
            pltpu.VMEM((heads, block, width), jnp.bfloat16),
            pltpu.VMEM((width, block), jnp.float32),
            pltpu.VMEM((heads, 8, block), jnp.float32),
            pltpu.VMEM((heads, 8, block), jnp.float32),
        ],
        compiler_params=pltpu.CompilerParams(vmem_limit_bytes=32 * MIB),
        cost_estimate=pl.CostEstimate(flops=MIB, bytes_accessed=MIB, transcendentals=0),
        name="attend",
    )(qkv, qkv, qkv)


def attend_back_kernel(
    heads, block, q_ref, k_ref, v_ref, g_ref, o_ref, log_ref, out_ref,
    kt, qh, gh, delta, acc, acc_k, acc_v,
):
    i = pl.program_id(0)
    width = heads * HEAD_DIM
    scale = HEAD_DIM**-0.5
    nt = ((1,), (1,))

    @pl.when(i == 0)
    def _():
        flip(kt, k_ref, block)
        acc_k[...] = jnp.zeros_like(acc_k)
        acc_v[...] = jnp.zeros_like(acc_v)

    scaled = q_ref[...] * jnp.asarray(scale, jnp.bfloat16)
    grads = g_ref[...]
    for h in range(heads):
        mask = head_mask(block, width, h)
        qh[pl.ds(h * block, block), :] = jnp.where(mask, scaled, jnp.zeros_like(scaled))
        gh[pl.ds(h * block, block), :] = jnp.where(mask, grads, jnp.zeros_like(grads))
    per_head = (
        lax.broadcasted_iota(jnp.int32, (8, width), 1) // HEAD_DIM
        == lax.broadcasted_iota(jnp.int32, (8, width), 0)
    ).astype(jnp.float32)
    delta[...] = lax.dot_general(
        per_head, grads.astype(jnp.float32) * o_ref[...], (nt, ((), ())), precision=HIGHEST,
        preferred_element_type=jnp.float32,
    )
    acc[...] = jnp.zeros_like(acc)

    def one(j, diagonal):
        at = pl.ds(j * block, block)
        keys, values = k_ref[at, :], v_ref[at, :]
        probs, raws = [], []
        for h in range(heads):
            s = dot(keys, qh[pl.ds(h * block, block), :], nt)
            p = jnp.exp(s - log_ref[pl.ds(h, 1), :])
            if diagonal:
                p = jnp.where(causal_tile(block), p, 0.0)
            dp = dot(values, gh[pl.ds(h * block, block), :], nt)
            raw = (p * (dp - delta[pl.ds(h, 1), :])).astype(jnp.bfloat16)
            low = slice(h * HEAD_DIM, (h + 1) * HEAD_DIM)
            acc[low, :] = acc[low, :] + dot(kt[low, at], raw)
            probs.append(p.astype(jnp.bfloat16))
            raws.append(raw)
        acc_v[at, :] = acc_v[at, :] + dot(jnp.concatenate(probs, axis=1), gh[...])
        acc_k[at, :] = acc_k[at, :] + dot(jnp.concatenate(raws, axis=1), qh[...])

    @pl.loop(0, i)
    def _(j):
        one(j, False)

    one(i, True)
    out_ref[pl.ds(pl.multiple_of(i * block, block), block), :width] = (acc[...].T * scale).astype(jnp.bfloat16)

    @pl.when(i == pl.num_programs(0) - 1)
    def _():
        out_ref[:, width : 2 * width] = acc_k[...].astype(jnp.bfloat16)
        out_ref[:, 2 * width :] = acc_v[...].astype(jnp.bfloat16)


def attend_back(qkv, grad, full, logs):
    rows, width = grad.shape
    heads = width // HEAD_DIM
    block = min(256, rows)
    strip = pl.BlockSpec((block, width), lambda i: (i, 0))
    return pl.pallas_call(
        functools.partial(attend_back_kernel, heads, block),
        grid=(rows // block,),
        in_specs=[
            strip,
            column(rows, width, 1),
            column(rows, width, 2),
            strip,
            strip,
            pl.BlockSpec((heads, block), lambda i: (0, i)),
        ],
        out_specs=pl.BlockSpec((rows, 3 * width), lambda i: (0, 0)),
        out_shape=jax.ShapeDtypeStruct((rows, 3 * width), jnp.bfloat16),
        scratch_shapes=[
            pltpu.VMEM((width, rows), jnp.bfloat16),
            pltpu.VMEM((heads * block, width), jnp.bfloat16),
            pltpu.VMEM((heads * block, width), jnp.bfloat16),
            pltpu.VMEM((8, block), jnp.float32),
            pltpu.VMEM((width, block), jnp.float32),
            pltpu.VMEM((rows, width), jnp.float32),
            pltpu.VMEM((rows, width), jnp.float32),
        ],
        compiler_params=pltpu.CompilerParams(vmem_limit_bytes=48 * MIB),
        cost_estimate=pl.CostEstimate(flops=32 * rows * rows * width * heads // 2, bytes_accessed=14 * rows * width, transcendentals=0),
        name="attend_back",
    )(qkv, qkv, qkv, grad, full, logs)


def swap_groups(x, axis):
    return lax.all_to_all(x, axis, split_axis=0, concat_axis=0, tiled=True)


def on_device(
    tokens,
    cotangent,
    w_qkv,
    w_out,
    w_fc_in,
    w_fc_out,
    norm1_gain,
    norm1_bias,
    norm2_gain,
    norm2_bias,
    coef_weight,
    expert_up,
    expert_down,
    routes,
    keep_mask,
):
    rows, width = tokens.shape
    n_es = lax.axis_size("es")
    n_ep = lax.axis_size("ep")
    me_es = lax.axis_index("es").astype(jnp.int32).reshape(1)
    me_ep = lax.axis_index("ep").astype(jnp.int32).reshape(1)
    ep_up, es_up = digits("ep"), digits("es")
    order_e = es_up[::-1]
    order_z = ep_up[::-1]
    order_y = ep_up[:1] + ep_up[:0:-1]
    group = width // n_es
    stripe = w_qkv.shape[0]
    block = w_fc_out.shape[0]
    units = n_ep * block
    tile = 128

    packed = jnp.concatenate(
        [jnp.stack([norm1_gain, norm1_bias, norm2_gain, norm2_bias]), coef_weight.T], axis=0
    )
    packed = jnp.pad(packed, ((0, stripe - packed.shape[0]), (0, tile - stripe)))
    shared = swap_groups(
        jnp.concatenate(
            [
                w_qkv.reshape(stripe, 3, n_es, group).transpose(2, 0, 1, 3).reshape(n_es, stripe, 3 * group),
                jnp.broadcast_to(packed, (n_es, stripe, tile)),
            ],
            axis=2,
        ),
        "es",
    ).reshape(n_es * stripe, 3 * group + tile)
    own_heads, own_small = shared[:, : 3 * group], shared[:, 3 * group :]
    token_pieces = gather_pieces(after(tokens, shared), order_e)
    by_units = w_fc_in.reshape(stripe, n_ep, n_es, block).transpose(2, 0, 1, 3).reshape(n_es, stripe, units)
    more = swap_groups(
        after(jnp.concatenate([by_units, jnp.broadcast_to(w_out, (n_es, *w_out.shape))], axis=2), shared), "es"
    ).reshape(n_es * stripe, units + width)
    cut = 2 * group
    w_heads, small = gather_rows(
        [own_heads, own_small],
        [(order_z, ((0, 0, cut),)), (order_y, ((0, cut, 3 * group - cut), (1, 0, tile)))],
        me_ep,
        token_pieces[1],
    )
    small = small.reshape(n_ep * n_es, stripe, tile)[:, :6, :stripe].transpose(1, 0, 2).reshape(6, width)
    small = small.astype(jnp.float32)
    gain_one, bias_one, gain_two, bias_two = (small[i : i + 1] for i in range(4))
    coef_full = small[4:6]
    normed_all = place_normed(token_pieces, order_e, me_es, gain_one, bias_one)
    dense_weights = lax.all_gather(
        after(jnp.concatenate([more, w_fc_out], axis=1), w_heads), "ep", axis=0, tiled=True
    )
    w_in, full_out, w_back = (
        dense_weights[:, :units],
        dense_weights[:, units : units + width],
        dense_weights[:, units + width :],
    )
    ups = gather_pieces(after(expert_up[0], token_pieces[1]), order_e)

    inputs = tokens.astype(jnp.float32)
    qkv = after(dot(normed_all, w_heads).astype(jnp.bfloat16), ups[2])
    attended_mine, attended_full, logs = attend(qkv)
    attended_mine = after(attended_mine, ups[1])
    attended = (
        swap_groups(attended_mine.reshape(n_es, rows, group), "es").transpose(1, 0, 2).reshape(rows, width)
    )
    hidden = inputs + dot(attended, full_out)
    normed_two, unit_two, inverse_two = norm_forward(hidden, gain_two, bias_two)
    normed_two_low = normed_two.astype(jnp.bfloat16)
    coefficients = softmax_pair(
        lax.dot_general(normed_two, coef_full, (((1,), (1,)), ((), ())), precision=HIGHEST)
    )
    keep = keep_mask.astype(jnp.float32)[:, None]
    grad_out = cotangent.astype(jnp.float32)
    grad_dense_low = (coefficients[:, 0:1] * grad_out).astype(jnp.bfloat16)
    grad_expert_low = (coefficients[:, 1:2] * keep * grad_out).astype(jnp.bfloat16)

    capacity = 2 * rows // n_ep
    expert_ids = routes[:, 0]
    chosen = (expert_ids[:, None] == lax.broadcasted_iota(jnp.int32, (1, n_ep), 1)).astype(jnp.float32)
    before = (
        lax.broadcasted_iota(jnp.int32, (rows, rows), 1) < lax.broadcasted_iota(jnp.int32, (rows, rows), 0)
    ).astype(jnp.float32)
    ranks = jnp.sum(dot(before, chosen) * chosen, axis=1).astype(jnp.int32)
    slots = expert_ids * capacity + ranks
    in_slot = (slots[None, :] == lax.broadcasted_iota(jnp.int32, (n_ep * capacity, 1), 0)).astype(
        jnp.bfloat16
    )

    def to_experts(values):
        return swap_groups(values.reshape(n_ep, capacity, width), "ep").reshape(n_ep * capacity, width)

    outgoing = dot(in_slot, normed_two_low).astype(jnp.bfloat16)
    downs = gather_pieces(after(expert_down[0], attended), order_e, outgoing)
    full_up, full_down = jnp.concatenate(ups, axis=0), jnp.concatenate(downs, axis=0)
    expert_in = to_experts(outgoing)
    expert_grad = to_experts(
        after(dot(in_slot, grad_expert_low).astype(jnp.bfloat16), expert_in, full_up, downs[1])
    )

    def split_pieces(values):
        return [values[i * rows : (i + 1) * rows] for i in range(n_es)]

    acts, expert_slope = gelu_and_slope(dot(expert_in, full_up, ((1,), (1,))))
    acts = acts.astype(jnp.bfloat16)
    expert_out = dot(acts, full_down).astype(jnp.bfloat16)
    dense_in = jnp.concatenate(gather_pieces(normed_two_low, order_e, acts), axis=0)
    grad_pieces = gather_pieces(grad_dense_low, order_e, expert_out)
    dense_grad = jnp.concatenate(grad_pieces, axis=0)
    inner = dot(after(dense_in, expert_out), w_in)
    activated, slope = gelu_and_slope(inner)
    activated_low = activated.astype(jnp.bfloat16)
    dense_part = dot(activated_low, w_back).astype(jnp.bfloat16)
    dense_folded = fold_all_but_last(split_pieces(dense_part), order_e)
    expert_grad = after(expert_grad, expert_out, dense_part)
    grad_inners = (dot(expert_grad, full_down, ((1,), (1,))) * expert_slope).astype(jnp.bfloat16)
    grad_expert_in = dot(after(grad_inners, dense_folded[1]), full_up).astype(jnp.bfloat16)
    home = swap_groups(
        jnp.stack([v.reshape(n_ep, capacity, width) for v in (expert_out, grad_expert_in)], axis=1), "ep"
    )
    out_home, grad_home = (home[:, i].reshape(n_ep * capacity, width) for i in range(2))

    dense = sum_pieces(dense_folded, order_e[:1])
    grad_inner_low = (dot(after(dense_grad, grad_expert_in), w_back, ((1,), (1,))) * slope).astype(jnp.bfloat16)
    grad_normed_part = dot(after(grad_inner_low, dense), w_in, ((1,), (1,))).astype(jnp.bfloat16)
    grad_normed_folded = fold_all_but_last(split_pieces(grad_normed_part), order_e)
    grad_normed_dense = sum_pieces(grad_normed_folded, order_e[:1])

    def outer_fold(left, right, hold):
        half = left.shape[1] // 2
        sent = exchange(dot(left[:, half:], right, ((0,), (0,))).astype(jnp.bfloat16), order_e[-1])
        kept = dot(left[:, :half], after(right, hold), ((0,), (0,))).astype(jnp.bfloat16)
        size = half // (n_es // 2)
        pieces = [
            (kept[i : i + size].astype(jnp.float32) + sent[i : i + size].astype(jnp.float32)).astype(jnp.bfloat16)
            for i in range(0, half, size)
        ]
        return fold_all_but_last(pieces, order_e[:-1])

    grad_ups = outer_fold(grad_inners, after(expert_in, grad_normed_part), grad_normed_folded[1])
    last_ups = exchange(after(grad_ups[1], grad_normed_dense), order_e[0])
    late_in, late_grad = after(dense_in, *grad_ups), after(dense_grad, *grad_ups)
    grad_w_back = dot(activated_low, late_grad, ((0,), (0,))).astype(jnp.bfloat16)
    grad_w_in = dot(late_in, grad_inner_low, ((0,), (0,))).astype(jnp.bfloat16)
    out_home = after(out_home, last_ups, grad_w_back, grad_w_in)
    expert_tokens = dot(in_slot, out_home, ((0,), (0,))) * keep
    grad_expert_home = dot(in_slot, grad_home, ((0,), (0,)))

    mixed = hidden + coefficients[:, 0:1] * dense + coefficients[:, 1:2] * expert_tokens
    out_tokens = mixed.astype(jnp.bfloat16)
    grad_pair = jnp.concatenate(
        [
            jnp.sum(grad_out * dense, axis=1, keepdims=True),
            jnp.sum(grad_out * expert_tokens, axis=1, keepdims=True),
        ],
        axis=1,
    )
    grad_logits = coefficients * (
        grad_pair - jnp.sum(coefficients * grad_pair, axis=1, keepdims=True)
    )
    grad_coef = lax.dot_general(grad_logits, normed_two, (((0,), (0,)), ((), ())), precision=HIGHEST)
    grad_normed_two = (
        grad_normed_dense
        + grad_expert_home
        + grad_logits[:, 0:1] * coef_full[0:1]
        + grad_logits[:, 1:2] * coef_full[1:2]
    )
    grad_hidden_norm, grad_gain_two, grad_bias_two = norm_backward(
        grad_normed_two, unit_two, inverse_two, gain_two
    )
    grad_hidden = grad_out + grad_hidden_norm
    grad_att_low = grad_hidden.astype(jnp.bfloat16)
    grad_w_out = dot(attended, grad_att_low, ((0,), (0,))).astype(jnp.bfloat16)
    grad_attended = dot(after(grad_att_low, grad_w_out), full_out, ((1,), (1,))).astype(jnp.bfloat16)

    grad_mine = swap_groups(grad_attended.reshape(rows, n_es, group).transpose(1, 0, 2), "es").reshape(
        n_es * rows, group
    )
    grad_downs = outer_fold(acts, after(expert_grad, grad_attended), grad_attended)
    last_downs = exchange(after(grad_downs[1], grad_mine), order_e[0])
    by_es = grad_w_out.reshape(n_ep, n_es, stripe, width).transpose(1, 0, 2, 3)
    out_part = scatter_sum(by_es.reshape(n_es * n_ep * stripe, width), order_e[::-1]).astype(jnp.bfloat16)
    dense_sum = lax.psum_scatter(
        jnp.concatenate([g.reshape(n_ep, -1, width) for g in (out_part, grad_w_in, grad_w_back)], axis=1),
        "ep",
        scatter_dimension=0,
        tiled=True,
    )[0]
    grad_qkv = attend_back(qkv, after(grad_mine, out_part, grad_downs[1]), attended_full, logs)
    grad_ups, grad_downs = (
        pieces[0].astype(jnp.float32) + last.astype(jnp.float32)
        for pieces, last in ((grad_ups, last_ups), (grad_downs, last_downs))
    )
    grad_qkv = after(grad_qkv, last_downs)
    grad_w_heads = dot(normed_all, grad_qkv, ((0,), (0,)))
    column_sums = jnp.sum(grad_qkv.astype(jnp.float32), axis=0, keepdims=True)
    grad_w_heads_low = grad_w_heads.astype(jnp.bfloat16)
    heads_wide = w_heads.astype(jnp.float32)
    grad_bias_one = jnp.sum(heads_wide * column_sums, axis=1)
    grad_gain_one = (jnp.sum(heads_wide * grad_w_heads, axis=1) - bias_one[0] * grad_bias_one) / gain_one[0]
    back_e = order_e[::-1]
    taps = []
    grad_rows = scatter_sum(
        dot(after(grad_qkv, grad_w_heads_low), w_heads, ((1,), (1,))).astype(jnp.bfloat16),
        back_e,
        taps=taps,
    )
    _, unit_one, inverse_one = norm_forward(inputs, gain_one, bias_one)
    grad_inputs_norm, _, _ = norm_backward(grad_rows, unit_one, inverse_one, gain_one)
    grad_tokens = grad_hidden + grad_inputs_norm

    back_z = order_z[::-1]
    small_grads = jnp.stack(
        [grad_gain_one, grad_bias_one, grad_gain_two, grad_bias_two, grad_coef[0], grad_coef[1]]
    )
    small_grads = small_grads.astype(jnp.bfloat16).reshape(6, n_ep, n_es * stripe).transpose(1, 0, 2)
    extra = 16
    small_grads = jnp.pad(small_grads, ((0, 0), (0, extra - 6), (0, 3 * group - n_es * stripe)))
    joined = jnp.concatenate([grad_w_heads_low.reshape(n_ep, n_es * stripe, 3 * group), small_grads], axis=1)
    joined = scatter_sum(joined.reshape(-1, 3 * group), back_z, hold=taps[:1])
    joined = joined.astype(jnp.bfloat16)
    small_sum = joined[n_es * stripe :][:6, : n_es * stripe].reshape(6, n_es, stripe).transpose(1, 0, 2)
    small_sum = jnp.pad(small_sum, ((0, 0), (0, stripe - 6), (0, tile - stripe)))
    cuts = (stripe, stripe + n_es * stripe)
    last = swap_groups(
        jnp.concatenate(
            [
                joined[: n_es * stripe].reshape(n_es, stripe, 3 * group),
                small_sum,
                dense_sum[cuts[0] : cuts[1]].reshape(n_es, stripe, units),
            ],
            axis=2,
        ),
        "es",
    ).astype(jnp.float32)
    cut = 3 * group
    grad_w_qkv = last[:, :, :cut].reshape(n_es, stripe, 3, group).transpose(1, 2, 0, 3).reshape(stripe, 3 * width)
    small_sum = jnp.sum(last[:, :6, cut : cut + stripe], axis=0)
    grad_fc_in = (
        last[:, :, cut + tile :]
        .reshape(n_es, stripe, n_ep, block)
        .transpose(1, 2, 0, 3)
        .reshape(stripe, n_ep * n_es * block)
    )
    return (
        out_tokens,
        grad_tokens,
        grad_w_qkv,
        dense_sum[: cuts[0]].astype(jnp.float32),
        grad_fc_in,
        dense_sum[cuts[1] :].astype(jnp.float32),
        small_sum[0],
        small_sum[1],
        small_sum[2],
        small_sum[3],
        small_sum[4:6].T,
        grad_ups[None],
        grad_downs[None],
    )


def solution(mesh):
    both = P(BOTH)
    table = P(BOTH, None)
    stack = P("ep", "es", None)
    return jax.shard_map(
        on_device,
        mesh=mesh,
        in_specs=(table,) * 6 + (both,) * 4 + (table, stack, stack, table, both),
        out_specs=(table,) * 6 + (both,) * 4 + (table, stack, stack),
        check_vma=False,
    )
```

```python
import functools

import jax
import jax.numpy as jnp
import numpy as np
from jax import lax
from jax.experimental import pallas as pl
from jax.experimental.pallas import tpu as pltpu
from jax.sharding import PartitionSpec as P

HEADS = 16
HEAD_DIM = 64
EPSILON = 1e-05
MASKED = -1e30
HIGHEST = lax.Precision.HIGHEST
BOTH = ("ep", "es")
MIB = 1 << 20


def norm_forward(values, gain, offset):
    average = jnp.mean(values, axis=-1, keepdims=True)
    centred = values - average
    variance = jnp.mean(centred * centred, axis=-1, keepdims=True)
    inverse = lax.rsqrt(variance + EPSILON)
    unit = centred * inverse
    return unit * gain + offset, unit, inverse


def norm_backward(grad, unit, inverse, gain):
    scaled = grad * gain
    mean_scaled = jnp.mean(scaled, axis=-1, keepdims=True)
    mean_unit = jnp.mean(scaled * unit, axis=-1, keepdims=True)
    grad_in = (scaled - mean_scaled - unit * mean_unit) * inverse
    return grad_in, jnp.sum(grad * unit, axis=0), jnp.sum(grad, axis=0)


def gelu_and_slope(values):
    cdf = 0.5 * (1.0 + lax.erf(values * (2.0**-0.5)))
    density = jnp.exp(-0.5 * values * values) * ((2.0 * np.pi) ** -0.5)
    return values * cdf, cdf + values * density


def dot(left, right, contract=((1,), (0,)), out=jnp.float32):
    return lax.dot_general(left, right, (contract, ((), ())), preferred_element_type=out)


def softmax_pair(logits):
    largest = jnp.max(logits, axis=-1, keepdims=True)
    expanded = jnp.exp(logits - largest)
    return expanded / jnp.sum(expanded, axis=-1, keepdims=True)


def digits(axis):
    size = lax.axis_size(axis)
    return [(axis, 1 << b) for b in range(size.bit_length() - 1)]


def exchange(x, digit):
    axis, stride = digit
    size = lax.axis_size(axis)
    return lax.ppermute(x, axis, [(i, i ^ stride) for i in range(size)])


def after(x, *others):
    return lax.optimization_barrier((x, *others))[0]


def weights_of(order):
    inner = 1 << sum(axis == "es" for axis, _ in order)
    return {(axis, stride): stride * (inner if axis == "ep" else 1) for axis, stride in order}


def relative_numbers(order):
    numbers, weights = [0], weights_of(order)
    for digit in order:
        numbers = numbers + [n + weights[digit] for n in numbers]
    return numbers


def gather_pieces(shard, order, hold=None):
    pieces = [shard]
    for number, digit in enumerate(order):
        if number == len(order) - 1 and hold is not None:
            pieces = [after(piece, hold) for piece in pieces]
        pieces = pieces + [exchange(piece, digit) for piece in pieces]
    return pieces


def gather_relative(shard, order, hold=None):
    held = shard[None]
    for number, digit in enumerate(order[:-1]):
        held = jnp.concatenate([held, exchange(held, digit)], axis=0)
        if number == len(order) - 2 and hold is not None:
            held = after(held, hold)
    return held, exchange(held, order[-1])


def place_kernel(plan, outputs, me_ref, *refs):
    sems_in, sems_out = refs[-2:]
    inputs = len(refs) - 2 - outputs - len({step[2] for step in plan})
    outs, held = refs[inputs : inputs + outputs], refs[inputs + outputs : -2]
    me = me_ref[0]
    arriving, leaving = [], []
    for which, row, chain, slot, relative, rows, segments in plan:
        here = held[chain].at[pl.ds(slot * rows, rows), :]
        copy = pltpu.make_async_copy(refs[which].at[row], here, sems_in.at[len(arriving)])
        copy.start()
        arriving.append(copy)
        start = pl.multiple_of((me ^ relative) * rows, rows)
        group = []
        for place, out, first, width in segments:
            group.append(
                pltpu.make_async_copy(
                    held[chain].at[pl.ds(slot * rows, rows), pl.ds(place, width)],
                    outs[out].at[pl.ds(start, rows), pl.ds(first, width)],
                    sems_out.at[sum(map(len, leaving)) + len(group)],
                )
            )
        leaving.append(group)
    for copy, group in zip(arriving, leaving):
        copy.wait()
        for out in group:
            out.start()
    for group in leaving:
        for out in group:
            out.wait()


def gather_rows(shards, chains, me, hold=None):
    rows = shards[0].shape[0]
    count = 1 << len(chains[0][0])
    if rows % 16 or any(w % 128 or f % 128 for _, ranges in chains for _, f, w in ranges):
        axes = tuple(a for a in BOTH if any(d[0] == a for d in chains[0][0]))
        return [lax.all_gather(shard, axes, axis=0, tiled=True) for shard in shards]
    parts, plan, widths = [], [], []
    for chain, (order, ranges) in enumerate(chains):
        numbers = relative_numbers(order)
        segments, place = [], 0
        for index, first, width in ranges:
            segments.append((place, index, first, width))
            place += width
        widths.append(place)
        cut = [shards[index][:, first : first + width] for index, first, width in ranges]
        joined = cut[0] if len(cut) == 1 else jnp.concatenate(cut, axis=1)
        for half, part in enumerate(gather_relative(joined, order, None if chain else hold)):
            for row in range(count // 2):
                slot = half * (count // 2) + row
                plan.append((len(parts), row, chain, slot, numbers[slot], rows, tuple(segments)))
            parts.append(part)
    return pl.pallas_call(
        functools.partial(place_kernel, tuple(plan), len(shards)),
        out_shape=[jax.ShapeDtypeStruct((count * rows, s.shape[1]), s.dtype) for s in shards],
        in_specs=[pl.BlockSpec(memory_space=pltpu.SMEM)] + [pl.BlockSpec(memory_space=pl.ANY)] * len(parts),
        out_specs=[pl.BlockSpec(memory_space=pl.ANY)] * len(shards),
        scratch_shapes=[pltpu.VMEM((count * rows, w), shards[0].dtype) for w in widths]
        + [
            pltpu.SemaphoreType.DMA((len(plan),)),
            pltpu.SemaphoreType.DMA((sum(len(step[-1]) for step in plan),)),
        ],
        compiler_params=pltpu.CompilerParams(vmem_limit_bytes=16 * MIB),
        name="place_rows",
    )(me, *parts)


def fold_pieces(pieces, digit):
    half = len(pieces) // 2
    return [
        kept.astype(jnp.float32) + exchange(sent.astype(jnp.bfloat16), digit).astype(jnp.float32)
        for kept, sent in zip(pieces[:half], pieces[half:])
    ]


def fold_all_but_last(pieces, order):
    for digit in order[:0:-1]:
        pieces = [piece.astype(jnp.bfloat16) for piece in fold_pieces(pieces, digit)]
    return pieces


def sum_pieces(pieces, order):
    for digit in order[::-1]:
        pieces = fold_pieces(pieces, digit)
    return pieces[0]


def scatter_sum(partial, order, hold=None, taps=None):
    count = 1 << len(order)
    rows = partial.shape[0] // count
    remaining = sorted(order, key=weights_of(order).get, reverse=True)
    held = partial.reshape((2,) * len(order) + (rows,) + partial.shape[1:])
    for number, digit in enumerate(order):
        axis, stride = digit
        place = remaining.index(digit)
        remaining.remove(digit)
        bit = (lax.axis_index(axis) // stride) % 2
        mine = lax.dynamic_index_in_dim(held, bit, place, keepdims=False)
        theirs = lax.dynamic_index_in_dim(held, 1 - bit, place, keepdims=False)
        held = mine.astype(jnp.float32) + exchange(theirs, digit).astype(jnp.float32)
        if number < len(order) - 1:
            held = held.astype(jnp.bfloat16)
        if taps is not None:
            taps.append(held)
        if number == 0 and hold is not None:
            held = after(held, *hold)
    return held


def norm_place_kernel(per, me_ref, *refs):
    gain_ref, bias_ref, out_ref = refs[-3:]
    for number, ref in enumerate(refs[:-3]):

        @pl.when(pl.program_id(0) // per == number)
        def _():
            values = ref[...].astype(jnp.float32)
            out_ref[...] = norm_forward(values, gain_ref[...], bias_ref[...])[0].astype(jnp.bfloat16)


def place_normed(pieces, order, me, gain, bias):
    rows, width = pieces[0].shape
    step = min(256, rows)
    per = rows // step
    weights = weights_of(order)

    def target(i, me_ref):
        block = me_ref[0]
        for bit, digit in enumerate(order):
            block = block ^ ((((i // per) >> bit) & 1) * weights[digit])
        return (block * per + i % per, 0)

    def source(number):
        return lambda i, me_ref: (jnp.clip(i - number * per, 0, per - 1), 0)

    line = pl.BlockSpec((1, width), lambda i, me_ref: (0, 0))
    return pl.pallas_call(
        functools.partial(norm_place_kernel, per),
        grid_spec=pltpu.PrefetchScalarGridSpec(
            num_scalar_prefetch=1,
            grid=(len(pieces) * per,),
            in_specs=[pl.BlockSpec((step, width), source(n)) for n in range(len(pieces))] + [line, line],
            out_specs=pl.BlockSpec((step, width), target),
        ),
        out_shape=jax.ShapeDtypeStruct((len(pieces) * rows, width), jnp.bfloat16),
        compiler_params=pltpu.CompilerParams(vmem_limit_bytes=24 * MIB),
        name="norm_place",
    )(me, *pieces, gain, bias)


def head_mask(rows, width, head):
    lane = lax.broadcasted_iota(jnp.int32, (rows, width), 1)
    return (lane // HEAD_DIM) == head


def causal_tile(keys, queries):
    key = lax.broadcasted_iota(jnp.int32, (keys, queries), 0)
    query = lax.broadcasted_iota(jnp.int32, (keys, queries), 1)
    return key <= query


def flip(dst, src):
    block = min(256, src.shape[0])
    for start in range(0, src.shape[0], block):
        dst[:, start : start + block] = src[start : start + block, :].T


def over_keys(step, query_block, key_block):
    i = pl.program_id(0)
    per = query_block // key_block

    @pl.loop(0, i * per)
    def _(j):
        step(j, 0, False)

    for r in range(per):
        step(i * per + r, r * key_block, True)


def attend_kernel(heads, bq, bk, q_ref, k_ref, v_ref, low_ref, full_ref, log_ref, vt, qh, acc, top, total):
    width = heads * HEAD_DIM

    @pl.when(pl.program_id(0) == 0)
    def _():
        flip(vt, v_ref)

    scaled = q_ref[...] * jnp.asarray(HEAD_DIM**-0.5, jnp.bfloat16)
    for h in range(heads):
        qh[h] = jnp.where(head_mask(bq, width, h), scaled, jnp.zeros_like(scaled))
    acc[...] = jnp.zeros_like(acc)
    total[...] = jnp.zeros_like(total)
    top[...] = jnp.full_like(top, MASKED)
    one = pl.ds(0, 1)

    def step(j, lo, diagonal):
        at = pl.ds(j * bk, bk)
        keys = k_ref[at, :]
        for h in range(heads):
            s = dot(keys, qh[h, lo:, :], ((1,), (1,)))
            if diagonal:
                s = jnp.where(causal_tile(bk, bq - lo), s, MASKED)
            old = top[h, one, lo:]
            new = jnp.maximum(old, jnp.max(s, axis=0, keepdims=True))
            p = jnp.exp(s - new)
            shrink = jnp.exp(old - new)
            top[h, one, lo:] = new
            total[h, one, lo:] = total[h, one, lo:] * shrink + jnp.sum(p, axis=0, keepdims=True)
            low = slice(h * HEAD_DIM, (h + 1) * HEAD_DIM)
            acc[low, lo:] = acc[low, lo:] * shrink + dot(vt[low, at], p.astype(jnp.bfloat16))

    over_keys(step, bq, bk)
    for h in range(heads):
        log_ref[pl.ds(h, 1), :] = top[h, one, :] + jnp.log(total[h, one, :])
        low = slice(h * HEAD_DIM, (h + 1) * HEAD_DIM)
        acc[low, :] = acc[low, :] / total[h, one, :]
    out = acc[...].T
    full_ref[...] = out
    low_ref[...] = out.astype(jnp.bfloat16)


def column(rows, width, place):
    return pl.BlockSpec((rows, width), lambda i: (0, place))


def attend(qkv):
    rows = qkv.shape[0]
    width = qkv.shape[1] // 3
    heads = width // HEAD_DIM
    bq = bk = min(512, rows)
    strip = pl.BlockSpec((bq, width), lambda i: (i, 0))
    return pl.pallas_call(
        functools.partial(attend_kernel, heads, bq, bk),
        grid=(rows // bq,),
        in_specs=[strip, column(rows, width, 1), column(rows, width, 2)],
        out_specs=[strip, strip, pl.BlockSpec((heads, bq), lambda i: (0, i))],
        out_shape=[
            jax.ShapeDtypeStruct((rows, width), jnp.bfloat16),
            jax.ShapeDtypeStruct((rows, width), jnp.float32),
            jax.ShapeDtypeStruct((heads, rows), jnp.float32),
        ],
        scratch_shapes=[
            pltpu.VMEM((width, rows), jnp.bfloat16),
            pltpu.VMEM((heads, bq, width), jnp.bfloat16),
            pltpu.VMEM((width, bq), jnp.float32),
            pltpu.VMEM((heads, 8, bq), jnp.float32),
            pltpu.VMEM((heads, 8, bq), jnp.float32),
        ],
        compiler_params=pltpu.CompilerParams(vmem_limit_bytes=40 * MIB),
        cost_estimate=pl.CostEstimate(flops=MIB, bytes_accessed=MIB, transcendentals=0),
        name="attend",
    )(qkv, qkv, qkv)


def attend_back_kernel(
    heads, bq, bk, q_ref, k_ref, v_ref, g_ref, o_ref, log_ref, out_ref,
    kt, qh, gh, delta, acc, acc_k, acc_v,
):
    i = pl.program_id(0)
    width = heads * HEAD_DIM
    scale = HEAD_DIM**-0.5
    nt = ((1,), (1,))

    @pl.when(i == 0)
    def _():
        flip(kt, k_ref)
        acc_k[...] = jnp.zeros_like(acc_k)
        acc_v[...] = jnp.zeros_like(acc_v)

    scaled = q_ref[...] * jnp.asarray(scale, jnp.bfloat16)
    grads = g_ref[...]
    for h in range(heads):
        mask = head_mask(bq, width, h)
        qh[h] = jnp.where(mask, scaled, jnp.zeros_like(scaled))
        gh[h] = jnp.where(mask, grads, jnp.zeros_like(grads))
    per_head = (
        lax.broadcasted_iota(jnp.int32, (8, width), 1) // HEAD_DIM
        == lax.broadcasted_iota(jnp.int32, (8, width), 0)
    ).astype(jnp.float32)
    delta[...] = lax.dot_general(
        per_head, grads.astype(jnp.float32) * o_ref[...], (nt, ((), ())), precision=HIGHEST,
        preferred_element_type=jnp.float32,
    )
    acc[...] = jnp.zeros_like(acc)

    def step(j, lo, diagonal):
        at = pl.ds(j * bk, bk)
        keys, values = k_ref[at, :], v_ref[at, :]
        sum_k = sum_v = 0.0
        for h in range(heads):
            queries, outer_grads = qh[h, lo:, :], gh[h, lo:, :]
            s = dot(keys, queries, nt)
            p = jnp.exp(s - log_ref[pl.ds(h, 1), lo:])
            if diagonal:
                p = jnp.where(causal_tile(bk, bq - lo), p, 0.0)
            dp = dot(values, outer_grads, nt)
            raw = (p * (dp - delta[pl.ds(h, 1), lo:])).astype(jnp.bfloat16)
            low = slice(h * HEAD_DIM, (h + 1) * HEAD_DIM)
            acc[low, lo:] = acc[low, lo:] + dot(kt[low, at], raw)
            sum_v = sum_v + dot(p.astype(jnp.bfloat16), outer_grads)
            sum_k = sum_k + dot(raw, queries)
        acc_v[at, :] = acc_v[at, :] + sum_v
        acc_k[at, :] = acc_k[at, :] + sum_k

    over_keys(step, bq, bk)
    out_ref[pl.ds(pl.multiple_of(i * bq, bq), bq), :width] = (acc[...].T * scale).astype(jnp.bfloat16)

    @pl.when(i == pl.num_programs(0) - 1)
    def _():
        out_ref[:, width : 2 * width] = acc_k[...].astype(jnp.bfloat16)
        out_ref[:, 2 * width :] = acc_v[...].astype(jnp.bfloat16)


def attend_back(qkv, grad, full, logs):
    rows, width = grad.shape
    heads = width // HEAD_DIM
    bq, bk = min(1024, rows), min(256, rows)
    strip = pl.BlockSpec((bq, width), lambda i: (i, 0))
    return pl.pallas_call(
        functools.partial(attend_back_kernel, heads, bq, bk),
        grid=(rows // bq,),
        in_specs=[
            strip,
            column(rows, width, 1),
            column(rows, width, 2),
            strip,
            strip,
            pl.BlockSpec((heads, bq), lambda i: (0, i)),
        ],
        out_specs=pl.BlockSpec((rows, 3 * width), lambda i: (0, 0)),
        out_shape=jax.ShapeDtypeStruct((rows, 3 * width), jnp.bfloat16),
        scratch_shapes=[
            pltpu.VMEM((width, rows), jnp.bfloat16),
            pltpu.VMEM((heads, bq, width), jnp.bfloat16),
            pltpu.VMEM((heads, bq, width), jnp.bfloat16),
            pltpu.VMEM((8, bq), jnp.float32),
            pltpu.VMEM((width, bq), jnp.float32),
            pltpu.VMEM((rows, width), jnp.float32),
            pltpu.VMEM((rows, width), jnp.float32),
        ],
        compiler_params=pltpu.CompilerParams(vmem_limit_bytes=56 * MIB),
        cost_estimate=pl.CostEstimate(
            flops=16 * rows * rows * width * heads, bytes_accessed=14 * rows * width, transcendentals=0
        ),
        name="attend_back",
    )(qkv, qkv, qkv, grad, full, logs)


def product_kernel(contract, left_ref, right_ref, out_ref):
    out_ref[...] = dot(left_ref[...], right_ref[...], contract).astype(out_ref.dtype)


LITTLE = pl.CostEstimate(flops=MIB, bytes_accessed=MIB, transcendentals=0)
ROOM = pltpu.CompilerParams(vmem_limit_bytes=40 * MIB)


def product(left, right, wide, contract=((1,), (0,)), place=0):
    rows, depth = left.shape
    tile = min(rows, 256 if depth > 2048 else 512)
    columns = wide if contract[1] == (0,) else right.shape[0]
    return pl.pallas_call(
        functools.partial(product_kernel, contract),
        grid=(rows // tile,),
        in_specs=[
            pl.BlockSpec((tile, depth), lambda i: (i, 0)),
            pl.BlockSpec((right.shape[0], wide), lambda i: (0, place)),
        ],
        out_specs=pl.BlockSpec((tile, columns), lambda i: (i, 0)),
        out_shape=jax.ShapeDtypeStruct((rows, columns), jnp.bfloat16),
        compiler_params=ROOM,
        cost_estimate=LITTLE,
        name="product",
    )(left, right)


def gelu_product_kernel(left_ref, right_ref, act_ref, slope_ref):
    act, slope = gelu_and_slope(dot(left_ref[...], right_ref[...]))
    act_ref[...] = act.astype(jnp.bfloat16)
    slope_ref[...] = slope


def gelu_product(left, right, wide):
    rows, depth = left.shape
    tile = min(rows, 256)
    strip = pl.BlockSpec((tile, wide), lambda i: (i, 0))
    return pl.pallas_call(
        gelu_product_kernel,
        grid=(rows // tile,),
        in_specs=[pl.BlockSpec((tile, depth), lambda i: (i, 0)), pl.BlockSpec((depth, wide), lambda i: (0, 0))],
        out_specs=[strip, strip],
        out_shape=[
            jax.ShapeDtypeStruct((rows, wide), jnp.bfloat16),
            jax.ShapeDtypeStruct((rows, wide), jnp.float32),
        ],
        compiler_params=ROOM,
        cost_estimate=LITTLE,
        name="gelu_product",
    )(left, right)


def slope_product_kernel(left_ref, right_ref, slope_ref, out_ref):
    out_ref[...] = (dot(left_ref[...], right_ref[...], ((1,), (1,))) * slope_ref[...]).astype(jnp.bfloat16)


def slope_product(left, right, slope, wide, place):
    rows = left.shape[0]
    tall = right.shape[0]
    tile = min(rows, 256)
    return pl.pallas_call(
        slope_product_kernel,
        grid=(rows // tile,),
        in_specs=[
            pl.BlockSpec((tile, wide), lambda i: (i, 0)),
            pl.BlockSpec((tall, wide), lambda i: (0, place)),
            pl.BlockSpec((tile, tall), lambda i: (i, 0)),
        ],
        out_specs=pl.BlockSpec((tile, tall), lambda i: (i, 0)),
        out_shape=jax.ShapeDtypeStruct((rows, tall), jnp.bfloat16),
        compiler_params=ROOM,
        cost_estimate=LITTLE,
        name="slope_product",
    )(left, right, slope)


def pieces_product_kernel(left_ref, *refs):
    *pieces, out_ref = refs
    tall = pieces[0].shape[0]
    total = 0.0
    for number, piece in enumerate(pieces):
        total = total + dot(left_ref[:, number * tall : (number + 1) * tall], piece[...])
    out_ref[...] = total.astype(jnp.bfloat16)


def pieces_product(left, pieces):
    rows, depth = left.shape
    tall, width = pieces[0].shape
    tile = min(rows, 256)
    return pl.pallas_call(
        pieces_product_kernel,
        grid=(rows // tile,),
        in_specs=[pl.BlockSpec((tile, depth), lambda i: (i, 0))]
        + [pl.BlockSpec((tall, width), lambda i: (0, 0))] * len(pieces),
        out_specs=pl.BlockSpec((tile, width), lambda i: (i, 0)),
        out_shape=jax.ShapeDtypeStruct((rows, width), jnp.bfloat16),
        compiler_params=ROOM,
        cost_estimate=LITTLE,
        name="pieces_product",
    )(left, *pieces)


def pieces_slope_kernel(left_ref, slope_ref, *refs):
    *pieces, out_ref = refs
    tall = pieces[0].shape[0]
    for number, piece in enumerate(pieces):
        place = slice(number * tall, (number + 1) * tall)
        value = dot(left_ref[...], piece[...], ((1,), (1,))) * slope_ref[:, place]
        out_ref[:, place] = value.astype(jnp.bfloat16)


def pieces_slope_product(left, pieces, slope):
    rows, width = left.shape
    tall = pieces[0].shape[0]
    depth = tall * len(pieces)
    tile = min(rows, 256)
    strip = pl.BlockSpec((tile, depth), lambda i: (i, 0))
    return pl.pallas_call(
        pieces_slope_kernel,
        grid=(rows // tile,),
        in_specs=[pl.BlockSpec((tile, width), lambda i: (i, 0)), strip]
        + [pl.BlockSpec((tall, width), lambda i: (0, 0))] * len(pieces),
        out_specs=strip,
        out_shape=jax.ShapeDtypeStruct((rows, depth), jnp.bfloat16),
        compiler_params=pltpu.CompilerParams(vmem_limit_bytes=48 * MIB),
        cost_estimate=LITTLE,
        name="pieces_slope_product",
    )(left, slope, *pieces)


def outer_kernel(half, left_ref, right_ref, later_ref, first_ref):
    value = dot(left_ref[...], right_ref[...], ((0,), (0,))).astype(later_ref.dtype)

    @pl.when(pl.program_id(0) < half)
    def _():
        later_ref[...] = value

    @pl.when(pl.program_id(0) >= half)
    def _():
        first_ref[...] = value


def outer_halves(left, right):
    rows, tall = left.shape
    width = right.shape[1]
    tile = min(512, tall // 2)
    half = tall // 2 // tile
    shape = jax.ShapeDtypeStruct((tall // 2, width), jnp.bfloat16)
    return pl.pallas_call(
        functools.partial(outer_kernel, half),
        grid=(2 * half,),
        in_specs=[
            pl.BlockSpec((rows, tile), lambda i: (0, jnp.where(i < half, i + half, i - half))),
            pl.BlockSpec((rows, width), lambda i: (0, 0)),
        ],
        out_specs=[
            pl.BlockSpec((tile, width), lambda i: (jnp.minimum(i, half - 1), 0)),
            pl.BlockSpec((tile, width), lambda i: (jnp.maximum(i - half, 0), 0)),
        ],
        out_shape=[shape, shape],
        compiler_params=ROOM,
        cost_estimate=LITTLE,
        name="outer_halves",
    )(left, right)


def outer(left, right):
    rows, tall = left.shape
    width = right.shape[1]
    tile = min(512, tall)
    return pl.pallas_call(
        functools.partial(product_kernel, ((0,), (0,))),
        grid=(tall // tile,),
        in_specs=[
            pl.BlockSpec((rows, tile), lambda i: (0, i)),
            pl.BlockSpec((rows, width), lambda i: (0, 0)),
        ],
        out_specs=pl.BlockSpec((tile, width), lambda i: (i, 0)),
        out_shape=jax.ShapeDtypeStruct((tall, width), jnp.bfloat16),
        compiler_params=ROOM,
        cost_estimate=LITTLE,
        name="outer",
    )(left, right)


def swap_groups(x, axis):
    return lax.all_to_all(x, axis, split_axis=0, concat_axis=0, tiled=True)


def on_device(
    tokens,
    cotangent,
    w_qkv,
    w_out,
    w_fc_in,
    w_fc_out,
    norm1_gain,
    norm1_bias,
    norm2_gain,
    norm2_bias,
    coef_weight,
    expert_up,
    expert_down,
    routes,
    keep_mask,
):
    rows, width = tokens.shape
    n_es = lax.axis_size("es")
    n_ep = lax.axis_size("ep")
    me_es = lax.axis_index("es").astype(jnp.int32).reshape(1)
    me_ep = lax.axis_index("ep").astype(jnp.int32).reshape(1)
    ep_up, es_up = digits("ep"), digits("es")
    order_e = es_up[::-1]
    order_z = ep_up[::-1]
    order_y = ep_up[:1] + ep_up[:0:-1]
    group = width // n_es
    stripe = w_qkv.shape[0]
    block = w_fc_out.shape[0]
    units = n_ep * block
    tile = 128

    packed = jnp.concatenate(
        [jnp.stack([norm1_gain, norm1_bias, norm2_gain, norm2_bias]), coef_weight.T], axis=0
    )
    packed = jnp.pad(packed, ((0, stripe - packed.shape[0]), (0, tile - stripe)))
    shared = swap_groups(
        jnp.concatenate(
            [
                w_qkv.reshape(stripe, 3, n_es, group).transpose(2, 0, 1, 3).reshape(n_es, stripe, 3 * group),
                jnp.broadcast_to(packed, (n_es, stripe, tile)),
            ],
            axis=2,
        ),
        "es",
    ).reshape(n_es * stripe, 3 * group + tile)
    own_heads, own_small = shared[:, : 3 * group], shared[:, 3 * group :]
    token_pieces = gather_pieces(after(tokens, shared), order_e)
    by_units = w_fc_in.reshape(stripe, n_ep, n_es, block).transpose(2, 0, 1, 3).reshape(n_es, stripe, units)
    more = swap_groups(
        after(jnp.concatenate([by_units, jnp.broadcast_to(w_out, (n_es, *w_out.shape))], axis=2), shared), "es"
    ).reshape(n_es * stripe, units + width)
    cut = 2 * group
    w_heads, small = gather_rows(
        [own_heads, own_small],
        [(order_z, ((0, 0, cut),)), (order_y, ((0, cut, 3 * group - cut), (1, 0, tile)))],
        me_ep,
        token_pieces[1],
    )
    small = small.reshape(n_ep * n_es, stripe, tile)[:, :6, :stripe].transpose(1, 0, 2).reshape(6, width)
    small = small.astype(jnp.float32)
    gain_one, bias_one, gain_two, bias_two = (small[i : i + 1] for i in range(4))
    coef_full = small[4:6]
    normed_all = place_normed(token_pieces, order_e, me_es, gain_one, bias_one)
    dense_weights = lax.all_gather(
        after(jnp.concatenate([more, w_fc_out], axis=1), w_heads), "ep", axis=0, tiled=True
    )
    full_out = dense_weights[:, units : units + width]
    ups = gather_pieces(after(expert_up[0], token_pieces[1]), order_e)

    inputs = tokens.astype(jnp.float32)
    qkv = after(dot(normed_all, w_heads).astype(jnp.bfloat16), ups[2])
    attended_mine, attended_full, logs = attend(qkv)
    attended_mine = after(attended_mine, ups[1])
    attended = (
        swap_groups(attended_mine.reshape(n_es, rows, group), "es").transpose(1, 0, 2).reshape(rows, width)
    )
    hidden = inputs + dot(attended, full_out)
    normed_two, unit_two, inverse_two = norm_forward(hidden, gain_two, bias_two)
    normed_two_low = normed_two.astype(jnp.bfloat16)
    coefficients = softmax_pair(
        lax.dot_general(normed_two, coef_full, (((1,), (1,)), ((), ())), precision=HIGHEST)
    )
    keep = keep_mask.astype(jnp.float32)[:, None]
    grad_out = cotangent.astype(jnp.float32)
    grad_dense_low = (coefficients[:, 0:1] * grad_out).astype(jnp.bfloat16)
    grad_expert_low = (coefficients[:, 1:2] * keep * grad_out).astype(jnp.bfloat16)

    capacity = 2 * rows // n_ep
    expert_ids = routes[:, 0]
    chosen = (expert_ids[:, None] == lax.broadcasted_iota(jnp.int32, (1, n_ep), 1)).astype(jnp.float32)
    before = (
        lax.broadcasted_iota(jnp.int32, (rows, rows), 1) < lax.broadcasted_iota(jnp.int32, (rows, rows), 0)
    ).astype(jnp.float32)
    ranks = jnp.sum(dot(before, chosen) * chosen, axis=1).astype(jnp.int32)
    slots = expert_ids * capacity + ranks
    in_slot = (slots[None, :] == lax.broadcasted_iota(jnp.int32, (n_ep * capacity, 1), 0)).astype(
        jnp.bfloat16
    )

    def to_experts(values):
        return swap_groups(values.reshape(n_ep, capacity, width), "ep").reshape(n_ep * capacity, width)

    outgoing = dot(in_slot, normed_two_low).astype(jnp.bfloat16)
    downs = gather_pieces(after(expert_down[0], attended), order_e, outgoing)
    full_up = jnp.concatenate(ups, axis=0)
    expert_in = to_experts(outgoing)
    expert_grad = to_experts(
        after(dot(in_slot, grad_expert_low).astype(jnp.bfloat16), expert_in, full_up, downs[1])
    )

    def split_pieces(values):
        return [values[i * rows : (i + 1) * rows] for i in range(n_es)]

    acts, expert_slope = gelu_and_slope(dot(expert_in, full_up, ((1,), (1,))))
    acts = acts.astype(jnp.bfloat16)
    expert_out = pieces_product(acts, downs)
    dense_in = jnp.concatenate(gather_pieces(normed_two_low, order_e, acts), axis=0)
    dense_grad = jnp.concatenate(gather_pieces(grad_dense_low, order_e, acts), axis=0)
    expert_grad = after(expert_grad, expert_out, dense_in, dense_grad)
    grad_inners = pieces_slope_product(expert_grad, downs, expert_slope)
    grad_expert_in = product(grad_inners, full_up, width)
    out_home = to_experts(after(expert_out, expert_grad))

    activated_low, slope = gelu_product(after(dense_in, grad_expert_in), dense_weights, units)
    dense_part = product(activated_low, dense_weights, width, place=2)
    grad_home = to_experts(after(grad_expert_in, out_home, dense_part))
    dense_folded = fold_all_but_last(split_pieces(dense_part), order_e)
    dense = sum_pieces(dense_folded, order_e[:1])
    grad_inner_low = slope_product(after(dense_grad, dense_part), dense_weights, slope, width, 2)
    grad_normed_part = product(grad_inner_low, dense_weights, units, ((1,), (1,)))
    grad_normed_folded = fold_all_but_last(split_pieces(grad_normed_part), order_e)
    grad_normed_dense = sum_pieces(grad_normed_folded, order_e[:1])

    def outer_fold(later, kept):
        half = later.shape[0]
        size = half // (n_es // 2)
        pieces = [
            (
                kept[i : i + size].astype(jnp.float32)
                + exchange(later[i : i + size], order_e[-1]).astype(jnp.float32)
            ).astype(jnp.bfloat16)
            for i in range(0, half, size)
        ]
        return fold_all_but_last(pieces, order_e[:-1])

    later_ups, kept_ups = outer_halves(grad_inners, after(expert_in, grad_normed_part, dense_folded[1]))
    later_downs, kept_downs = outer_halves(acts, after(expert_grad, later_ups))
    grad_w_back = outer(activated_low, after(dense_grad, later_downs, grad_normed_folded[1]))
    grad_w_in = outer(after(dense_in, later_downs), grad_inner_low)
    grad_home = after(grad_home, later_downs, grad_w_back, grad_w_in, dense, grad_normed_dense)
    out_home = after(out_home, grad_home)
    grad_ups = outer_fold(later_ups, after(kept_ups, grad_home))
    grad_downs = outer_fold(later_downs, after(kept_downs, grad_home))
    dense_sum = lax.psum_scatter(
        after(
            jnp.concatenate([g.reshape(n_ep, -1, width) for g in (grad_w_in, grad_w_back)], axis=1), grad_home
        ),
        "ep",
        scatter_dimension=0,
        tiled=True,
    )[0]
    expert_tokens = dot(in_slot, out_home, ((0,), (0,))) * keep
    grad_expert_home = dot(in_slot, grad_home, ((0,), (0,)))

    mixed = hidden + coefficients[:, 0:1] * dense + coefficients[:, 1:2] * expert_tokens
    out_tokens = mixed.astype(jnp.bfloat16)
    grad_pair = jnp.concatenate(
        [
            jnp.sum(grad_out * dense, axis=1, keepdims=True),
            jnp.sum(grad_out * expert_tokens, axis=1, keepdims=True),
        ],
        axis=1,
    )
    grad_logits = coefficients * (
        grad_pair - jnp.sum(coefficients * grad_pair, axis=1, keepdims=True)
    )
    grad_coef = lax.dot_general(grad_logits, normed_two, (((0,), (0,)), ((), ())), precision=HIGHEST)
    grad_normed_two = (
        grad_normed_dense
        + grad_expert_home
        + grad_logits[:, 0:1] * coef_full[0:1]
        + grad_logits[:, 1:2] * coef_full[1:2]
    )
    grad_hidden_norm, grad_gain_two, grad_bias_two = norm_backward(
        grad_normed_two, unit_two, inverse_two, gain_two
    )
    grad_hidden = grad_out + grad_hidden_norm
    grad_att_low = grad_hidden.astype(jnp.bfloat16)
    grad_attended = dot(grad_att_low, full_out, ((1,), (1,))).astype(jnp.bfloat16)

    grad_mine = swap_groups(grad_attended.reshape(rows, n_es, group).transpose(1, 0, 2), "es").reshape(
        n_es * rows, group
    )
    grad_w_out = dot(attended, after(grad_att_low, grad_attended), ((0,), (0,))).astype(jnp.bfloat16)
    by_es = grad_w_out.reshape(n_ep, n_es, stripe, width).transpose(1, 0, 2, 3)
    taps = []
    out_part = scatter_sum(by_es.reshape(n_es * n_ep * stripe, width), order_e[::-1], taps=taps).astype(jnp.bfloat16)
    grad_mine = after(grad_mine, grad_downs[1], taps[0])
    last_downs = exchange(after(grad_downs[1], grad_mine), order_e[0])
    grad_qkv = attend_back(qkv, after(grad_mine, grad_downs[1]), attended_full, logs)
    last_ups = exchange(after(grad_ups[1], grad_qkv), order_e[0])
    grad_ups, grad_downs = (
        pieces[0].astype(jnp.float32) + last.astype(jnp.float32)
        for pieces, last in ((grad_ups, last_ups), (grad_downs, last_downs))
    )
    grad_qkv = after(grad_qkv, last_downs)
    taps = []
    back_e = order_e[::-1]
    grad_rows_part = dot(grad_qkv, w_heads, ((1,), (1,))).astype(jnp.bfloat16)
    grad_rows = scatter_sum(grad_rows_part, back_e, taps=taps)
    grad_w_heads = dot(normed_all, after(grad_qkv, grad_rows_part), ((0,), (0,)))
    column_sums = jnp.sum(grad_qkv.astype(jnp.float32), axis=0, keepdims=True)
    grad_w_heads_low = grad_w_heads.astype(jnp.bfloat16)
    heads_wide = w_heads.astype(jnp.float32)
    grad_bias_one = jnp.sum(heads_wide * column_sums, axis=1)
    grad_gain_one = (jnp.sum(heads_wide * grad_w_heads, axis=1) - bias_one[0] * grad_bias_one) / gain_one[0]
    _, unit_one, inverse_one = norm_forward(inputs, gain_one, bias_one)
    grad_inputs_norm, _, _ = norm_backward(grad_rows, unit_one, inverse_one, gain_one)
    grad_tokens = grad_hidden + grad_inputs_norm

    back_z = order_z[::-1]
    back_y = [order_z[1], order_z[-1], *order_z[2:-1], order_z[0]] if len(order_z) > 2 else back_z
    small_grads = jnp.stack(
        [grad_gain_one, grad_bias_one, grad_gain_two, grad_bias_two, grad_coef[0], grad_coef[1]]
    )
    small_grads = small_grads.astype(jnp.bfloat16).reshape(6, n_ep, n_es * stripe).transpose(1, 0, 2)
    extra = 16
    small_grads = jnp.pad(small_grads, ((0, 0), (0, extra - 6), (0, 3 * group - n_es * stripe)))
    joined = jnp.concatenate([grad_w_heads_low.reshape(n_ep, n_es * stripe, 3 * group), small_grads], axis=1)
    by_columns = out_part.reshape(n_ep, stripe, n_es, group).transpose(0, 2, 1, 3).reshape(n_ep, -1, group)
    by_columns = jnp.pad(by_columns, ((0, 0), (0, extra), (0, 0)))
    joined = jnp.concatenate([joined, by_columns], axis=2).reshape(-1, 4 * group)
    cut = 2 * group
    joined = jnp.concatenate(
        [scatter_sum(joined[:, :cut], back_z, hold=taps[:1]), scatter_sum(joined[:, cut:], back_y)], axis=1
    )
    grad_w_out = (
        joined[: n_es * stripe, 3 * group :].reshape(n_es, stripe, group).transpose(1, 0, 2).reshape(stripe, width)
    )
    joined = joined.astype(jnp.bfloat16)
    small_sum = joined[n_es * stripe :][:6, : n_es * stripe].reshape(6, n_es, stripe).transpose(1, 0, 2)
    small_sum = jnp.pad(small_sum, ((0, 0), (0, stripe - 6), (0, tile - stripe)))
    last = swap_groups(
        jnp.concatenate(
            [
                joined[: n_es * stripe, : 3 * group].reshape(n_es, stripe, 3 * group),
                small_sum,
                dense_sum[: n_es * stripe].reshape(n_es, stripe, units),
            ],
            axis=2,
        ),
        "es",
    ).astype(jnp.float32)
    cut = 3 * group
    grad_w_qkv = last[:, :, :cut].reshape(n_es, stripe, 3, group).transpose(1, 2, 0, 3).reshape(stripe, 3 * width)
    small_sum = jnp.sum(last[:, :6, cut : cut + stripe], axis=0)
    grad_fc_in = (
        last[:, :, cut + tile :]
        .reshape(n_es, stripe, n_ep, block)
        .transpose(1, 2, 0, 3)
        .reshape(stripe, n_ep * n_es * block)
    )
    return (
        out_tokens,
        grad_tokens,
        grad_w_qkv,
        grad_w_out,
        grad_fc_in,
        dense_sum[n_es * stripe :].astype(jnp.float32),
        small_sum[0],
        small_sum[1],
        small_sum[2],
        small_sum[3],
        small_sum[4:6].T,
        grad_ups[None],
        grad_downs[None],
    )


def solution(mesh):
    both = P(BOTH)
    table = P(BOTH, None)
    stack = P("ep", "es", None)
    return jax.shard_map(
        on_device,
        mesh=mesh,
        in_specs=(table,) * 6 + (both,) * 4 + (table, stack, stack, table, both),
        out_specs=(table,) * 6 + (both,) * 4 + (table, stack, stack),
        check_vma=False,
    )
```

```python
import functools

import jax
import jax.numpy as jnp
import numpy as np
from jax import lax
from jax.experimental import pallas as pl
from jax.experimental.pallas import tpu as pltpu
from jax.sharding import PartitionSpec as P

HEADS = 16
HEAD_DIM = 64
EPSILON = 1e-05
MASKED = -1e30
HIGHEST = lax.Precision.HIGHEST
BOTH = ("ep", "es")
MIB = 1 << 20


def norm_forward(values, gain, offset):
    average = jnp.mean(values, axis=-1, keepdims=True)
    centred = values - average
    variance = jnp.mean(centred * centred, axis=-1, keepdims=True)
    inverse = lax.rsqrt(variance + EPSILON)
    unit = centred * inverse
    return unit * gain + offset, unit, inverse


def norm_backward(grad, unit, inverse, gain):
    scaled = grad * gain
    mean_scaled = jnp.mean(scaled, axis=-1, keepdims=True)
    mean_unit = jnp.mean(scaled * unit, axis=-1, keepdims=True)
    grad_in = (scaled - mean_scaled - unit * mean_unit) * inverse
    return grad_in, jnp.sum(grad * unit, axis=0), jnp.sum(grad, axis=0)


def gelu_and_slope(values):
    cdf = 0.5 * (1.0 + lax.erf(values * (2.0**-0.5)))
    density = jnp.exp(-0.5 * values * values) * ((2.0 * np.pi) ** -0.5)
    return values * cdf, cdf + values * density


def dot(left, right, contract=((1,), (0,)), out=jnp.float32):
    return lax.dot_general(left, right, (contract, ((), ())), preferred_element_type=out)


def softmax_pair(logits):
    largest = jnp.max(logits, axis=-1, keepdims=True)
    expanded = jnp.exp(logits - largest)
    return expanded / jnp.sum(expanded, axis=-1, keepdims=True)


def digits(axis):
    size = lax.axis_size(axis)
    return [(axis, 1 << b) for b in range(size.bit_length() - 1)]


def exchange(x, digit):
    axis, stride = digit
    size = lax.axis_size(axis)
    return lax.ppermute(x, axis, [(i, i ^ stride) for i in range(size)])


def after(x, *others):
    return lax.optimization_barrier((x, *others))[0]


def weights_of(order):
    inner = 1 << sum(axis == "es" for axis, _ in order)
    return {(axis, stride): stride * (inner if axis == "ep" else 1) for axis, stride in order}


def relative_numbers(order):
    numbers, weights = [0], weights_of(order)
    for digit in order:
        numbers = numbers + [n + weights[digit] for n in numbers]
    return numbers


def gather_pieces(shard, order, hold=None):
    pieces = [shard]
    for number, digit in enumerate(order):
        if number == len(order) - 1 and hold is not None:
            pieces = [after(piece, hold) for piece in pieces]
        pieces = pieces + [exchange(piece, digit) for piece in pieces]
    return pieces


def gather_relative(shard, order, hold=None):
    held = shard[None]
    for number, digit in enumerate(order[:-1]):
        held = jnp.concatenate([held, exchange(held, digit)], axis=0)
        if number == len(order) - 2 and hold is not None:
            held = after(held, hold)
    return held, exchange(held, order[-1])


def place_kernel(plan, outputs, me_ref, *refs):
    sems_in, sems_out = refs[-2:]
    inputs = len(refs) - 2 - outputs - len({step[2] for step in plan})
    outs, held = refs[inputs : inputs + outputs], refs[inputs + outputs : -2]
    me = me_ref[0]
    arriving, leaving = [], []
    for which, row, chain, slot, relative, rows, segments in plan:
        here = held[chain].at[pl.ds(slot * rows, rows), :]
        copy = pltpu.make_async_copy(refs[which].at[row], here, sems_in.at[len(arriving)])
        copy.start()
        arriving.append(copy)
        start = pl.multiple_of((me ^ relative) * rows, rows)
        group = []
        for place, out, first, width in segments:
            group.append(
                pltpu.make_async_copy(
                    held[chain].at[pl.ds(slot * rows, rows), pl.ds(place, width)],
                    outs[out].at[pl.ds(start, rows), pl.ds(first, width)],
                    sems_out.at[sum(map(len, leaving)) + len(group)],
                )
            )
        leaving.append(group)
    for copy, group in zip(arriving, leaving):
        copy.wait()
        for out in group:
            out.start()
    for group in leaving:
        for out in group:
            out.wait()


def gather_rows(shards, chains, me, hold=None):
    rows = shards[0].shape[0]
    count = 1 << len(chains[0][0])
    if rows % 16 or any(w % 128 or f % 128 for _, ranges in chains for _, f, w in ranges):
        axes = tuple(a for a in BOTH if any(d[0] == a for d in chains[0][0]))
        return [lax.all_gather(shard, axes, axis=0, tiled=True) for shard in shards]
    parts, plan, widths = [], [], []
    for chain, (order, ranges) in enumerate(chains):
        numbers = relative_numbers(order)
        segments, place = [], 0
        for index, first, width in ranges:
            segments.append((place, index, first, width))
            place += width
        widths.append(place)
        cut = [shards[index][:, first : first + width] for index, first, width in ranges]
        joined = cut[0] if len(cut) == 1 else jnp.concatenate(cut, axis=1)
        for half, part in enumerate(gather_relative(joined, order, None if chain else hold)):
            for row in range(count // 2):
                slot = half * (count // 2) + row
                plan.append((len(parts), row, chain, slot, numbers[slot], rows, tuple(segments)))
            parts.append(part)
    return pl.pallas_call(
        functools.partial(place_kernel, tuple(plan), len(shards)),
        out_shape=[jax.ShapeDtypeStruct((count * rows, s.shape[1]), s.dtype) for s in shards],
        in_specs=[pl.BlockSpec(memory_space=pltpu.SMEM)] + [pl.BlockSpec(memory_space=pl.ANY)] * len(parts),
        out_specs=[pl.BlockSpec(memory_space=pl.ANY)] * len(shards),
        scratch_shapes=[pltpu.VMEM((count * rows, w), shards[0].dtype) for w in widths]
        + [
            pltpu.SemaphoreType.DMA((len(plan),)),
            pltpu.SemaphoreType.DMA((sum(len(step[-1]) for step in plan),)),
        ],
        compiler_params=pltpu.CompilerParams(vmem_limit_bytes=16 * MIB),
        name="place_rows",
    )(me, *parts)


def fold_pieces(pieces, digit):
    half = len(pieces) // 2
    return [
        kept.astype(jnp.float32) + exchange(sent.astype(jnp.bfloat16), digit).astype(jnp.float32)
        for kept, sent in zip(pieces[:half], pieces[half:])
    ]


def fold_all_but_last(pieces, order):
    for digit in order[:0:-1]:
        pieces = [piece.astype(jnp.bfloat16) for piece in fold_pieces(pieces, digit)]
    return pieces


def sum_pieces(pieces, order):
    for digit in order[::-1]:
        pieces = fold_pieces(pieces, digit)
    return pieces[0]


def scatter_sum(partial, order, hold=None, taps=None, beside=None):
    count = 1 << len(order)
    rows = partial.shape[0] // count
    remaining = sorted(order, key=weights_of(order).get, reverse=True)
    held = partial.reshape((2,) * len(order) + (rows,) + partial.shape[1:])
    for number, digit in enumerate(order):
        axis, stride = digit
        place = remaining.index(digit)
        remaining.remove(digit)
        bit = (lax.axis_index(axis) // stride) % 2
        mine = lax.dynamic_index_in_dim(held, bit, place, keepdims=False)
        theirs = lax.dynamic_index_in_dim(held, 1 - bit, place, keepdims=False)
        if beside is not None and number == len(order) - 1:
            mine = after(mine, beside())
        held = mine.astype(jnp.float32) + exchange(theirs, digit).astype(jnp.float32)
        if number < len(order) - 1:
            held = held.astype(jnp.bfloat16)
        if taps is not None:
            taps.append(held)
        if number == 0 and hold is not None:
            held = after(held, *hold)
    return held


def norm_place_kernel(per, me_ref, *refs):
    gain_ref, bias_ref, out_ref = refs[-3:]
    for number, ref in enumerate(refs[:-3]):

        @pl.when(pl.program_id(0) // per == number)
        def _():
            values = ref[...].astype(jnp.float32)
            out_ref[...] = norm_forward(values, gain_ref[...], bias_ref[...])[0].astype(jnp.bfloat16)


def place_normed(pieces, order, me, gain, bias):
    rows, width = pieces[0].shape
    step = min(256, rows)
    per = rows // step
    weights = weights_of(order)

    def target(i, me_ref):
        block = me_ref[0]
        for bit, digit in enumerate(order):
            block = block ^ ((((i // per) >> bit) & 1) * weights[digit])
        return (block * per + i % per, 0)

    def source(number):
        return lambda i, me_ref: (jnp.clip(i - number * per, 0, per - 1), 0)

    line = pl.BlockSpec((1, width), lambda i, me_ref: (0, 0))
    return pl.pallas_call(
        functools.partial(norm_place_kernel, per),
        grid_spec=pltpu.PrefetchScalarGridSpec(
            num_scalar_prefetch=1,
            grid=(len(pieces) * per,),
            in_specs=[pl.BlockSpec((step, width), source(n)) for n in range(len(pieces))] + [line, line],
            out_specs=pl.BlockSpec((step, width), target),
        ),
        out_shape=jax.ShapeDtypeStruct((len(pieces) * rows, width), jnp.bfloat16),
        compiler_params=pltpu.CompilerParams(vmem_limit_bytes=24 * MIB),
        name="norm_place",
    )(me, *pieces, gain, bias)


def head_mask(rows, width, head):
    lane = lax.broadcasted_iota(jnp.int32, (rows, width), 1)
    return (lane // HEAD_DIM) == head


def causal_tile(keys, queries):
    key = lax.broadcasted_iota(jnp.int32, (keys, queries), 0)
    query = lax.broadcasted_iota(jnp.int32, (keys, queries), 1)
    return key <= query


def flip(dst, src):
    block = min(256, src.shape[0])
    for start in range(0, src.shape[0], block):
        dst[:, start : start + block] = src[start : start + block, :].T


def over_keys(step, query_block, key_block):
    i = pl.program_id(0)
    per = query_block // key_block

    @pl.loop(0, i * per)
    def _(j):
        step(j, 0, False)

    for r in range(per):
        step(i * per + r, r * key_block, True)


def attend_kernel(heads, bq, bk, q_ref, k_ref, v_ref, low_ref, full_ref, log_ref, vt, qh, acc, top, total):
    width = heads * HEAD_DIM

    @pl.when(pl.program_id(0) == 0)
    def _():
        flip(vt, v_ref)

    scaled = q_ref[...] * jnp.asarray(HEAD_DIM**-0.5, jnp.bfloat16)
    for h in range(heads):
        qh[h] = jnp.where(head_mask(bq, width, h), scaled, jnp.zeros_like(scaled))
    acc[...] = jnp.zeros_like(acc)
    total[...] = jnp.zeros_like(total)
    top[...] = jnp.full_like(top, MASKED)
    one = pl.ds(0, 1)

    def step(j, lo, diagonal):
        at = pl.ds(j * bk, bk)
        keys = k_ref[at, :]
        for h in range(heads):
            s = dot(keys, qh[h, lo:, :], ((1,), (1,)))
            if diagonal:
                s = jnp.where(causal_tile(bk, bq - lo), s, MASKED)
            old = top[h, one, lo:]
            new = jnp.maximum(old, jnp.max(s, axis=0, keepdims=True))
            p = jnp.exp(s - new)
            shrink = jnp.exp(old - new)
            top[h, one, lo:] = new
            total[h, one, lo:] = total[h, one, lo:] * shrink + jnp.sum(p, axis=0, keepdims=True)
            low = slice(h * HEAD_DIM, (h + 1) * HEAD_DIM)
            acc[low, lo:] = acc[low, lo:] * shrink + dot(vt[low, at], p.astype(jnp.bfloat16))

    over_keys(step, bq, bk)
    for h in range(heads):
        log_ref[pl.ds(h, 1), :] = top[h, one, :] + jnp.log(total[h, one, :])
        low = slice(h * HEAD_DIM, (h + 1) * HEAD_DIM)
        acc[low, :] = acc[low, :] / total[h, one, :]
    out = acc[...].T
    full_ref[...] = out
    low_ref[...] = out.astype(jnp.bfloat16)


def column(rows, width, place):
    return pl.BlockSpec((rows, width), lambda i: (0, place))


def attend(qkv):
    rows = qkv.shape[0]
    width = qkv.shape[1] // 3
    heads = width // HEAD_DIM
    bq = bk = min(512, rows)
    strip = pl.BlockSpec((bq, width), lambda i: (i, 0))
    return pl.pallas_call(
        functools.partial(attend_kernel, heads, bq, bk),
        grid=(rows // bq,),
        in_specs=[strip, column(rows, width, 1), column(rows, width, 2)],
        out_specs=[strip, strip, pl.BlockSpec((heads, bq), lambda i: (0, i))],
        out_shape=[
            jax.ShapeDtypeStruct((rows, width), jnp.bfloat16),
            jax.ShapeDtypeStruct((rows, width), jnp.float32),
            jax.ShapeDtypeStruct((heads, rows), jnp.float32),
        ],
        scratch_shapes=[
            pltpu.VMEM((width, rows), jnp.bfloat16),
            pltpu.VMEM((heads, bq, width), jnp.bfloat16),
            pltpu.VMEM((width, bq), jnp.float32),
            pltpu.VMEM((heads, 8, bq), jnp.float32),
            pltpu.VMEM((heads, 8, bq), jnp.float32),
        ],
        compiler_params=pltpu.CompilerParams(vmem_limit_bytes=40 * MIB),
        cost_estimate=pl.CostEstimate(flops=MIB, bytes_accessed=MIB, transcendentals=0),
        name="attend",
    )(qkv, qkv, qkv)


def attend_back_kernel(
    heads, bq, bk, q_ref, k_ref, v_ref, g_ref, o_ref, log_ref, out_ref,
    kt, qh, gh, delta, acc, acc_k, acc_v,
):
    i = pl.program_id(0)
    width = heads * HEAD_DIM
    scale = HEAD_DIM**-0.5
    nt = ((1,), (1,))

    @pl.when(i == 0)
    def _():
        flip(kt, k_ref)
        acc_k[...] = jnp.zeros_like(acc_k)
        acc_v[...] = jnp.zeros_like(acc_v)

    scaled = q_ref[...] * jnp.asarray(scale, jnp.bfloat16)
    grads = g_ref[...]
    for h in range(heads):
        mask = head_mask(bq, width, h)
        qh[h] = jnp.where(mask, scaled, jnp.zeros_like(scaled))
        gh[h] = jnp.where(mask, grads, jnp.zeros_like(grads))
    per_head = (
        lax.broadcasted_iota(jnp.int32, (8, width), 1) // HEAD_DIM
        == lax.broadcasted_iota(jnp.int32, (8, width), 0)
    ).astype(jnp.float32)
    delta[...] = lax.dot_general(
        per_head, grads.astype(jnp.float32) * o_ref[...], (nt, ((), ())), precision=HIGHEST,
        preferred_element_type=jnp.float32,
    )
    acc[...] = jnp.zeros_like(acc)

    def step(j, lo, diagonal):
        at = pl.ds(j * bk, bk)
        keys, values = k_ref[at, :], v_ref[at, :]
        sum_k = sum_v = 0.0
        for h in range(heads):
            queries, outer_grads = qh[h, lo:, :], gh[h, lo:, :]
            s = dot(keys, queries, nt)
            p = jnp.exp(s - log_ref[pl.ds(h, 1), lo:])
            if diagonal:
                p = jnp.where(causal_tile(bk, bq - lo), p, 0.0)
            dp = dot(values, outer_grads, nt)
            raw = (p * (dp - delta[pl.ds(h, 1), lo:])).astype(jnp.bfloat16)
            low = slice(h * HEAD_DIM, (h + 1) * HEAD_DIM)
            acc[low, lo:] = acc[low, lo:] + dot(kt[low, at], raw)
            sum_v = sum_v + dot(p.astype(jnp.bfloat16), outer_grads)
            sum_k = sum_k + dot(raw, queries)
        acc_v[at, :] = acc_v[at, :] + sum_v
        acc_k[at, :] = acc_k[at, :] + sum_k

    over_keys(step, bq, bk)
    out_ref[pl.ds(pl.multiple_of(i * bq, bq), bq), :width] = (acc[...].T * scale).astype(jnp.bfloat16)

    @pl.when(i == pl.num_programs(0) - 1)
    def _():
        out_ref[:, width : 2 * width] = acc_k[...].astype(jnp.bfloat16)
        out_ref[:, 2 * width :] = acc_v[...].astype(jnp.bfloat16)


def attend_back(qkv, grad, full, logs):
    rows, width = grad.shape
    heads = width // HEAD_DIM
    bq, bk = min(1024, rows), min(256, rows)
    strip = pl.BlockSpec((bq, width), lambda i: (i, 0))
    return pl.pallas_call(
        functools.partial(attend_back_kernel, heads, bq, bk),
        grid=(rows // bq,),
        in_specs=[
            strip,
            column(rows, width, 1),
            column(rows, width, 2),
            strip,
            strip,
            pl.BlockSpec((heads, bq), lambda i: (0, i)),
        ],
        out_specs=pl.BlockSpec((rows, 3 * width), lambda i: (0, 0)),
        out_shape=jax.ShapeDtypeStruct((rows, 3 * width), jnp.bfloat16),
        scratch_shapes=[
            pltpu.VMEM((width, rows), jnp.bfloat16),
            pltpu.VMEM((heads, bq, width), jnp.bfloat16),
            pltpu.VMEM((heads, bq, width), jnp.bfloat16),
            pltpu.VMEM((8, bq), jnp.float32),
            pltpu.VMEM((width, bq), jnp.float32),
            pltpu.VMEM((rows, width), jnp.float32),
            pltpu.VMEM((rows, width), jnp.float32),
        ],
        compiler_params=pltpu.CompilerParams(vmem_limit_bytes=56 * MIB),
        cost_estimate=pl.CostEstimate(
            flops=16 * rows * rows * width * heads, bytes_accessed=14 * rows * width, transcendentals=0
        ),
        name="attend_back",
    )(qkv, qkv, qkv, grad, full, logs)


def product_kernel(contract, left_ref, right_ref, out_ref):
    out_ref[...] = dot(left_ref[...], right_ref[...], contract).astype(out_ref.dtype)


LITTLE = pl.CostEstimate(flops=MIB, bytes_accessed=MIB, transcendentals=0)
ROOM = pltpu.CompilerParams(vmem_limit_bytes=40 * MIB)


def product(left, right, wide, contract=((1,), (0,)), place=0):
    rows, depth = left.shape
    tile = min(rows, 256 if depth > 2048 else 512)
    columns = wide if contract[1] == (0,) else right.shape[0]
    return pl.pallas_call(
        functools.partial(product_kernel, contract),
        grid=(rows // tile,),
        in_specs=[
            pl.BlockSpec((tile, depth), lambda i: (i, 0)),
            pl.BlockSpec((right.shape[0], wide), lambda i: (0, place)),
        ],
        out_specs=pl.BlockSpec((tile, columns), lambda i: (i, 0)),
        out_shape=jax.ShapeDtypeStruct((rows, columns), jnp.bfloat16),
        compiler_params=ROOM,
        cost_estimate=LITTLE,
        name="product",
    )(left, right)


def gelu_product_kernel(left_ref, right_ref, act_ref, slope_ref):
    act, slope = gelu_and_slope(dot(left_ref[...], right_ref[...]))
    act_ref[...] = act.astype(jnp.bfloat16)
    slope_ref[...] = slope


def gelu_product(left, right, wide):
    rows, depth = left.shape
    tile = min(rows, 256)
    strip = pl.BlockSpec((tile, wide), lambda i: (i, 0))
    return pl.pallas_call(
        gelu_product_kernel,
        grid=(rows // tile,),
        in_specs=[pl.BlockSpec((tile, depth), lambda i: (i, 0)), pl.BlockSpec((depth, wide), lambda i: (0, 0))],
        out_specs=[strip, strip],
        out_shape=[
            jax.ShapeDtypeStruct((rows, wide), jnp.bfloat16),
            jax.ShapeDtypeStruct((rows, wide), jnp.float32),
        ],
        compiler_params=ROOM,
        cost_estimate=LITTLE,
        name="gelu_product",
    )(left, right)


def slope_product_kernel(left_ref, right_ref, slope_ref, out_ref):
    out_ref[...] = (dot(left_ref[...], right_ref[...], ((1,), (1,))) * slope_ref[...]).astype(jnp.bfloat16)


def slope_product(left, right, slope, wide, place):
    rows = left.shape[0]
    tall = right.shape[0]
    tile = min(rows, 256)
    return pl.pallas_call(
        slope_product_kernel,
        grid=(rows // tile,),
        in_specs=[
            pl.BlockSpec((tile, wide), lambda i: (i, 0)),
            pl.BlockSpec((tall, wide), lambda i: (0, place)),
            pl.BlockSpec((tile, tall), lambda i: (i, 0)),
        ],
        out_specs=pl.BlockSpec((tile, tall), lambda i: (i, 0)),
        out_shape=jax.ShapeDtypeStruct((rows, tall), jnp.bfloat16),
        compiler_params=ROOM,
        cost_estimate=LITTLE,
        name="slope_product",
    )(left, right, slope)


def pieces_product_kernel(left_ref, *refs):
    *pieces, out_ref = refs
    tall = pieces[0].shape[0]
    total = 0.0
    for number, piece in enumerate(pieces):
        total = total + dot(left_ref[:, number * tall : (number + 1) * tall], piece[...])
    out_ref[...] = total.astype(jnp.bfloat16)


def pieces_product(left, pieces):
    rows, depth = left.shape
    tall, width = pieces[0].shape
    tile = min(rows, 256)
    return pl.pallas_call(
        pieces_product_kernel,
        grid=(rows // tile,),
        in_specs=[pl.BlockSpec((tile, depth), lambda i: (i, 0))]
        + [pl.BlockSpec((tall, width), lambda i: (0, 0))] * len(pieces),
        out_specs=pl.BlockSpec((tile, width), lambda i: (i, 0)),
        out_shape=jax.ShapeDtypeStruct((rows, width), jnp.bfloat16),
        compiler_params=ROOM,
        cost_estimate=LITTLE,
        name="pieces_product",
    )(left, *pieces)


def pieces_slope_kernel(left_ref, slope_ref, *refs):
    *pieces, out_ref = refs
    tall = pieces[0].shape[0]
    for number, piece in enumerate(pieces):
        place = slice(number * tall, (number + 1) * tall)
        value = dot(left_ref[...], piece[...], ((1,), (1,))) * slope_ref[:, place]
        out_ref[:, place] = value.astype(jnp.bfloat16)


def pieces_slope_product(left, pieces, slope):
    rows, width = left.shape
    tall = pieces[0].shape[0]
    depth = tall * len(pieces)
    tile = min(rows, 256)
    strip = pl.BlockSpec((tile, depth), lambda i: (i, 0))
    return pl.pallas_call(
        pieces_slope_kernel,
        grid=(rows // tile,),
        in_specs=[pl.BlockSpec((tile, width), lambda i: (i, 0)), strip]
        + [pl.BlockSpec((tall, width), lambda i: (0, 0))] * len(pieces),
        out_specs=strip,
        out_shape=jax.ShapeDtypeStruct((rows, depth), jnp.bfloat16),
        compiler_params=pltpu.CompilerParams(vmem_limit_bytes=48 * MIB),
        cost_estimate=LITTLE,
        name="pieces_slope_product",
    )(left, slope, *pieces)


def outer_kernel(per, left_ref, right_ref, *outs):
    value = dot(left_ref[...], right_ref[...], ((0,), (0,))).astype(jnp.bfloat16)
    for number, out in enumerate(outs):

        @pl.when(pl.program_id(0) // per == number)
        def _():
            out[...] = value


def outer_pieces(left, right, count):
    rows, tall = left.shape
    width = right.shape[1]
    size = tall // count
    tile = min(512, size)
    per = size // tile
    half = tall // 2 // tile

    def piece(number):
        return pl.BlockSpec((tile, width), lambda i: (jnp.clip(i - number * per, 0, per - 1), 0))

    outs = pl.pallas_call(
        functools.partial(outer_kernel, per),
        grid=(2 * half,),
        in_specs=[
            pl.BlockSpec((rows, tile), lambda i: (0, jnp.where(i < half, i + half, i - half))),
            pl.BlockSpec((rows, width), lambda i: (0, 0)),
        ],
        out_specs=[piece(number) for number in range(count)],
        out_shape=[jax.ShapeDtypeStruct((size, width), jnp.bfloat16)] * count,
        compiler_params=ROOM,
        cost_estimate=LITTLE,
        name="outer_pieces",
    )(left, right)
    return outs[: count // 2], outs[count // 2 :]


def outer(left, right):
    rows, tall = left.shape
    width = right.shape[1]
    tile = min(512, tall)
    return pl.pallas_call(
        functools.partial(product_kernel, ((0,), (0,))),
        grid=(tall // tile,),
        in_specs=[
            pl.BlockSpec((rows, tile), lambda i: (0, i)),
            pl.BlockSpec((rows, width), lambda i: (0, 0)),
        ],
        out_specs=pl.BlockSpec((tile, width), lambda i: (i, 0)),
        out_shape=jax.ShapeDtypeStruct((tall, width), jnp.bfloat16),
        compiler_params=ROOM,
        cost_estimate=LITTLE,
        name="outer",
    )(left, right)


def swap_groups(x, axis):
    return lax.all_to_all(x, axis, split_axis=0, concat_axis=0, tiled=True)


def on_device(
    tokens,
    cotangent,
    w_qkv,
    w_out,
    w_fc_in,
    w_fc_out,
    norm1_gain,
    norm1_bias,
    norm2_gain,
    norm2_bias,
    coef_weight,
    expert_up,
    expert_down,
    routes,
    keep_mask,
):
    rows, width = tokens.shape
    n_es = lax.axis_size("es")
    n_ep = lax.axis_size("ep")
    me_es = lax.axis_index("es").astype(jnp.int32).reshape(1)
    me_ep = lax.axis_index("ep").astype(jnp.int32).reshape(1)
    ep_up, es_up = digits("ep"), digits("es")
    order_e = es_up[::-1]
    order_z = ep_up[::-1]
    order_y = ep_up[:1] + ep_up[:0:-1]
    group = width // n_es
    stripe = w_qkv.shape[0]
    block = w_fc_out.shape[0]
    units = n_ep * block
    tile = 128

    packed = jnp.concatenate(
        [jnp.stack([norm1_gain, norm1_bias, norm2_gain, norm2_bias]), coef_weight.T], axis=0
    )
    packed = jnp.pad(packed, ((0, stripe - packed.shape[0]), (0, tile - stripe)))
    shared = swap_groups(
        jnp.concatenate(
            [
                w_qkv.reshape(stripe, 3, n_es, group).transpose(2, 0, 1, 3).reshape(n_es, stripe, 3 * group),
                jnp.broadcast_to(packed, (n_es, stripe, tile)),
            ],
            axis=2,
        ),
        "es",
    ).reshape(n_es * stripe, 3 * group + tile)
    own_heads, own_small = shared[:, : 3 * group], shared[:, 3 * group :]
    token_pieces = gather_pieces(after(tokens, shared), order_e)
    by_units = w_fc_in.reshape(stripe, n_ep, n_es, block).transpose(2, 0, 1, 3).reshape(n_es, stripe, units)
    more = swap_groups(
        after(jnp.concatenate([by_units, jnp.broadcast_to(w_out, (n_es, *w_out.shape))], axis=2), shared), "es"
    ).reshape(n_es * stripe, units + width)
    cut = 2 * group
    w_heads, small = gather_rows(
        [own_heads, own_small],
        [(order_z, ((0, 0, cut),)), (order_y, ((0, cut, 3 * group - cut), (1, 0, tile)))],
        me_ep,
        token_pieces[1],
    )
    small = small.reshape(n_ep * n_es, stripe, tile)[:, :6, :stripe].transpose(1, 0, 2).reshape(6, width)
    small = small.astype(jnp.float32)
    gain_one, bias_one, gain_two, bias_two = (small[i : i + 1] for i in range(4))
    coef_full = small[4:6]
    normed_all = place_normed(token_pieces, order_e, me_es, gain_one, bias_one)
    dense_weights = lax.all_gather(
        after(jnp.concatenate([more, w_fc_out], axis=1), w_heads), "ep", axis=0, tiled=True
    )
    full_out = dense_weights[:, units : units + width]
    ups = gather_pieces(after(expert_up[0], token_pieces[1]), order_e)

    inputs = tokens.astype(jnp.float32)
    qkv = after(dot(normed_all, w_heads).astype(jnp.bfloat16), ups[2])
    attended_mine, attended_full, logs = attend(qkv)
    attended_mine = after(attended_mine, ups[1])
    attended = (
        swap_groups(attended_mine.reshape(n_es, rows, group), "es").transpose(1, 0, 2).reshape(rows, width)
    )
    hidden = inputs + dot(attended, full_out)
    normed_two, unit_two, inverse_two = norm_forward(hidden, gain_two, bias_two)
    normed_two_low = normed_two.astype(jnp.bfloat16)
    coefficients = softmax_pair(
        lax.dot_general(normed_two, coef_full, (((1,), (1,)), ((), ())), precision=HIGHEST)
    )
    keep = keep_mask.astype(jnp.float32)[:, None]
    grad_out = cotangent.astype(jnp.float32)
    grad_dense_low = (coefficients[:, 0:1] * grad_out).astype(jnp.bfloat16)
    grad_expert_low = (coefficients[:, 1:2] * keep * grad_out).astype(jnp.bfloat16)

    capacity = 2 * rows // n_ep
    expert_ids = routes[:, 0]
    chosen = (expert_ids[:, None] == lax.broadcasted_iota(jnp.int32, (1, n_ep), 1)).astype(jnp.float32)
    before = (
        lax.broadcasted_iota(jnp.int32, (rows, rows), 1) < lax.broadcasted_iota(jnp.int32, (rows, rows), 0)
    ).astype(jnp.float32)
    ranks = jnp.sum(dot(before, chosen) * chosen, axis=1).astype(jnp.int32)
    slots = expert_ids * capacity + ranks
    in_slot = (slots[None, :] == lax.broadcasted_iota(jnp.int32, (n_ep * capacity, 1), 0)).astype(
        jnp.bfloat16
    )

    def to_experts(values):
        return swap_groups(values.reshape(n_ep, capacity, width), "ep").reshape(n_ep * capacity, width)

    outgoing = dot(in_slot, normed_two_low).astype(jnp.bfloat16)
    downs = gather_pieces(after(expert_down[0], attended), order_e, outgoing)
    full_up = jnp.concatenate(ups, axis=0)
    expert_in = to_experts(outgoing)
    expert_grad = to_experts(
        after(dot(in_slot, grad_expert_low).astype(jnp.bfloat16), expert_in, full_up, downs[1])
    )

    def split_pieces(values):
        return [values[i * rows : (i + 1) * rows] for i in range(n_es)]

    acts, expert_slope = gelu_and_slope(dot(expert_in, full_up, ((1,), (1,))))
    acts = acts.astype(jnp.bfloat16)
    expert_out = pieces_product(acts, downs)
    dense_in = jnp.concatenate(gather_pieces(normed_two_low, order_e, acts), axis=0)
    dense_grad = jnp.concatenate(gather_pieces(grad_dense_low, order_e, acts), axis=0)
    expert_grad = after(expert_grad, expert_out, dense_in, dense_grad)
    def fold(kept, got):
        return (kept.astype(jnp.float32) + got.astype(jnp.float32)).astype(jnp.bfloat16)

    def outer_fold(later, kept):
        got = [exchange(piece, order_e[-1]) for piece in later]
        pieces = [fold(k, g) for k, g in zip(kept[1:], got[1:])]
        return kept[0], got[0], pieces

    later_downs, kept_downs = outer_pieces(acts, expert_grad, n_es)
    own_downs, got_downs, pass_downs = outer_fold(later_downs, kept_downs)
    grad_inners = pieces_slope_product(after(expert_grad, later_downs[0]), downs, expert_slope)
    grad_expert_in = product(after(grad_inners, pass_downs[0]), full_up, width)
    last_downs = exchange(pass_downs[0], order_e[0])
    out_home = to_experts(after(expert_out, expert_grad))

    activated_low, slope = gelu_product(after(dense_in, grad_expert_in), dense_weights, units)
    dense_part = product(activated_low, dense_weights, width, place=2)
    grad_home = to_experts(after(grad_expert_in, out_home))
    dense_folded = fold_all_but_last(split_pieces(dense_part), order_e)
    dense = sum_pieces(dense_folded, order_e[:1])
    grad_inner_low = slope_product(after(dense_grad, dense_part), dense_weights, slope, width, 2)
    grad_normed_part = product(after(grad_inner_low, last_downs, dense_folded[1]), dense_weights, units, ((1,), (1,)))
    grad_normed_folded = fold_all_but_last(split_pieces(grad_normed_part), order_e)
    grad_normed_dense = sum_pieces(grad_normed_folded, order_e[:1])

    later_ups, kept_ups = outer_pieces(grad_inners, after(expert_in, grad_normed_part), n_es)
    grad_w_back = outer(activated_low, after(dense_grad, later_ups[0], grad_normed_folded[1]))
    grad_w_in = outer(after(dense_in, later_ups[0]), grad_inner_low)
    dense_stack = jnp.concatenate([g.reshape(n_ep, -1, width) for g in (grad_w_in, grad_w_back)], axis=1)
    grad_home = after(grad_home, dense_stack, dense, grad_normed_dense)
    out_home = after(out_home, grad_home)
    own_ups, got_ups, pass_ups = outer_fold(later_ups, [after(kept, grad_home) for kept in kept_ups])
    expert_tokens = dot(in_slot, out_home, ((0,), (0,))) * keep
    grad_expert_home = dot(in_slot, grad_home, ((0,), (0,)))

    mixed = hidden + coefficients[:, 0:1] * dense + coefficients[:, 1:2] * expert_tokens
    out_tokens = mixed.astype(jnp.bfloat16)
    grad_pair = jnp.concatenate(
        [
            jnp.sum(grad_out * dense, axis=1, keepdims=True),
            jnp.sum(grad_out * expert_tokens, axis=1, keepdims=True),
        ],
        axis=1,
    )
    grad_logits = coefficients * (
        grad_pair - jnp.sum(coefficients * grad_pair, axis=1, keepdims=True)
    )
    grad_coef = lax.dot_general(grad_logits, normed_two, (((0,), (0,)), ((), ())), precision=HIGHEST)
    grad_normed_two = (
        grad_normed_dense
        + grad_expert_home
        + grad_logits[:, 0:1] * coef_full[0:1]
        + grad_logits[:, 1:2] * coef_full[1:2]
    )
    grad_hidden_norm, grad_gain_two, grad_bias_two = norm_backward(
        grad_normed_two, unit_two, inverse_two, gain_two
    )
    grad_hidden = grad_out + grad_hidden_norm
    grad_att_low = grad_hidden.astype(jnp.bfloat16)
    grad_attended = dot(grad_att_low, full_out, ((1,), (1,))).astype(jnp.bfloat16)

    grad_mine = swap_groups(grad_attended.reshape(rows, n_es, group).transpose(1, 0, 2), "es").reshape(
        n_es * rows, group
    )
    dense_sum = lax.psum_scatter(after(dense_stack, grad_home), "ep", scatter_dimension=0, tiled=True)[0]
    grad_w_out = dot(attended, after(grad_att_low, grad_attended), ((0,), (0,))).astype(jnp.bfloat16)
    by_es = grad_w_out.reshape(n_ep, n_es // 2, 2, stripe, width).transpose(2, 1, 0, 3, 4)
    out_folded = scatter_sum(by_es.reshape(n_es * n_ep * stripe, width), order_e[-1:]).astype(jnp.bfloat16)
    grad_mine = after(grad_mine, pass_ups[0], out_folded)
    last_ups = exchange(after(pass_ups[0], grad_mine), order_e[0])
    grad_qkv = after(attend_back(qkv, grad_mine, attended_full, logs), last_ups)
    out_part = scatter_sum(after(out_folded, grad_qkv), order_e[:-1][::-1]).astype(jnp.bfloat16)
    back_e = order_e[::-1]
    grad_rows_part = dot(grad_qkv, w_heads, ((1,), (1,))).astype(jnp.bfloat16)
    grad_w_heads = dot(normed_all, after(grad_qkv, grad_rows_part), ((0,), (0,)))
    column_sums = jnp.sum(grad_qkv.astype(jnp.float32), axis=0, keepdims=True)
    grad_w_heads_low = grad_w_heads.astype(jnp.bfloat16)
    heads_wide = w_heads.astype(jnp.float32)
    grad_bias_one = jnp.sum(heads_wide * column_sums, axis=1)
    grad_gain_one = (jnp.sum(heads_wide * grad_w_heads, axis=1) - bias_one[0] * grad_bias_one) / gain_one[0]
    taps, chain, sums = [], [], []

    def last_sums():
        back_z = order_z[::-1]
        back_y = [order_z[1], order_z[-1], *order_z[2:-1], order_z[0]] if len(order_z) > 2 else back_z
        small_grads = jnp.stack(
            [grad_gain_one, grad_bias_one, grad_gain_two, grad_bias_two, grad_coef[0], grad_coef[1]]
        )
        small_grads = small_grads.astype(jnp.bfloat16).reshape(6, n_ep, n_es * stripe).transpose(1, 0, 2)
        extra = 16
        small_grads = jnp.pad(small_grads, ((0, 0), (0, extra - 6), (0, 3 * group - n_es * stripe)))
        joined = jnp.concatenate([grad_w_heads_low.reshape(n_ep, n_es * stripe, 3 * group), small_grads], axis=1)
        by_columns = out_part.reshape(n_ep, stripe, n_es, group).transpose(0, 2, 1, 3).reshape(n_ep, -1, group)
        by_columns = jnp.pad(by_columns, ((0, 0), (0, extra), (0, 0)))
        joined = jnp.concatenate([joined, by_columns], axis=2).reshape(-1, 4 * group)
        cut = 2 * group
        joined = jnp.concatenate(
            [scatter_sum(joined[:, :cut], back_z, hold=taps[:1], taps=chain), scatter_sum(joined[:, cut:], back_y)], axis=1
        )
        joined = joined.astype(jnp.bfloat16)
        small_sum = joined[n_es * stripe :][:6, : n_es * stripe].reshape(6, n_es, stripe).transpose(1, 0, 2)
        small_sum = jnp.pad(small_sum, ((0, 0), (0, stripe - 6), (0, tile - stripe)))
        sums.append(joined)
        sums.append(
            jnp.concatenate(
                [
                    joined[: n_es * stripe, : 3 * group].reshape(n_es, stripe, 3 * group),
                    small_sum,
                    dense_sum[: n_es * stripe].reshape(n_es, stripe, units),
                ],
                axis=2,
            )
        )
        return sums[1]

    grad_rows = scatter_sum(grad_rows_part, back_e, taps=taps, beside=last_sums)
    joined, outgoing = sums
    last = swap_groups(outgoing, "es")
    _, unit_one, inverse_one = norm_forward(inputs, gain_one, bias_one)
    grad_inputs_norm, _, _ = norm_backward(grad_rows, unit_one, inverse_one, gain_one)
    grad_tokens = grad_hidden + grad_inputs_norm
    grad_w_out = (
        joined[: n_es * stripe, 3 * group :]
        .reshape(n_es, stripe, group)
        .transpose(1, 0, 2)
        .reshape(stripe, width)
        .astype(jnp.float32)
    )
    grad_ups, grad_downs = (
        after(own, chain[0]).astype(jnp.float32) + got.astype(jnp.float32) + came.astype(jnp.float32)
        for own, got, came in ((own_ups, got_ups, last_ups), (own_downs, got_downs, last_downs))
    )
    cut = 3 * group
    grad_w_qkv = (
        last[:, :, :cut]
        .reshape(n_es, stripe, 3, group)
        .transpose(1, 2, 0, 3)
        .reshape(stripe, 3 * width)
        .astype(jnp.float32)
    )
    small_sum = jnp.sum(last[:, :6, cut : cut + stripe].astype(jnp.float32), axis=0)
    grad_fc_in = (
        last[:, :, cut + tile :]
        .reshape(n_es, stripe, n_ep, block)
        .transpose(1, 2, 0, 3)
        .reshape(stripe, n_ep * n_es * block)
        .astype(jnp.float32)
    )
    return (
        out_tokens,
        grad_tokens,
        grad_w_qkv,
        grad_w_out,
        grad_fc_in,
        dense_sum[n_es * stripe :].astype(jnp.float32),
        small_sum[0],
        small_sum[1],
        small_sum[2],
        small_sum[3],
        small_sum[4:6].T,
        grad_ups[None],
        grad_downs[None],
    )


def solution(mesh):
    both = P(BOTH)
    table = P(BOTH, None)
    stack = P("ep", "es", None)
    return jax.shard_map(
        on_device,
        mesh=mesh,
        in_specs=(table,) * 6 + (both,) * 4 + (table, stack, stack, table, both),
        out_specs=(table,) * 6 + (both,) * 4 + (table, stack, stack),
        check_vma=False,
    )
```

```python
import functools

import jax
import jax.numpy as jnp
import numpy as np
from jax import lax
from jax.experimental import pallas as pl
from jax.experimental.pallas import tpu as pltpu
from jax.sharding import PartitionSpec as P

HEADS = 16
HEAD_DIM = 64
EPSILON = 1e-05
MASKED = -1e30
HIGHEST = lax.Precision.HIGHEST
BOTH = ("ep", "es")
MIB = 1 << 20


def norm_forward(values, gain, offset):
    average = jnp.mean(values, axis=-1, keepdims=True)
    centred = values - average
    variance = jnp.mean(centred * centred, axis=-1, keepdims=True)
    inverse = lax.rsqrt(variance + EPSILON)
    unit = centred * inverse
    return unit * gain + offset, unit, inverse


def norm_backward(grad, unit, inverse, gain):
    scaled = grad * gain
    mean_scaled = jnp.mean(scaled, axis=-1, keepdims=True)
    mean_unit = jnp.mean(scaled * unit, axis=-1, keepdims=True)
    grad_in = (scaled - mean_scaled - unit * mean_unit) * inverse
    return grad_in, jnp.sum(grad * unit, axis=0), jnp.sum(grad, axis=0)


def gelu_and_slope(values):
    cdf = 0.5 * (1.0 + lax.erf(values * (2.0**-0.5)))
    density = jnp.exp(-0.5 * values * values) * ((2.0 * np.pi) ** -0.5)
    return values * cdf, cdf + values * density


def dot(left, right, contract=((1,), (0,)), out=jnp.float32):
    return lax.dot_general(left, right, (contract, ((), ())), preferred_element_type=out)


def softmax_pair(logits):
    largest = jnp.max(logits, axis=-1, keepdims=True)
    expanded = jnp.exp(logits - largest)
    return expanded / jnp.sum(expanded, axis=-1, keepdims=True)


def digits(axis):
    size = lax.axis_size(axis)
    return [(axis, 1 << b) for b in range(size.bit_length() - 1)]


def exchange(x, digit):
    axis, stride = digit
    size = lax.axis_size(axis)
    return lax.ppermute(x, axis, [(i, i ^ stride) for i in range(size)])


def after(x, *others):
    return lax.optimization_barrier((x, *others))[0]


def weights_of(order):
    inner = 1 << sum(axis == "es" for axis, _ in order)
    return {(axis, stride): stride * (inner if axis == "ep" else 1) for axis, stride in order}


def relative_numbers(order):
    numbers, weights = [0], weights_of(order)
    for digit in order:
        numbers = numbers + [n + weights[digit] for n in numbers]
    return numbers


def gather_pieces(shard, order, hold=None):
    pieces = [shard]
    for number, digit in enumerate(order):
        if number == len(order) - 1 and hold is not None:
            pieces = [after(piece, hold) for piece in pieces]
        pieces = pieces + [exchange(piece, digit) for piece in pieces]
    return pieces


def gather_relative(shard, order, hold=None):
    held = shard[None]
    for number, digit in enumerate(order[:-1]):
        held = jnp.concatenate([held, exchange(held, digit)], axis=0)
        if number == len(order) - 2 and hold is not None:
            held = after(held, hold)
    return held, exchange(held, order[-1])


def place_kernel(plan, outputs, me_ref, *refs):
    sems_in, sems_out = refs[-2:]
    inputs = len(refs) - 2 - outputs - len({step[2] for step in plan})
    outs, held = refs[inputs : inputs + outputs], refs[inputs + outputs : -2]
    me = me_ref[0]
    arriving, leaving = [], []
    for which, row, chain, slot, relative, rows, segments in plan:
        here = held[chain].at[pl.ds(slot * rows, rows), :]
        copy = pltpu.make_async_copy(refs[which].at[row], here, sems_in.at[len(arriving)])
        copy.start()
        arriving.append(copy)
        start = pl.multiple_of((me ^ relative) * rows, rows)
        group = []
        for place, out, first, width in segments:
            group.append(
                pltpu.make_async_copy(
                    held[chain].at[pl.ds(slot * rows, rows), pl.ds(place, width)],
                    outs[out].at[pl.ds(start, rows), pl.ds(first, width)],
                    sems_out.at[sum(map(len, leaving)) + len(group)],
                )
            )
        leaving.append(group)
    for copy, group in zip(arriving, leaving):
        copy.wait()
        for out in group:
            out.start()
    for group in leaving:
        for out in group:
            out.wait()


def gather_rows(shards, chains, me, hold=None):
    rows = shards[0].shape[0]
    count = 1 << len(chains[0][0])
    if rows % 16 or any(w % 128 or f % 128 for _, ranges in chains for _, f, w in ranges):
        axes = tuple(a for a in BOTH if any(d[0] == a for d in chains[0][0]))
        return [lax.all_gather(shard, axes, axis=0, tiled=True) for shard in shards]
    parts, plan, widths = [], [], []
    for chain, (order, ranges) in enumerate(chains):
        numbers = relative_numbers(order)
        segments, place = [], 0
        for index, first, width in ranges:
            segments.append((place, index, first, width))
            place += width
        widths.append(place)
        cut = [shards[index][:, first : first + width] for index, first, width in ranges]
        joined = cut[0] if len(cut) == 1 else jnp.concatenate(cut, axis=1)
        for half, part in enumerate(gather_relative(joined, order, None if chain else hold)):
            for row in range(count // 2):
                slot = half * (count // 2) + row
                plan.append((len(parts), row, chain, slot, numbers[slot], rows, tuple(segments)))
            parts.append(part)
    return pl.pallas_call(
        functools.partial(place_kernel, tuple(plan), len(shards)),
        out_shape=[jax.ShapeDtypeStruct((count * rows, s.shape[1]), s.dtype) for s in shards],
        in_specs=[pl.BlockSpec(memory_space=pltpu.SMEM)] + [pl.BlockSpec(memory_space=pl.ANY)] * len(parts),
        out_specs=[pl.BlockSpec(memory_space=pl.ANY)] * len(shards),
        scratch_shapes=[pltpu.VMEM((count * rows, w), shards[0].dtype) for w in widths]
        + [
            pltpu.SemaphoreType.DMA((len(plan),)),
            pltpu.SemaphoreType.DMA((sum(len(step[-1]) for step in plan),)),
        ],
        compiler_params=pltpu.CompilerParams(vmem_limit_bytes=16 * MIB),
        name="place_rows",
    )(me, *parts)


def fold_pieces(pieces, digit):
    half = len(pieces) // 2
    return [
        kept.astype(jnp.float32) + exchange(sent.astype(jnp.bfloat16), digit).astype(jnp.float32)
        for kept, sent in zip(pieces[:half], pieces[half:])
    ]


def fold_all_but_last(pieces, order):
    for digit in order[:0:-1]:
        pieces = [piece.astype(jnp.bfloat16) for piece in fold_pieces(pieces, digit)]
    return pieces


def sum_pieces(pieces, order):
    for digit in order[::-1]:
        pieces = fold_pieces(pieces, digit)
    return pieces[0]


def scatter_sum(partial, order, hold=None, taps=None, beside=None):
    count = 1 << len(order)
    rows = partial.shape[0] // count
    remaining = sorted(order, key=weights_of(order).get, reverse=True)
    held = partial.reshape((2,) * len(order) + (rows,) + partial.shape[1:])
    for number, digit in enumerate(order):
        axis, stride = digit
        place = remaining.index(digit)
        remaining.remove(digit)
        bit = (lax.axis_index(axis) // stride) % 2
        mine = lax.dynamic_index_in_dim(held, bit, place, keepdims=False)
        theirs = lax.dynamic_index_in_dim(held, 1 - bit, place, keepdims=False)
        if beside is not None and number == len(order) - 1:
            mine = after(mine, beside())
        held = mine.astype(jnp.float32) + exchange(theirs, digit).astype(jnp.float32)
        if number < len(order) - 1:
            held = held.astype(jnp.bfloat16)
        if taps is not None:
            taps.append(held)
        if number == 0 and hold is not None:
            held = after(held, *hold)
    return held


def norm_place_kernel(per, me_ref, *refs):
    gain_ref, bias_ref, out_ref = refs[-3:]
    for number, ref in enumerate(refs[:-3]):

        @pl.when(pl.program_id(0) // per == number)
        def _():
            values = ref[...].astype(jnp.float32)
            out_ref[...] = norm_forward(values, gain_ref[...], bias_ref[...])[0].astype(jnp.bfloat16)


def place_normed(pieces, order, me, gain, bias):
    rows, width = pieces[0].shape
    step = min(256, rows)
    per = rows // step
    weights = weights_of(order)

    def target(i, me_ref):
        block = me_ref[0]
        for bit, digit in enumerate(order):
            block = block ^ ((((i // per) >> bit) & 1) * weights[digit])
        return (block * per + i % per, 0)

    def source(number):
        return lambda i, me_ref: (jnp.clip(i - number * per, 0, per - 1), 0)

    line = pl.BlockSpec((1, width), lambda i, me_ref: (0, 0))
    return pl.pallas_call(
        functools.partial(norm_place_kernel, per),
        grid_spec=pltpu.PrefetchScalarGridSpec(
            num_scalar_prefetch=1,
            grid=(len(pieces) * per,),
            in_specs=[pl.BlockSpec((step, width), source(n)) for n in range(len(pieces))] + [line, line],
            out_specs=pl.BlockSpec((step, width), target),
        ),
        out_shape=jax.ShapeDtypeStruct((len(pieces) * rows, width), jnp.bfloat16),
        compiler_params=pltpu.CompilerParams(vmem_limit_bytes=24 * MIB),
        name="norm_place",
    )(me, *pieces, gain, bias)


def head_mask(rows, width, head):
    lane = lax.broadcasted_iota(jnp.int32, (rows, width), 1)
    return (lane // HEAD_DIM) == head


def causal_tile(keys, queries):
    key = lax.broadcasted_iota(jnp.int32, (keys, queries), 0)
    query = lax.broadcasted_iota(jnp.int32, (keys, queries), 1)
    return key <= query


def flip(dst, src):
    block = min(256, src.shape[0])
    for start in range(0, src.shape[0], block):
        dst[:, start : start + block] = src[start : start + block, :].T


def over_keys(step, query_block, key_block):
    i = pl.program_id(0)
    per = query_block // key_block

    @pl.loop(0, i * per)
    def _(j):
        step(j, 0, False)

    for r in range(per):
        step(i * per + r, r * key_block, True)


def attend_kernel(heads, bq, bk, q_ref, k_ref, v_ref, low_ref, full_ref, log_ref, vt, qh, acc, top, total):
    width = heads * HEAD_DIM

    @pl.when(pl.program_id(0) == 0)
    def _():
        flip(vt, v_ref)

    scaled = q_ref[...] * jnp.asarray(HEAD_DIM**-0.5, jnp.bfloat16)
    for h in range(heads):
        qh[h] = jnp.where(head_mask(bq, width, h), scaled, jnp.zeros_like(scaled))
    acc[...] = jnp.zeros_like(acc)
    total[...] = jnp.zeros_like(total)
    top[...] = jnp.full_like(top, MASKED)
    one = pl.ds(0, 1)

    def step(j, lo, diagonal):
        at = pl.ds(j * bk, bk)
        keys = k_ref[at, :]
        for h in range(heads):
            s = dot(keys, qh[h, lo:, :], ((1,), (1,)))
            if diagonal:
                s = jnp.where(causal_tile(bk, bq - lo), s, MASKED)
            old = top[h, one, lo:]
            new = jnp.maximum(old, jnp.max(s, axis=0, keepdims=True))
            p = jnp.exp(s - new)
            shrink = jnp.exp(old - new)
            top[h, one, lo:] = new
            total[h, one, lo:] = total[h, one, lo:] * shrink + jnp.sum(p, axis=0, keepdims=True)
            low = slice(h * HEAD_DIM, (h + 1) * HEAD_DIM)
            acc[low, lo:] = acc[low, lo:] * shrink + dot(vt[low, at], p.astype(jnp.bfloat16))

    over_keys(step, bq, bk)
    for h in range(heads):
        log_ref[pl.ds(h, 1), :] = top[h, one, :] + jnp.log(total[h, one, :])
        low = slice(h * HEAD_DIM, (h + 1) * HEAD_DIM)
        acc[low, :] = acc[low, :] / total[h, one, :]
    out = acc[...].T
    full_ref[...] = out
    low_ref[...] = out.astype(jnp.bfloat16)


def column(rows, width, place):
    return pl.BlockSpec((rows, width), lambda i: (0, place))


def attend(qkv):
    rows = qkv.shape[0]
    width = qkv.shape[1] // 3
    heads = width // HEAD_DIM
    bq = bk = min(512, rows)
    strip = pl.BlockSpec((bq, width), lambda i: (i, 0))
    return pl.pallas_call(
        functools.partial(attend_kernel, heads, bq, bk),
        grid=(rows // bq,),
        in_specs=[strip, column(rows, width, 1), column(rows, width, 2)],
        out_specs=[strip, strip, pl.BlockSpec((heads, bq), lambda i: (0, i))],
        out_shape=[
            jax.ShapeDtypeStruct((rows, width), jnp.bfloat16),
            jax.ShapeDtypeStruct((rows, width), jnp.float32),
            jax.ShapeDtypeStruct((heads, rows), jnp.float32),
        ],
        scratch_shapes=[
            pltpu.VMEM((width, rows), jnp.bfloat16),
            pltpu.VMEM((heads, bq, width), jnp.bfloat16),
            pltpu.VMEM((width, bq), jnp.float32),
            pltpu.VMEM((heads, 8, bq), jnp.float32),
            pltpu.VMEM((heads, 8, bq), jnp.float32),
        ],
        compiler_params=pltpu.CompilerParams(vmem_limit_bytes=40 * MIB),
        cost_estimate=pl.CostEstimate(flops=MIB, bytes_accessed=MIB, transcendentals=0),
        name="attend",
    )(qkv, qkv, qkv)


def attend_back_kernel(
    heads, bq, bk, q_ref, k_ref, v_ref, g_ref, o_ref, log_ref, out_ref,
    kt, qh, gh, delta, acc, acc_k, acc_v,
):
    i = pl.program_id(0)
    width = heads * HEAD_DIM
    scale = HEAD_DIM**-0.5
    nt = ((1,), (1,))

    @pl.when(i == 0)
    def _():
        flip(kt, k_ref)
        acc_k[...] = jnp.zeros_like(acc_k)
        acc_v[...] = jnp.zeros_like(acc_v)

    scaled = q_ref[...] * jnp.asarray(scale, jnp.bfloat16)
    grads = g_ref[...]
    for h in range(heads):
        mask = head_mask(bq, width, h)
        qh[h] = jnp.where(mask, scaled, jnp.zeros_like(scaled))
        gh[h] = jnp.where(mask, grads, jnp.zeros_like(grads))
    per_head = (
        lax.broadcasted_iota(jnp.int32, (8, width), 1) // HEAD_DIM
        == lax.broadcasted_iota(jnp.int32, (8, width), 0)
    ).astype(jnp.float32)
    delta[...] = lax.dot_general(
        per_head, grads.astype(jnp.float32) * o_ref[...], (nt, ((), ())), precision=HIGHEST,
        preferred_element_type=jnp.float32,
    )
    acc[...] = jnp.zeros_like(acc)

    def step(j, lo, diagonal):
        at = pl.ds(j * bk, bk)
        keys, values = k_ref[at, :], v_ref[at, :]
        sum_k = sum_v = 0.0
        for h in range(heads):
            queries, outer_grads = qh[h, lo:, :], gh[h, lo:, :]
            s = dot(keys, queries, nt)
            p = jnp.exp(s - log_ref[pl.ds(h, 1), lo:])
            if diagonal:
                p = jnp.where(causal_tile(bk, bq - lo), p, 0.0)
            dp = dot(values, outer_grads, nt)
            raw = (p * (dp - delta[pl.ds(h, 1), lo:])).astype(jnp.bfloat16)
            low = slice(h * HEAD_DIM, (h + 1) * HEAD_DIM)
            acc[low, lo:] = acc[low, lo:] + dot(kt[low, at], raw)
            sum_v = sum_v + dot(p.astype(jnp.bfloat16), outer_grads)
            sum_k = sum_k + dot(raw, queries)
        acc_v[at, :] = acc_v[at, :] + sum_v
        acc_k[at, :] = acc_k[at, :] + sum_k

    over_keys(step, bq, bk)
    out_ref[pl.ds(pl.multiple_of(i * bq, bq), bq), :width] = (acc[...].T * scale).astype(jnp.bfloat16)

    @pl.when(i == pl.num_programs(0) - 1)
    def _():
        out_ref[:, width : 2 * width] = acc_k[...].astype(jnp.bfloat16)
        out_ref[:, 2 * width :] = acc_v[...].astype(jnp.bfloat16)


def attend_back(qkv, grad, full, logs):
    rows, width = grad.shape
    heads = width // HEAD_DIM
    bq, bk = min(1024, rows), min(256, rows)
    strip = pl.BlockSpec((bq, width), lambda i: (i, 0))
    return pl.pallas_call(
        functools.partial(attend_back_kernel, heads, bq, bk),
        grid=(rows // bq,),
        in_specs=[
            strip,
            column(rows, width, 1),
            column(rows, width, 2),
            strip,
            strip,
            pl.BlockSpec((heads, bq), lambda i: (0, i)),
        ],
        out_specs=pl.BlockSpec((rows, 3 * width), lambda i: (0, 0)),
        out_shape=jax.ShapeDtypeStruct((rows, 3 * width), jnp.bfloat16),
        scratch_shapes=[
            pltpu.VMEM((width, rows), jnp.bfloat16),
            pltpu.VMEM((heads, bq, width), jnp.bfloat16),
            pltpu.VMEM((heads, bq, width), jnp.bfloat16),
            pltpu.VMEM((8, bq), jnp.float32),
            pltpu.VMEM((width, bq), jnp.float32),
            pltpu.VMEM((rows, width), jnp.float32),
            pltpu.VMEM((rows, width), jnp.float32),
        ],
        compiler_params=pltpu.CompilerParams(vmem_limit_bytes=56 * MIB),
        cost_estimate=pl.CostEstimate(
            flops=16 * rows * rows * width * heads, bytes_accessed=14 * rows * width, transcendentals=0
        ),
        name="attend_back",
    )(qkv, qkv, qkv, grad, full, logs)


def product_kernel(contract, left_ref, right_ref, out_ref):
    out_ref[...] = dot(left_ref[...], right_ref[...], contract).astype(out_ref.dtype)


LITTLE = pl.CostEstimate(flops=MIB, bytes_accessed=MIB, transcendentals=0)
ROOM = pltpu.CompilerParams(vmem_limit_bytes=40 * MIB)


def product(left, right, wide, contract=((1,), (0,)), place=0):
    rows, depth = left.shape
    tile = min(rows, 256 if depth > 2048 else 512)
    columns = wide if contract[1] == (0,) else right.shape[0]
    return pl.pallas_call(
        functools.partial(product_kernel, contract),
        grid=(rows // tile,),
        in_specs=[
            pl.BlockSpec((tile, depth), lambda i: (i, 0)),
            pl.BlockSpec((right.shape[0], wide), lambda i: (0, place)),
        ],
        out_specs=pl.BlockSpec((tile, columns), lambda i: (i, 0)),
        out_shape=jax.ShapeDtypeStruct((rows, columns), jnp.bfloat16),
        compiler_params=ROOM,
        cost_estimate=LITTLE,
        name="product",
    )(left, right)


def gelu_product_kernel(left_ref, right_ref, act_ref, slope_ref):
    act, slope = gelu_and_slope(dot(left_ref[...], right_ref[...]))
    act_ref[...] = act.astype(jnp.bfloat16)
    slope_ref[...] = slope


def gelu_product(left, right, wide):
    rows, depth = left.shape
    tile = min(rows, 256)
    strip = pl.BlockSpec((tile, wide), lambda i: (i, 0))
    return pl.pallas_call(
        gelu_product_kernel,
        grid=(rows // tile,),
        in_specs=[pl.BlockSpec((tile, depth), lambda i: (i, 0)), pl.BlockSpec((depth, wide), lambda i: (0, 0))],
        out_specs=[strip, strip],
        out_shape=[
            jax.ShapeDtypeStruct((rows, wide), jnp.bfloat16),
            jax.ShapeDtypeStruct((rows, wide), jnp.float32),
        ],
        compiler_params=ROOM,
        cost_estimate=LITTLE,
        name="gelu_product",
    )(left, right)


def slope_product_kernel(left_ref, right_ref, slope_ref, out_ref):
    out_ref[...] = (dot(left_ref[...], right_ref[...], ((1,), (1,))) * slope_ref[...]).astype(jnp.bfloat16)


def slope_product(left, right, slope, wide, place):
    rows = left.shape[0]
    tall = right.shape[0]
    tile = min(rows, 256)
    return pl.pallas_call(
        slope_product_kernel,
        grid=(rows // tile,),
        in_specs=[
            pl.BlockSpec((tile, wide), lambda i: (i, 0)),
            pl.BlockSpec((tall, wide), lambda i: (0, place)),
            pl.BlockSpec((tile, tall), lambda i: (i, 0)),
        ],
        out_specs=pl.BlockSpec((tile, tall), lambda i: (i, 0)),
        out_shape=jax.ShapeDtypeStruct((rows, tall), jnp.bfloat16),
        compiler_params=ROOM,
        cost_estimate=LITTLE,
        name="slope_product",
    )(left, right, slope)


def pieces_product_kernel(left_ref, *refs):
    *pieces, out_ref = refs
    tall = pieces[0].shape[0]
    total = 0.0
    for number, piece in enumerate(pieces):
        total = total + dot(left_ref[:, number * tall : (number + 1) * tall], piece[...])
    out_ref[...] = total.astype(jnp.bfloat16)


def pieces_product(left, pieces):
    rows, depth = left.shape
    tall, width = pieces[0].shape
    tile = min(rows, 256)
    return pl.pallas_call(
        pieces_product_kernel,
        grid=(rows // tile,),
        in_specs=[pl.BlockSpec((tile, depth), lambda i: (i, 0))]
        + [pl.BlockSpec((tall, width), lambda i: (0, 0))] * len(pieces),
        out_specs=pl.BlockSpec((tile, width), lambda i: (i, 0)),
        out_shape=jax.ShapeDtypeStruct((rows, width), jnp.bfloat16),
        compiler_params=ROOM,
        cost_estimate=LITTLE,
        name="pieces_product",
    )(left, *pieces)


def pieces_slope_kernel(left_ref, slope_ref, *refs):
    *pieces, out_ref = refs
    tall = pieces[0].shape[0]
    for number, piece in enumerate(pieces):
        place = slice(number * tall, (number + 1) * tall)
        value = dot(left_ref[...], piece[...], ((1,), (1,))) * slope_ref[:, place]
        out_ref[:, place] = value.astype(jnp.bfloat16)


def pieces_slope_product(left, pieces, slope):
    rows, width = left.shape
    tall = pieces[0].shape[0]
    depth = tall * len(pieces)
    tile = min(rows, 256)
    strip = pl.BlockSpec((tile, depth), lambda i: (i, 0))
    return pl.pallas_call(
        pieces_slope_kernel,
        grid=(rows // tile,),
        in_specs=[pl.BlockSpec((tile, width), lambda i: (i, 0)), strip]
        + [pl.BlockSpec((tall, width), lambda i: (0, 0))] * len(pieces),
        out_specs=strip,
        out_shape=jax.ShapeDtypeStruct((rows, depth), jnp.bfloat16),
        compiler_params=pltpu.CompilerParams(vmem_limit_bytes=48 * MIB),
        cost_estimate=LITTLE,
        name="pieces_slope_product",
    )(left, slope, *pieces)


def outer_kernel(per, left_ref, right_ref, *outs):
    value = dot(left_ref[...], right_ref[...], ((0,), (0,))).astype(jnp.bfloat16)
    for number, out in enumerate(outs):

        @pl.when(pl.program_id(0) // per == number)
        def _():
            out[...] = value


def outer_pieces(left, right, count):
    rows, tall = left.shape
    width = right.shape[1]
    size = tall // count
    tile = min(512, size)
    per = size // tile
    half = tall // 2 // tile

    def piece(number):
        return pl.BlockSpec((tile, width), lambda i: (jnp.clip(i - number * per, 0, per - 1), 0))

    outs = pl.pallas_call(
        functools.partial(outer_kernel, per),
        grid=(2 * half,),
        in_specs=[
            pl.BlockSpec((rows, tile), lambda i: (0, jnp.where(i < half, i + half, i - half))),
            pl.BlockSpec((rows, width), lambda i: (0, 0)),
        ],
        out_specs=[piece(number) for number in range(count)],
        out_shape=[jax.ShapeDtypeStruct((size, width), jnp.bfloat16)] * count,
        compiler_params=ROOM,
        cost_estimate=LITTLE,
        name="outer_pieces",
    )(left, right)
    return outs[: count // 2], outs[count // 2 :]


def outer(left, right):
    rows, tall = left.shape
    width = right.shape[1]
    tile = min(512, tall)
    return pl.pallas_call(
        functools.partial(product_kernel, ((0,), (0,))),
        grid=(tall // tile,),
        in_specs=[
            pl.BlockSpec((rows, tile), lambda i: (0, i)),
            pl.BlockSpec((rows, width), lambda i: (0, 0)),
        ],
        out_specs=pl.BlockSpec((tile, width), lambda i: (i, 0)),
        out_shape=jax.ShapeDtypeStruct((tall, width), jnp.bfloat16),
        compiler_params=ROOM,
        cost_estimate=LITTLE,
        name="outer",
    )(left, right)


def swap_groups(x, axis):
    return lax.all_to_all(x, axis, split_axis=0, concat_axis=0, tiled=True)


def on_device(
    tokens,
    cotangent,
    w_qkv,
    w_out,
    w_fc_in,
    w_fc_out,
    norm1_gain,
    norm1_bias,
    norm2_gain,
    norm2_bias,
    coef_weight,
    expert_up,
    expert_down,
    routes,
    keep_mask,
):
    rows, width = tokens.shape
    n_es = lax.axis_size("es")
    n_ep = lax.axis_size("ep")
    me_es = lax.axis_index("es").astype(jnp.int32).reshape(1)
    me_ep = lax.axis_index("ep").astype(jnp.int32).reshape(1)
    ep_up, es_up = digits("ep"), digits("es")
    order_e = es_up[::-1]
    order_z = ep_up[::-1]
    order_y = ep_up[:1] + ep_up[:0:-1]
    group = width // n_es
    stripe = w_qkv.shape[0]
    block = w_fc_out.shape[0]
    units = n_ep * block
    tile = 128

    packed = jnp.concatenate(
        [jnp.stack([norm1_gain, norm1_bias, norm2_gain, norm2_bias]), coef_weight.T], axis=0
    )
    packed = jnp.pad(packed, ((0, stripe - packed.shape[0]), (0, tile - stripe)))
    shared = swap_groups(
        jnp.concatenate(
            [
                w_qkv.reshape(stripe, 3, n_es, group).transpose(2, 0, 1, 3).reshape(n_es, stripe, 3 * group),
                jnp.broadcast_to(packed, (n_es, stripe, tile)),
            ],
            axis=2,
        ),
        "es",
    ).reshape(n_es * stripe, 3 * group + tile)
    own_heads, own_small = shared[:, : 3 * group], shared[:, 3 * group :]
    token_pieces = gather_pieces(after(tokens, shared), order_e)
    by_units = w_fc_in.reshape(stripe, n_ep, n_es, block).transpose(2, 0, 1, 3).reshape(n_es, stripe, units)
    more = swap_groups(
        after(jnp.concatenate([by_units, jnp.broadcast_to(w_out, (n_es, *w_out.shape))], axis=2), shared), "es"
    ).reshape(n_es * stripe, units + width)
    cut = 2 * group
    w_heads, small = gather_rows(
        [own_heads, own_small],
        [(order_z, ((0, 0, cut),)), (order_y, ((0, cut, 3 * group - cut), (1, 0, tile)))],
        me_ep,
        token_pieces[1],
    )
    small = small.reshape(n_ep * n_es, stripe, tile)[:, :6, :stripe].transpose(1, 0, 2).reshape(6, width)
    small = small.astype(jnp.float32)
    gain_one, bias_one, gain_two, bias_two = (small[i : i + 1] for i in range(4))
    coef_full = small[4:6]
    normed_all = place_normed(token_pieces, order_e, me_es, gain_one, bias_one)
    dense_weights = lax.all_gather(
        after(jnp.concatenate([more, w_fc_out], axis=1), w_heads), "ep", axis=0, tiled=True
    )
    full_out = dense_weights[:, units : units + width]
    ups = gather_pieces(after(expert_up[0], token_pieces[1]), order_e)

    inputs = tokens.astype(jnp.float32)
    qkv = after(dot(normed_all, w_heads).astype(jnp.bfloat16), ups[2])
    attended_mine, attended_full, logs = attend(qkv)
    attended_mine = after(attended_mine, ups[1])
    attended = (
        swap_groups(attended_mine.reshape(n_es, rows, group), "es").transpose(1, 0, 2).reshape(rows, width)
    )
    hidden = inputs + dot(attended, full_out)
    normed_two, unit_two, inverse_two = norm_forward(hidden, gain_two, bias_two)
    normed_two_low = normed_two.astype(jnp.bfloat16)
    coefficients = softmax_pair(
        lax.dot_general(normed_two, coef_full, (((1,), (1,)), ((), ())), precision=HIGHEST)
    )
    keep = keep_mask.astype(jnp.float32)[:, None]
    grad_out = cotangent.astype(jnp.float32)
    grad_dense_low = (coefficients[:, 0:1] * grad_out).astype(jnp.bfloat16)
    grad_expert_low = (coefficients[:, 1:2] * keep * grad_out).astype(jnp.bfloat16)

    capacity = 2 * rows // n_ep
    expert_ids = routes[:, 0]
    chosen = (expert_ids[:, None] == lax.broadcasted_iota(jnp.int32, (1, n_ep), 1)).astype(jnp.float32)
    before = (
        lax.broadcasted_iota(jnp.int32, (rows, rows), 1) < lax.broadcasted_iota(jnp.int32, (rows, rows), 0)
    ).astype(jnp.float32)
    ranks = jnp.sum(dot(before, chosen) * chosen, axis=1).astype(jnp.int32)
    slots = expert_ids * capacity + ranks
    in_slot = (slots[None, :] == lax.broadcasted_iota(jnp.int32, (n_ep * capacity, 1), 0)).astype(
        jnp.bfloat16
    )

    def to_experts(values):
        return swap_groups(values.reshape(n_ep, capacity, width), "ep").reshape(n_ep * capacity, width)

    outgoing = dot(in_slot, normed_two_low).astype(jnp.bfloat16)
    downs = gather_pieces(after(expert_down[0], attended), order_e, outgoing)
    full_up = jnp.concatenate(ups, axis=0)
    expert_in = to_experts(outgoing)
    expert_grad = to_experts(
        after(dot(in_slot, grad_expert_low).astype(jnp.bfloat16), expert_in, full_up, downs[1])
    )

    def split_pieces(values):
        return [values[i * rows : (i + 1) * rows] for i in range(n_es)]

    acts, expert_slope = gelu_and_slope(dot(expert_in, full_up, ((1,), (1,))))
    acts = acts.astype(jnp.bfloat16)
    expert_out = pieces_product(acts, downs)
    dense_in = jnp.concatenate(gather_pieces(normed_two_low, order_e, acts), axis=0)
    dense_grad = jnp.concatenate(gather_pieces(grad_dense_low, order_e, acts), axis=0)
    expert_grad = after(expert_grad, expert_out, dense_in, dense_grad)
    def fold(kept, got):
        return (kept.astype(jnp.float32) + got.astype(jnp.float32)).astype(jnp.bfloat16)

    def outer_fold(later, kept):
        got = [exchange(piece, order_e[-1]) for piece in later]
        pieces = [fold(k, g) for k, g in zip(kept[1:], got[1:])]
        return kept[0], got[0], pieces

    later_downs, kept_downs = outer_pieces(acts, expert_grad, n_es)
    own_downs, got_downs, pass_downs = outer_fold(later_downs, kept_downs)
    grad_inners = pieces_slope_product(after(expert_grad, later_downs[0]), downs, expert_slope)
    grad_expert_in = product(after(grad_inners, pass_downs[0]), full_up, width)
    last_downs = exchange(pass_downs[0], order_e[0])
    out_home = to_experts(after(expert_out, expert_grad))

    activated_low, slope = gelu_product(after(dense_in, grad_expert_in), dense_weights, units)
    dense_part = product(activated_low, dense_weights, width, place=2)
    grad_home = to_experts(after(grad_expert_in, out_home))
    dense_folded = fold_all_but_last(split_pieces(dense_part), order_e)
    dense = sum_pieces(dense_folded, order_e[:1])
    grad_inner_low = slope_product(after(dense_grad, dense_part), dense_weights, slope, width, 2)
    grad_normed_part = product(after(grad_inner_low, last_downs, dense_folded[1]), dense_weights, units, ((1,), (1,)))
    grad_normed_folded = fold_all_but_last(split_pieces(grad_normed_part), order_e)
    grad_normed_dense = sum_pieces(grad_normed_folded, order_e[:1])

    later_ups, kept_ups = outer_pieces(grad_inners, after(expert_in, grad_normed_part), n_es)
    grad_w_back = outer(activated_low, after(dense_grad, later_ups[0], grad_normed_folded[1]))
    grad_w_in = outer(after(dense_in, later_ups[0]), grad_inner_low)
    dense_stack = jnp.concatenate([g.reshape(n_ep, -1, width) for g in (grad_w_in, grad_w_back)], axis=1)
    grad_home = after(grad_home, dense_stack, dense, grad_normed_dense)
    out_home = after(out_home, grad_home)
    own_ups, got_ups, pass_ups = outer_fold(later_ups, [after(kept, grad_home) for kept in kept_ups])
    expert_tokens = dot(in_slot, out_home, ((0,), (0,))) * keep
    grad_expert_home = dot(in_slot, grad_home, ((0,), (0,)))

    mixed = hidden + coefficients[:, 0:1] * dense + coefficients[:, 1:2] * expert_tokens
    out_tokens = mixed.astype(jnp.bfloat16)
    grad_pair = jnp.concatenate(
        [
            jnp.sum(grad_out * dense, axis=1, keepdims=True),
            jnp.sum(grad_out * expert_tokens, axis=1, keepdims=True),
        ],
        axis=1,
    )
    grad_logits = coefficients * (
        grad_pair - jnp.sum(coefficients * grad_pair, axis=1, keepdims=True)
    )
    grad_coef = lax.dot_general(grad_logits, normed_two, (((0,), (0,)), ((), ())), precision=HIGHEST)
    grad_normed_two = (
        grad_normed_dense
        + grad_expert_home
        + grad_logits[:, 0:1] * coef_full[0:1]
        + grad_logits[:, 1:2] * coef_full[1:2]
    )
    grad_hidden_norm, grad_gain_two, grad_bias_two = norm_backward(
        grad_normed_two, unit_two, inverse_two, gain_two
    )
    grad_hidden = grad_out + grad_hidden_norm
    grad_att_low = grad_hidden.astype(jnp.bfloat16)
    grad_attended = dot(grad_att_low, full_out, ((1,), (1,))).astype(jnp.bfloat16)

    grad_mine = swap_groups(grad_attended.reshape(rows, n_es, group).transpose(1, 0, 2), "es").reshape(
        n_es * rows, group
    )
    dense_sum = lax.psum_scatter(after(dense_stack, grad_home), "ep", scatter_dimension=0, tiled=True)[0]
    grad_w_out = dot(attended, after(grad_att_low, grad_attended), ((0,), (0,))).astype(jnp.bfloat16)
    by_es = grad_w_out.reshape(n_ep, n_es // 2, 2, stripe, width).transpose(2, 1, 0, 3, 4)
    out_folded = scatter_sum(by_es.reshape(n_es * n_ep * stripe, width), order_e[-1:]).astype(jnp.bfloat16)
    grad_mine = after(grad_mine, pass_ups[0], out_folded)
    last_ups = exchange(after(pass_ups[0], grad_mine), order_e[0])
    grad_qkv = attend_back(qkv, grad_mine, attended_full, logs)
    out_part = scatter_sum(after(out_folded, grad_qkv), order_e[:-1][::-1]).astype(jnp.bfloat16)
    back_e = order_e[::-1]
    grad_rows_part = dot(grad_qkv, w_heads, ((1,), (1,))).astype(jnp.bfloat16)
    grad_w_heads = dot(normed_all, after(grad_qkv, grad_rows_part, last_ups), ((0,), (0,)))
    column_sums = jnp.sum(grad_qkv.astype(jnp.float32), axis=0, keepdims=True)
    grad_w_heads_low = grad_w_heads.astype(jnp.bfloat16)
    heads_wide = w_heads.astype(jnp.float32)
    grad_bias_one = jnp.sum(heads_wide * column_sums, axis=1)
    grad_gain_one = (jnp.sum(heads_wide * grad_w_heads, axis=1) - bias_one[0] * grad_bias_one) / gain_one[0]
    taps, chain, sums = [], [], []

    def last_sums():
        back_z = order_z[::-1]
        back_y = [order_z[1], order_z[-1], *order_z[2:-1], order_z[0]] if len(order_z) > 2 else back_z
        small_grads = jnp.stack(
            [grad_gain_one, grad_bias_one, grad_gain_two, grad_bias_two, grad_coef[0], grad_coef[1]]
        )
        small_grads = small_grads.astype(jnp.bfloat16).reshape(6, n_ep, n_es * stripe).transpose(1, 0, 2)
        extra = 16
        small_grads = jnp.pad(small_grads, ((0, 0), (0, extra - 6), (0, 3 * group - n_es * stripe)))
        joined = jnp.concatenate([grad_w_heads_low.reshape(n_ep, n_es * stripe, 3 * group), small_grads], axis=1)
        by_columns = out_part.reshape(n_ep, stripe, n_es, group).transpose(0, 2, 1, 3).reshape(n_ep, -1, group)
        by_columns = jnp.pad(by_columns, ((0, 0), (0, extra), (0, 0)))
        joined = jnp.concatenate([joined, by_columns], axis=2).reshape(-1, 4 * group)
        cut = 2 * group
        joined = jnp.concatenate(
            [scatter_sum(joined[:, :cut], back_z, hold=taps[:1], taps=chain), scatter_sum(joined[:, cut:], back_y)], axis=1
        )
        joined = joined.astype(jnp.bfloat16)
        small_sum = joined[n_es * stripe :][:6, : n_es * stripe].reshape(6, n_es, stripe).transpose(1, 0, 2)
        small_sum = jnp.pad(small_sum, ((0, 0), (0, stripe - 6), (0, tile - stripe)))
        sums.append(joined)
        sums.append(
            jnp.concatenate(
                [
                    joined[: n_es * stripe, : 3 * group].reshape(n_es, stripe, 3 * group),
                    small_sum,
                    dense_sum[: n_es * stripe].reshape(n_es, stripe, units),
                ],
                axis=2,
            )
        )
        return sums[1]

    grad_rows = scatter_sum(grad_rows_part, back_e, taps=taps, beside=last_sums)
    joined, outgoing = sums
    last = swap_groups(outgoing, "es")
    _, unit_one, inverse_one = norm_forward(inputs, gain_one, bias_one)
    grad_inputs_norm, _, _ = norm_backward(grad_rows, unit_one, inverse_one, gain_one)
    grad_tokens = grad_hidden + grad_inputs_norm
    grad_w_out = (
        joined[: n_es * stripe, 3 * group :]
        .reshape(n_es, stripe, group)
        .transpose(1, 0, 2)
        .reshape(stripe, width)
        .astype(jnp.float32)
    )
    grad_ups, grad_downs = (
        after(own, chain[0]).astype(jnp.float32) + got.astype(jnp.float32) + came.astype(jnp.float32)
        for own, got, came in ((own_ups, got_ups, last_ups), (own_downs, got_downs, last_downs))
    )
    cut = 3 * group
    grad_w_qkv = (
        last[:, :, :cut]
        .reshape(n_es, stripe, 3, group)
        .transpose(1, 2, 0, 3)
        .reshape(stripe, 3 * width)
        .astype(jnp.float32)
    )
    small_sum = jnp.sum(last[:, :6, cut : cut + stripe].astype(jnp.float32), axis=0)
    grad_fc_in = (
        last[:, :, cut + tile :]
        .reshape(n_es, stripe, n_ep, block)
        .transpose(1, 2, 0, 3)
        .reshape(stripe, n_ep * n_es * block)
        .astype(jnp.float32)
    )
    return (
        out_tokens,
        grad_tokens,
        grad_w_qkv,
        grad_w_out,
        grad_fc_in,
        dense_sum[n_es * stripe :].astype(jnp.float32),
        small_sum[0],
        small_sum[1],
        small_sum[2],
        small_sum[3],
        small_sum[4:6].T,
        grad_ups[None],
        grad_downs[None],
    )


def solution(mesh):
    both = P(BOTH)
    table = P(BOTH, None)
    stack = P("ep", "es", None)
    return jax.shard_map(
        on_device,
        mesh=mesh,
        in_specs=(table,) * 6 + (both,) * 4 + (table, stack, stack, table, both),
        out_specs=(table,) * 6 + (both,) * 4 + (table, stack, stack),
        check_vma=False,
    )
```

```python
import functools

import jax
import jax.numpy as jnp
import numpy as np
from jax import lax
from jax.experimental import pallas as pl
from jax.experimental.pallas import tpu as pltpu
from jax.sharding import PartitionSpec as P

HEADS = 16
HEAD_DIM = 64
EPSILON = 1e-05
MASKED = -1e30
HIGHEST = lax.Precision.HIGHEST
BOTH = ("ep", "es")
MIB = 1 << 20


def norm_forward(values, gain, offset):
    average = jnp.mean(values, axis=-1, keepdims=True)
    centred = values - average
    variance = jnp.mean(centred * centred, axis=-1, keepdims=True)
    inverse = lax.rsqrt(variance + EPSILON)
    unit = centred * inverse
    return unit * gain + offset, unit, inverse


def norm_backward(grad, unit, inverse, gain):
    scaled = grad * gain
    mean_scaled = jnp.mean(scaled, axis=-1, keepdims=True)
    mean_unit = jnp.mean(scaled * unit, axis=-1, keepdims=True)
    grad_in = (scaled - mean_scaled - unit * mean_unit) * inverse
    return grad_in, jnp.sum(grad * unit, axis=0), jnp.sum(grad, axis=0)


def gelu_and_slope(values):
    cdf = 0.5 * (1.0 + lax.erf(values * (2.0**-0.5)))
    density = jnp.exp(-0.5 * values * values) * ((2.0 * np.pi) ** -0.5)
    return values * cdf, cdf + values * density


def dot(left, right, contract=((1,), (0,)), out=jnp.float32):
    return lax.dot_general(left, right, (contract, ((), ())), preferred_element_type=out)


def softmax_pair(logits):
    largest = jnp.max(logits, axis=-1, keepdims=True)
    expanded = jnp.exp(logits - largest)
    return expanded / jnp.sum(expanded, axis=-1, keepdims=True)


def digits(axis):
    size = lax.axis_size(axis)
    return [(axis, 1 << b) for b in range(size.bit_length() - 1)]


def exchange(x, digit):
    axis, stride = digit
    size = lax.axis_size(axis)
    return lax.ppermute(x, axis, [(i, i ^ stride) for i in range(size)])


def after(x, *others):
    return lax.optimization_barrier((x, *others))[0]


def weights_of(order):
    inner = 1 << sum(axis == "es" for axis, _ in order)
    return {(axis, stride): stride * (inner if axis == "ep" else 1) for axis, stride in order}


def relative_numbers(order):
    numbers, weights = [0], weights_of(order)
    for digit in order:
        numbers = numbers + [n + weights[digit] for n in numbers]
    return numbers


def gather_pieces(shard, order, hold=None):
    pieces = [shard]
    for number, digit in enumerate(order):
        if number == len(order) - 1 and hold is not None:
            pieces = [after(piece, hold) for piece in pieces]
        pieces = pieces + [exchange(piece, digit) for piece in pieces]
    return pieces


def gather_relative(shard, order, hold=None):
    held = shard[None]
    for number, digit in enumerate(order[:-1]):
        held = jnp.concatenate([held, exchange(held, digit)], axis=0)
        if number == len(order) - 2 and hold is not None:
            held = after(held, hold)
    return held, exchange(held, order[-1])


def place_kernel(plan, outputs, me_ref, *refs):
    sems_in, sems_out = refs[-2:]
    inputs = len(refs) - 2 - outputs - len({step[2] for step in plan})
    outs, held = refs[inputs : inputs + outputs], refs[inputs + outputs : -2]
    me = me_ref[0]
    arriving, leaving = [], []
    for which, row, chain, slot, relative, rows, segments in plan:
        here = held[chain].at[pl.ds(slot * rows, rows), :]
        copy = pltpu.make_async_copy(refs[which].at[row], here, sems_in.at[len(arriving)])
        copy.start()
        arriving.append(copy)
        start = pl.multiple_of((me ^ relative) * rows, rows)
        group = []
        for place, out, first, width in segments:
            group.append(
                pltpu.make_async_copy(
                    held[chain].at[pl.ds(slot * rows, rows), pl.ds(place, width)],
                    outs[out].at[pl.ds(start, rows), pl.ds(first, width)],
                    sems_out.at[sum(map(len, leaving)) + len(group)],
                )
            )
        leaving.append(group)
    for copy, group in zip(arriving, leaving):
        copy.wait()
        for out in group:
            out.start()
    for group in leaving:
        for out in group:
            out.wait()


def gather_rows(shards, chains, me, hold=None):
    rows = shards[0].shape[0]
    count = 1 << len(chains[0][0])
    if rows % 16 or any(w % 128 or f % 128 for _, ranges in chains for _, f, w in ranges):
        axes = tuple(a for a in BOTH if any(d[0] == a for d in chains[0][0]))
        return [lax.all_gather(shard, axes, axis=0, tiled=True) for shard in shards]
    parts, plan, widths = [], [], []
    for chain, (order, ranges) in enumerate(chains):
        numbers = relative_numbers(order)
        segments, place = [], 0
        for index, first, width in ranges:
            segments.append((place, index, first, width))
            place += width
        widths.append(place)
        cut = [shards[index][:, first : first + width] for index, first, width in ranges]
        joined = cut[0] if len(cut) == 1 else jnp.concatenate(cut, axis=1)
        for half, part in enumerate(gather_relative(joined, order, None if chain else hold)):
            for row in range(count // 2):
                slot = half * (count // 2) + row
                plan.append((len(parts), row, chain, slot, numbers[slot], rows, tuple(segments)))
            parts.append(part)
    return pl.pallas_call(
        functools.partial(place_kernel, tuple(plan), len(shards)),
        out_shape=[jax.ShapeDtypeStruct((count * rows, s.shape[1]), s.dtype) for s in shards],
        in_specs=[pl.BlockSpec(memory_space=pltpu.SMEM)] + [pl.BlockSpec(memory_space=pl.ANY)] * len(parts),
        out_specs=[pl.BlockSpec(memory_space=pl.ANY)] * len(shards),
        scratch_shapes=[pltpu.VMEM((count * rows, w), shards[0].dtype) for w in widths]
        + [
            pltpu.SemaphoreType.DMA((len(plan),)),
            pltpu.SemaphoreType.DMA((sum(len(step[-1]) for step in plan),)),
        ],
        compiler_params=pltpu.CompilerParams(vmem_limit_bytes=16 * MIB),
        name="place_rows",
    )(me, *parts)


def fold_pieces(pieces, digit):
    half = len(pieces) // 2
    return [
        kept.astype(jnp.float32) + exchange(sent.astype(jnp.bfloat16), digit).astype(jnp.float32)
        for kept, sent in zip(pieces[:half], pieces[half:])
    ]


def fold_all_but_last(pieces, order):
    for digit in order[:0:-1]:
        pieces = [piece.astype(jnp.bfloat16) for piece in fold_pieces(pieces, digit)]
    return pieces


def sum_pieces(pieces, order):
    for digit in order[::-1]:
        pieces = fold_pieces(pieces, digit)
    return pieces[0]


def scatter_sum(partial, order, hold=None, taps=None, beside=None):
    count = 1 << len(order)
    rows = partial.shape[0] // count
    remaining = sorted(order, key=weights_of(order).get, reverse=True)
    held = partial.reshape((2,) * len(order) + (rows,) + partial.shape[1:])
    for number, digit in enumerate(order):
        axis, stride = digit
        place = remaining.index(digit)
        remaining.remove(digit)
        bit = (lax.axis_index(axis) // stride) % 2
        mine = lax.dynamic_index_in_dim(held, bit, place, keepdims=False)
        theirs = lax.dynamic_index_in_dim(held, 1 - bit, place, keepdims=False)
        if beside is not None and number == len(order) - 1:
            mine = after(mine, beside())
        held = mine.astype(jnp.float32) + exchange(theirs, digit).astype(jnp.float32)
        if number < len(order) - 1:
            held = held.astype(jnp.bfloat16)
        if taps is not None:
            taps.append(held)
        if number == 0 and hold is not None:
            held = after(held, *hold)
    return held


def norm_place_kernel(per, me_ref, *refs):
    gain_ref, bias_ref, out_ref = refs[-3:]
    for number, ref in enumerate(refs[:-3]):

        @pl.when(pl.program_id(0) // per == number)
        def _():
            values = ref[...].astype(jnp.float32)
            out_ref[...] = norm_forward(values, gain_ref[...], bias_ref[...])[0].astype(jnp.bfloat16)


def place_normed(pieces, order, me, gain, bias):
    rows, width = pieces[0].shape
    step = min(256, rows)
    per = rows // step
    weights = weights_of(order)

    def target(i, me_ref):
        block = me_ref[0]
        for bit, digit in enumerate(order):
            block = block ^ ((((i // per) >> bit) & 1) * weights[digit])
        return (block * per + i % per, 0)

    def source(number):
        return lambda i, me_ref: (jnp.clip(i - number * per, 0, per - 1), 0)

    line = pl.BlockSpec((1, width), lambda i, me_ref: (0, 0))
    return pl.pallas_call(
        functools.partial(norm_place_kernel, per),
        grid_spec=pltpu.PrefetchScalarGridSpec(
            num_scalar_prefetch=1,
            grid=(len(pieces) * per,),
            in_specs=[pl.BlockSpec((step, width), source(n)) for n in range(len(pieces))] + [line, line],
            out_specs=pl.BlockSpec((step, width), target),
        ),
        out_shape=jax.ShapeDtypeStruct((len(pieces) * rows, width), jnp.bfloat16),
        compiler_params=pltpu.CompilerParams(vmem_limit_bytes=24 * MIB),
        name="norm_place",
    )(me, *pieces, gain, bias)


def head_mask(rows, width, head):
    lane = lax.broadcasted_iota(jnp.int32, (rows, width), 1)
    return (lane // HEAD_DIM) == head


def causal_tile(keys, queries):
    key = lax.broadcasted_iota(jnp.int32, (keys, queries), 0)
    query = lax.broadcasted_iota(jnp.int32, (keys, queries), 1)
    return key <= query


def flip(dst, src):
    block = min(256, src.shape[0])
    for start in range(0, src.shape[0], block):
        dst[:, start : start + block] = src[start : start + block, :].T


def over_keys(step, query_block, key_block):
    i = pl.program_id(0)
    per = query_block // key_block

    @pl.loop(0, i * per)
    def _(j):
        step(j, 0, False)

    for r in range(per):
        step(i * per + r, r * key_block, True)


def attend_kernel(heads, bq, bk, q_ref, k_ref, v_ref, low_ref, full_ref, log_ref, vt, qh, acc, top, total):
    width = heads * HEAD_DIM

    @pl.when(pl.program_id(0) == 0)
    def _():
        flip(vt, v_ref)

    scaled = q_ref[...] * jnp.asarray(HEAD_DIM**-0.5, jnp.bfloat16)
    for h in range(heads):
        qh[h] = jnp.where(head_mask(bq, width, h), scaled, jnp.zeros_like(scaled))
    acc[...] = jnp.zeros_like(acc)
    total[...] = jnp.zeros_like(total)
    top[...] = jnp.full_like(top, MASKED)
    one = pl.ds(0, 1)

    def step(j, lo, diagonal):
        at = pl.ds(j * bk, bk)
        keys = k_ref[at, :]
        for h in range(heads):
            s = dot(keys, qh[h, lo:, :], ((1,), (1,)))
            if diagonal:
                s = jnp.where(causal_tile(bk, bq - lo), s, MASKED)
            old = top[h, one, lo:]
            new = jnp.maximum(old, jnp.max(s, axis=0, keepdims=True))
            p = jnp.exp(s - new)
            shrink = jnp.exp(old - new)
            top[h, one, lo:] = new
            total[h, one, lo:] = total[h, one, lo:] * shrink + jnp.sum(p, axis=0, keepdims=True)
            low = slice(h * HEAD_DIM, (h + 1) * HEAD_DIM)
            acc[low, lo:] = acc[low, lo:] * shrink + dot(vt[low, at], p.astype(jnp.bfloat16))

    over_keys(step, bq, bk)
    for h in range(heads):
        log_ref[pl.ds(h, 1), :] = top[h, one, :] + jnp.log(total[h, one, :])
        low = slice(h * HEAD_DIM, (h + 1) * HEAD_DIM)
        acc[low, :] = acc[low, :] / total[h, one, :]
    out = acc[...].T
    full_ref[...] = out
    low_ref[...] = out.astype(jnp.bfloat16)


def column(rows, width, place):
    return pl.BlockSpec((rows, width), lambda i: (0, place))


def attend(qkv):
    rows = qkv.shape[0]
    width = qkv.shape[1] // 3
    heads = width // HEAD_DIM
    bq = bk = min(512, rows)
    strip = pl.BlockSpec((bq, width), lambda i: (i, 0))
    return pl.pallas_call(
        functools.partial(attend_kernel, heads, bq, bk),
        grid=(rows // bq,),
        in_specs=[strip, column(rows, width, 1), column(rows, width, 2)],
        out_specs=[strip, strip, pl.BlockSpec((heads, bq), lambda i: (0, i))],
        out_shape=[
            jax.ShapeDtypeStruct((rows, width), jnp.bfloat16),
            jax.ShapeDtypeStruct((rows, width), jnp.float32),
            jax.ShapeDtypeStruct((heads, rows), jnp.float32),
        ],
        scratch_shapes=[
            pltpu.VMEM((width, rows), jnp.bfloat16),
            pltpu.VMEM((heads, bq, width), jnp.bfloat16),
            pltpu.VMEM((width, bq), jnp.float32),
            pltpu.VMEM((heads, 8, bq), jnp.float32),
            pltpu.VMEM((heads, 8, bq), jnp.float32),
        ],
        compiler_params=pltpu.CompilerParams(vmem_limit_bytes=40 * MIB),
        cost_estimate=pl.CostEstimate(flops=MIB, bytes_accessed=MIB, transcendentals=0),
        name="attend",
    )(qkv, qkv, qkv)


def attend_back_kernel(
    heads, bq, bk, q_ref, k_ref, v_ref, g_ref, o_ref, log_ref, out_ref,
    kt, qh, gh, delta, acc, acc_k, acc_v,
):
    i = pl.program_id(0)
    width = heads * HEAD_DIM
    scale = HEAD_DIM**-0.5
    nt = ((1,), (1,))

    @pl.when(i == 0)
    def _():
        flip(kt, k_ref)
        acc_k[...] = jnp.zeros_like(acc_k)
        acc_v[...] = jnp.zeros_like(acc_v)

    scaled = q_ref[...] * jnp.asarray(scale, jnp.bfloat16)
    grads = g_ref[...]
    for h in range(heads):
        mask = head_mask(bq, width, h)
        qh[h] = jnp.where(mask, scaled, jnp.zeros_like(scaled))
        gh[h] = jnp.where(mask, grads, jnp.zeros_like(grads))
    per_head = (
        lax.broadcasted_iota(jnp.int32, (8, width), 1) // HEAD_DIM
        == lax.broadcasted_iota(jnp.int32, (8, width), 0)
    ).astype(jnp.float32)
    delta[...] = lax.dot_general(
        per_head, grads.astype(jnp.float32) * o_ref[...], (nt, ((), ())), precision=HIGHEST,
        preferred_element_type=jnp.float32,
    )
    acc[...] = jnp.zeros_like(acc)

    def step(j, lo, diagonal):
        at = pl.ds(j * bk, bk)
        keys, values = k_ref[at, :], v_ref[at, :]
        sum_k = sum_v = 0.0
        for h in range(heads):
            queries, outer_grads = qh[h, lo:, :], gh[h, lo:, :]
            s = dot(keys, queries, nt)
            p = jnp.exp(s - log_ref[pl.ds(h, 1), lo:])
            if diagonal:
                p = jnp.where(causal_tile(bk, bq - lo), p, 0.0)
            dp = dot(values, outer_grads, nt)
            raw = (p * (dp - delta[pl.ds(h, 1), lo:])).astype(jnp.bfloat16)
            low = slice(h * HEAD_DIM, (h + 1) * HEAD_DIM)
            acc[low, lo:] = acc[low, lo:] + dot(kt[low, at], raw)
            sum_v = sum_v + dot(p.astype(jnp.bfloat16), outer_grads)
            sum_k = sum_k + dot(raw, queries)
        acc_v[at, :] = acc_v[at, :] + sum_v
        acc_k[at, :] = acc_k[at, :] + sum_k

    over_keys(step, bq, bk)
    out_ref[pl.ds(pl.multiple_of(i * bq, bq), bq), :width] = (acc[...].T * scale).astype(jnp.bfloat16)

    @pl.when(i == pl.num_programs(0) - 1)
    def _():
        out_ref[:, width : 2 * width] = acc_k[...].astype(jnp.bfloat16)
        out_ref[:, 2 * width :] = acc_v[...].astype(jnp.bfloat16)


def attend_back(qkv, grad, full, logs):
    rows, width = grad.shape
    heads = width // HEAD_DIM
    bq, bk = min(1024, rows), min(256, rows)
    strip = pl.BlockSpec((bq, width), lambda i: (i, 0))
    return pl.pallas_call(
        functools.partial(attend_back_kernel, heads, bq, bk),
        grid=(rows // bq,),
        in_specs=[
            strip,
            column(rows, width, 1),
            column(rows, width, 2),
            strip,
            strip,
            pl.BlockSpec((heads, bq), lambda i: (0, i)),
        ],
        out_specs=pl.BlockSpec((rows, 3 * width), lambda i: (0, 0)),
        out_shape=jax.ShapeDtypeStruct((rows, 3 * width), jnp.bfloat16),
        scratch_shapes=[
            pltpu.VMEM((width, rows), jnp.bfloat16),
            pltpu.VMEM((heads, bq, width), jnp.bfloat16),
            pltpu.VMEM((heads, bq, width), jnp.bfloat16),
            pltpu.VMEM((8, bq), jnp.float32),
            pltpu.VMEM((width, bq), jnp.float32),
            pltpu.VMEM((rows, width), jnp.float32),
            pltpu.VMEM((rows, width), jnp.float32),
        ],
        compiler_params=pltpu.CompilerParams(vmem_limit_bytes=56 * MIB),
        cost_estimate=pl.CostEstimate(
            flops=16 * rows * rows * width * heads, bytes_accessed=14 * rows * width, transcendentals=0
        ),
        name="attend_back",
    )(qkv, qkv, qkv, grad, full, logs)


def product_kernel(contract, left_ref, right_ref, out_ref):
    out_ref[...] = dot(left_ref[...], right_ref[...], contract).astype(out_ref.dtype)


LITTLE = pl.CostEstimate(flops=MIB, bytes_accessed=MIB, transcendentals=0)
ROOM = pltpu.CompilerParams(vmem_limit_bytes=40 * MIB)


def product(left, right, wide, contract=((1,), (0,)), place=0):
    rows, depth = left.shape
    tile = min(rows, 256 if depth > 2048 else 512)
    columns = wide if contract[1] == (0,) else right.shape[0]
    return pl.pallas_call(
        functools.partial(product_kernel, contract),
        grid=(rows // tile,),
        in_specs=[
            pl.BlockSpec((tile, depth), lambda i: (i, 0)),
            pl.BlockSpec((right.shape[0], wide), lambda i: (0, place)),
        ],
        out_specs=pl.BlockSpec((tile, columns), lambda i: (i, 0)),
        out_shape=jax.ShapeDtypeStruct((rows, columns), jnp.bfloat16),
        compiler_params=ROOM,
        cost_estimate=LITTLE,
        name="product",
    )(left, right)


def gelu_product_kernel(left_ref, right_ref, act_ref, slope_ref):
    act, slope = gelu_and_slope(dot(left_ref[...], right_ref[...]))
    act_ref[...] = act.astype(jnp.bfloat16)
    slope_ref[...] = slope


def gelu_product(left, right, wide):
    rows, depth = left.shape
    tile = min(rows, 256)
    strip = pl.BlockSpec((tile, wide), lambda i: (i, 0))
    return pl.pallas_call(
        gelu_product_kernel,
        grid=(rows // tile,),
        in_specs=[pl.BlockSpec((tile, depth), lambda i: (i, 0)), pl.BlockSpec((depth, wide), lambda i: (0, 0))],
        out_specs=[strip, strip],
        out_shape=[
            jax.ShapeDtypeStruct((rows, wide), jnp.bfloat16),
            jax.ShapeDtypeStruct((rows, wide), jnp.float32),
        ],
        compiler_params=ROOM,
        cost_estimate=LITTLE,
        name="gelu_product",
    )(left, right)


def slope_product_kernel(left_ref, right_ref, slope_ref, out_ref):
    out_ref[...] = (dot(left_ref[...], right_ref[...], ((1,), (1,))) * slope_ref[...]).astype(jnp.bfloat16)


def slope_product(left, right, slope, wide, place):
    rows = left.shape[0]
    tall = right.shape[0]
    tile = min(rows, 256)
    return pl.pallas_call(
        slope_product_kernel,
        grid=(rows // tile,),
        in_specs=[
            pl.BlockSpec((tile, wide), lambda i: (i, 0)),
            pl.BlockSpec((tall, wide), lambda i: (0, place)),
            pl.BlockSpec((tile, tall), lambda i: (i, 0)),
        ],
        out_specs=pl.BlockSpec((tile, tall), lambda i: (i, 0)),
        out_shape=jax.ShapeDtypeStruct((rows, tall), jnp.bfloat16),
        compiler_params=ROOM,
        cost_estimate=LITTLE,
        name="slope_product",
    )(left, right, slope)


def pieces_product_kernel(left_ref, *refs):
    *pieces, out_ref = refs
    tall = pieces[0].shape[0]
    total = 0.0
    for number, piece in enumerate(pieces):
        total = total + dot(left_ref[:, number * tall : (number + 1) * tall], piece[...])
    out_ref[...] = total.astype(jnp.bfloat16)


def pieces_product(left, pieces):
    rows, depth = left.shape
    tall, width = pieces[0].shape
    tile = min(rows, 256)
    return pl.pallas_call(
        pieces_product_kernel,
        grid=(rows // tile,),
        in_specs=[pl.BlockSpec((tile, depth), lambda i: (i, 0))]
        + [pl.BlockSpec((tall, width), lambda i: (0, 0))] * len(pieces),
        out_specs=pl.BlockSpec((tile, width), lambda i: (i, 0)),
        out_shape=jax.ShapeDtypeStruct((rows, width), jnp.bfloat16),
        compiler_params=ROOM,
        cost_estimate=LITTLE,
        name="pieces_product",
    )(left, *pieces)


def pieces_slope_kernel(left_ref, slope_ref, *refs):
    *pieces, out_ref = refs
    tall = pieces[0].shape[0]
    for number, piece in enumerate(pieces):
        place = slice(number * tall, (number + 1) * tall)
        value = dot(left_ref[...], piece[...], ((1,), (1,))) * slope_ref[:, place]
        out_ref[:, place] = value.astype(jnp.bfloat16)


def pieces_slope_product(left, pieces, slope):
    rows, width = left.shape
    tall = pieces[0].shape[0]
    depth = tall * len(pieces)
    tile = min(rows, 256)
    strip = pl.BlockSpec((tile, depth), lambda i: (i, 0))
    return pl.pallas_call(
        pieces_slope_kernel,
        grid=(rows // tile,),
        in_specs=[pl.BlockSpec((tile, width), lambda i: (i, 0)), strip]
        + [pl.BlockSpec((tall, width), lambda i: (0, 0))] * len(pieces),
        out_specs=strip,
        out_shape=jax.ShapeDtypeStruct((rows, depth), jnp.bfloat16),
        compiler_params=pltpu.CompilerParams(vmem_limit_bytes=48 * MIB),
        cost_estimate=LITTLE,
        name="pieces_slope_product",
    )(left, slope, *pieces)


def outer_kernel(per, left_ref, right_ref, *outs):
    value = dot(left_ref[...], right_ref[...], ((0,), (0,))).astype(jnp.bfloat16)
    for number, out in enumerate(outs):

        @pl.when(pl.program_id(0) // per == number)
        def _():
            out[...] = value


def outer_pieces(left, right, count):
    rows, tall = left.shape
    width = right.shape[1]
    size = tall // count
    tile = min(512, size)
    per = size // tile
    half = tall // 2 // tile

    def piece(number):
        return pl.BlockSpec((tile, width), lambda i: (jnp.clip(i - number * per, 0, per - 1), 0))

    outs = pl.pallas_call(
        functools.partial(outer_kernel, per),
        grid=(2 * half,),
        in_specs=[
            pl.BlockSpec((rows, tile), lambda i: (0, jnp.where(i < half, i + half, i - half))),
            pl.BlockSpec((rows, width), lambda i: (0, 0)),
        ],
        out_specs=[piece(number) for number in range(count)],
        out_shape=[jax.ShapeDtypeStruct((size, width), jnp.bfloat16)] * count,
        compiler_params=ROOM,
        cost_estimate=LITTLE,
        name="outer_pieces",
    )(left, right)
    return outs[: count // 2], outs[count // 2 :]


def outer(left, right):
    rows, tall = left.shape
    width = right.shape[1]
    tile = min(512, tall)
    return pl.pallas_call(
        functools.partial(product_kernel, ((0,), (0,))),
        grid=(tall // tile,),
        in_specs=[
            pl.BlockSpec((rows, tile), lambda i: (0, i)),
            pl.BlockSpec((rows, width), lambda i: (0, 0)),
        ],
        out_specs=pl.BlockSpec((tile, width), lambda i: (i, 0)),
        out_shape=jax.ShapeDtypeStruct((tall, width), jnp.bfloat16),
        compiler_params=ROOM,
        cost_estimate=LITTLE,
        name="outer",
    )(left, right)


def swap_groups(x, axis):
    return lax.all_to_all(x, axis, split_axis=0, concat_axis=0, tiled=True)


def on_device(
    tokens,
    cotangent,
    w_qkv,
    w_out,
    w_fc_in,
    w_fc_out,
    norm1_gain,
    norm1_bias,
    norm2_gain,
    norm2_bias,
    coef_weight,
    expert_up,
    expert_down,
    routes,
    keep_mask,
):
    rows, width = tokens.shape
    n_es = lax.axis_size("es")
    n_ep = lax.axis_size("ep")
    me_es = lax.axis_index("es").astype(jnp.int32).reshape(1)
    me_ep = lax.axis_index("ep").astype(jnp.int32).reshape(1)
    ep_up, es_up = digits("ep"), digits("es")
    order_e = es_up[::-1]
    order_z = ep_up[::-1]
    order_y = ep_up[:1] + ep_up[:0:-1]
    group = width // n_es
    stripe = w_qkv.shape[0]
    block = w_fc_out.shape[0]
    units = n_ep * block
    tile = 128

    packed = jnp.concatenate(
        [jnp.stack([norm1_gain, norm1_bias, norm2_gain, norm2_bias]), coef_weight.T], axis=0
    )
    packed = jnp.pad(packed, ((0, stripe - packed.shape[0]), (0, tile - stripe)))
    shared = swap_groups(
        jnp.concatenate(
            [
                w_qkv.reshape(stripe, 3, n_es, group).transpose(2, 0, 1, 3).reshape(n_es, stripe, 3 * group),
                jnp.broadcast_to(packed, (n_es, stripe, tile)),
            ],
            axis=2,
        ),
        "es",
    ).reshape(n_es * stripe, 3 * group + tile)
    own_heads, own_small = shared[:, : 3 * group], shared[:, 3 * group :]
    token_pieces = gather_pieces(after(tokens, shared), order_e)
    by_units = w_fc_in.reshape(stripe, n_ep, n_es, block).transpose(2, 0, 1, 3).reshape(n_es, stripe, units)
    more = swap_groups(
        after(jnp.concatenate([by_units, jnp.broadcast_to(w_out, (n_es, *w_out.shape))], axis=2), shared), "es"
    ).reshape(n_es * stripe, units + width)
    cut = 2 * group
    w_heads, small = gather_rows(
        [own_heads, own_small],
        [(order_z, ((0, 0, cut),)), (order_y, ((0, cut, 3 * group - cut), (1, 0, tile)))],
        me_ep,
        token_pieces[1],
    )
    small = small.reshape(n_ep * n_es, stripe, tile)[:, :6, :stripe].transpose(1, 0, 2).reshape(6, width)
    small = small.astype(jnp.float32)
    gain_one, bias_one, gain_two, bias_two = (small[i : i + 1] for i in range(4))
    coef_full = small[4:6]
    normed_all = place_normed(token_pieces, order_e, me_es, gain_one, bias_one)
    own_in, own_out = more[:, :units], more[:, units:]
    full_out = lax.all_gather(after(own_out, w_heads), "ep", axis=0, tiled=True)
    ups = gather_pieces(after(expert_up[0], token_pieces[1]), order_e)

    inputs = tokens.astype(jnp.float32)
    qkv = after(dot(normed_all, w_heads).astype(jnp.bfloat16), ups[2])
    attended_mine, attended_full, logs = attend(qkv)
    attended_mine = after(attended_mine, ups[1])
    attended = (
        swap_groups(attended_mine.reshape(n_es, rows, group), "es").transpose(1, 0, 2).reshape(rows, width)
    )
    dense_weights = lax.all_gather(
        after(jnp.concatenate([own_in, w_fc_out], axis=1), attended), "ep", axis=0, tiled=True
    )
    hidden = inputs + dot(attended, full_out)
    normed_two, unit_two, inverse_two = norm_forward(hidden, gain_two, bias_two)
    normed_two_low = normed_two.astype(jnp.bfloat16)
    coefficients = softmax_pair(
        lax.dot_general(normed_two, coef_full, (((1,), (1,)), ((), ())), precision=HIGHEST)
    )
    keep = keep_mask.astype(jnp.float32)[:, None]
    grad_out = cotangent.astype(jnp.float32)
    grad_dense_low = (coefficients[:, 0:1] * grad_out).astype(jnp.bfloat16)
    grad_expert_low = (coefficients[:, 1:2] * keep * grad_out).astype(jnp.bfloat16)

    capacity = 2 * rows // n_ep
    expert_ids = routes[:, 0]
    chosen = (expert_ids[:, None] == lax.broadcasted_iota(jnp.int32, (1, n_ep), 1)).astype(jnp.float32)
    before = (
        lax.broadcasted_iota(jnp.int32, (rows, rows), 1) < lax.broadcasted_iota(jnp.int32, (rows, rows), 0)
    ).astype(jnp.float32)
    ranks = jnp.sum(dot(before, chosen) * chosen, axis=1).astype(jnp.int32)
    slots = expert_ids * capacity + ranks
    in_slot = (slots[None, :] == lax.broadcasted_iota(jnp.int32, (n_ep * capacity, 1), 0)).astype(
        jnp.bfloat16
    )

    def to_experts(values):
        return swap_groups(values.reshape(n_ep, capacity, width), "ep").reshape(n_ep * capacity, width)

    outgoing = dot(in_slot, normed_two_low).astype(jnp.bfloat16)
    downs = gather_pieces(after(expert_down[0], attended), order_e, outgoing)
    full_up = jnp.concatenate(ups, axis=0)
    expert_in = to_experts(outgoing)
    expert_grad = to_experts(
        after(dot(in_slot, grad_expert_low).astype(jnp.bfloat16), expert_in, full_up, downs[1])
    )

    def split_pieces(values):
        return [values[i * rows : (i + 1) * rows] for i in range(n_es)]

    acts, expert_slope = gelu_and_slope(dot(expert_in, full_up, ((1,), (1,))))
    acts = acts.astype(jnp.bfloat16)
    expert_out = pieces_product(acts, downs)
    dense_in = jnp.concatenate(gather_pieces(normed_two_low, order_e, acts), axis=0)
    dense_grad = jnp.concatenate(gather_pieces(grad_dense_low, order_e, acts), axis=0)
    expert_grad = after(expert_grad, expert_out, dense_in, dense_grad)
    def fold(kept, got):
        return (kept.astype(jnp.float32) + got.astype(jnp.float32)).astype(jnp.bfloat16)

    def outer_fold(later, kept):
        got = [exchange(piece, order_e[-1]) for piece in later]
        pieces = [fold(k, g) for k, g in zip(kept[1:], got[1:])]
        return kept[0], got[0], pieces

    later_downs, kept_downs = outer_pieces(acts, expert_grad, n_es)
    own_downs, got_downs, pass_downs = outer_fold(later_downs, kept_downs)
    grad_inners = pieces_slope_product(after(expert_grad, later_downs[0]), downs, expert_slope)
    grad_expert_in = product(after(grad_inners, pass_downs[0]), full_up, width)
    last_downs = exchange(pass_downs[0], order_e[0])
    out_home = to_experts(after(expert_out, expert_grad))

    activated_low, slope = gelu_product(after(dense_in, grad_expert_in), dense_weights, units)
    dense_part = product(activated_low, dense_weights, width, place=1)
    grad_home = to_experts(after(grad_expert_in, out_home))
    dense_folded = fold_all_but_last(split_pieces(dense_part), order_e)
    dense = sum_pieces(dense_folded, order_e[:1])
    grad_inner_low = slope_product(after(dense_grad, dense_part), dense_weights, slope, width, 1)
    grad_normed_part = product(after(grad_inner_low, last_downs, dense_folded[1]), dense_weights, units, ((1,), (1,)))
    grad_normed_folded = fold_all_but_last(split_pieces(grad_normed_part), order_e)
    grad_normed_dense = sum_pieces(grad_normed_folded, order_e[:1])

    later_ups, kept_ups = outer_pieces(grad_inners, after(expert_in, grad_normed_part), n_es)
    grad_w_back = outer(activated_low, after(dense_grad, later_ups[0], grad_normed_folded[1]))
    grad_w_in = outer(after(dense_in, later_ups[0]), grad_inner_low)
    dense_stack = jnp.concatenate([g.reshape(n_ep, -1, width) for g in (grad_w_in, grad_w_back)], axis=1)
    grad_home = after(grad_home, dense_stack, dense, grad_normed_dense)
    out_home = after(out_home, grad_home)
    own_ups, got_ups, pass_ups = outer_fold(later_ups, [after(kept, grad_home) for kept in kept_ups])
    expert_tokens = dot(in_slot, out_home, ((0,), (0,))) * keep
    grad_expert_home = dot(in_slot, grad_home, ((0,), (0,)))

    mixed = hidden + coefficients[:, 0:1] * dense + coefficients[:, 1:2] * expert_tokens
    out_tokens = mixed.astype(jnp.bfloat16)
    grad_pair = jnp.concatenate(
        [
            jnp.sum(grad_out * dense, axis=1, keepdims=True),
            jnp.sum(grad_out * expert_tokens, axis=1, keepdims=True),
        ],
        axis=1,
    )
    grad_logits = coefficients * (
        grad_pair - jnp.sum(coefficients * grad_pair, axis=1, keepdims=True)
    )
    grad_coef = lax.dot_general(grad_logits, normed_two, (((0,), (0,)), ((), ())), precision=HIGHEST)
    grad_normed_two = (
        grad_normed_dense
        + grad_expert_home
        + grad_logits[:, 0:1] * coef_full[0:1]
        + grad_logits[:, 1:2] * coef_full[1:2]
    )
    grad_hidden_norm, grad_gain_two, grad_bias_two = norm_backward(
        grad_normed_two, unit_two, inverse_two, gain_two
    )
    grad_hidden = grad_out + grad_hidden_norm
    grad_att_low = grad_hidden.astype(jnp.bfloat16)
    grad_attended = dot(grad_att_low, full_out, ((1,), (1,))).astype(jnp.bfloat16)

    grad_mine = swap_groups(grad_attended.reshape(rows, n_es, group).transpose(1, 0, 2), "es").reshape(
        n_es * rows, group
    )
    dense_sum = lax.psum_scatter(after(dense_stack, grad_home), "ep", scatter_dimension=0, tiled=True)[0]
    grad_w_out = dot(attended, after(grad_att_low, grad_attended), ((0,), (0,))).astype(jnp.bfloat16)
    by_es = grad_w_out.reshape(n_ep, n_es // 2, 2, stripe, width).transpose(2, 1, 0, 3, 4)
    out_folded = scatter_sum(by_es.reshape(n_es * n_ep * stripe, width), order_e[-1:]).astype(jnp.bfloat16)
    grad_mine = after(grad_mine, pass_ups[0], out_folded)
    last_ups = exchange(after(pass_ups[0], grad_mine), order_e[0])
    grad_qkv = attend_back(qkv, grad_mine, attended_full, logs)
    out_part = scatter_sum(after(out_folded, grad_qkv), order_e[:-1][::-1]).astype(jnp.bfloat16)
    back_e = order_e[::-1]
    grad_rows_part = dot(grad_qkv, w_heads, ((1,), (1,))).astype(jnp.bfloat16)
    grad_w_heads = dot(normed_all, after(grad_qkv, grad_rows_part, last_ups), ((0,), (0,)))
    column_sums = jnp.sum(grad_qkv.astype(jnp.float32), axis=0, keepdims=True)
    grad_w_heads_low = grad_w_heads.astype(jnp.bfloat16)
    heads_wide = w_heads.astype(jnp.float32)
    grad_bias_one = jnp.sum(heads_wide * column_sums, axis=1)
    grad_gain_one = (jnp.sum(heads_wide * grad_w_heads, axis=1) - bias_one[0] * grad_bias_one) / gain_one[0]
    taps, chain, sums = [], [], []

    def last_sums():
        back_z = order_z[::-1]
        back_y = [order_z[1], order_z[-1], *order_z[2:-1], order_z[0]] if len(order_z) > 2 else back_z
        small_grads = jnp.stack(
            [grad_gain_one, grad_bias_one, grad_gain_two, grad_bias_two, grad_coef[0], grad_coef[1]]
        )
        small_grads = small_grads.astype(jnp.bfloat16).reshape(6, n_ep, n_es * stripe).transpose(1, 0, 2)
        extra = 16
        small_grads = jnp.pad(small_grads, ((0, 0), (0, extra - 6), (0, 3 * group - n_es * stripe)))
        joined = jnp.concatenate([grad_w_heads_low.reshape(n_ep, n_es * stripe, 3 * group), small_grads], axis=1)
        by_columns = out_part.reshape(n_ep, stripe, n_es, group).transpose(0, 2, 1, 3).reshape(n_ep, -1, group)
        by_columns = jnp.pad(by_columns, ((0, 0), (0, extra), (0, 0)))
        joined = jnp.concatenate([joined, by_columns], axis=2).reshape(-1, 4 * group)
        cut = 2 * group
        joined = jnp.concatenate(
            [scatter_sum(joined[:, :cut], back_z, hold=taps[:1], taps=chain), scatter_sum(joined[:, cut:], back_y)], axis=1
        )
        joined = joined.astype(jnp.bfloat16)
        small_sum = joined[n_es * stripe :][:6, : n_es * stripe].reshape(6, n_es, stripe).transpose(1, 0, 2)
        small_sum = jnp.pad(small_sum, ((0, 0), (0, stripe - 6), (0, tile - stripe)))
        sums.append(joined)
        sums.append(
            jnp.concatenate(
                [
                    joined[: n_es * stripe, : 3 * group].reshape(n_es, stripe, 3 * group),
                    small_sum,
                    dense_sum[: n_es * stripe].reshape(n_es, stripe, units),
                ],
                axis=2,
            )
        )
        return sums[1]

    grad_rows = scatter_sum(grad_rows_part, back_e, taps=taps, beside=last_sums)
    joined, outgoing = sums
    last = swap_groups(outgoing, "es")
    _, unit_one, inverse_one = norm_forward(inputs, gain_one, bias_one)
    grad_inputs_norm, _, _ = norm_backward(grad_rows, unit_one, inverse_one, gain_one)
    grad_tokens = grad_hidden + grad_inputs_norm
    grad_w_out = (
        joined[: n_es * stripe, 3 * group :]
        .reshape(n_es, stripe, group)
        .transpose(1, 0, 2)
        .reshape(stripe, width)
        .astype(jnp.float32)
    )
    grad_ups, grad_downs = (
        after(own, chain[0]).astype(jnp.float32) + got.astype(jnp.float32) + came.astype(jnp.float32)
        for own, got, came in ((own_ups, got_ups, last_ups), (own_downs, got_downs, last_downs))
    )
    cut = 3 * group
    grad_w_qkv = (
        last[:, :, :cut]
        .reshape(n_es, stripe, 3, group)
        .transpose(1, 2, 0, 3)
        .reshape(stripe, 3 * width)
        .astype(jnp.float32)
    )
    small_sum = jnp.sum(last[:, :6, cut : cut + stripe].astype(jnp.float32), axis=0)
    grad_fc_in = (
        last[:, :, cut + tile :]
        .reshape(n_es, stripe, n_ep, block)
        .transpose(1, 2, 0, 3)
        .reshape(stripe, n_ep * n_es * block)
        .astype(jnp.float32)
    )
    return (
        out_tokens,
        grad_tokens,
        grad_w_qkv,
        grad_w_out,
        grad_fc_in,
        dense_sum[n_es * stripe :].astype(jnp.float32),
        small_sum[0],
        small_sum[1],
        small_sum[2],
        small_sum[3],
        small_sum[4:6].T,
        grad_ups[None],
        grad_downs[None],
    )


def solution(mesh):
    both = P(BOTH)
    table = P(BOTH, None)
    stack = P("ep", "es", None)
    return jax.shard_map(
        on_device,
        mesh=mesh,
        in_specs=(table,) * 6 + (both,) * 4 + (table, stack, stack, table, both),
        out_specs=(table,) * 6 + (both,) * 4 + (table, stack, stack),
        check_vma=False,
    )
```
